32 devices in a mesh: lat: 4 (over x, core), lev: 4 (over z), lon: 2 (over y).
Axes of the slice: x: 2, y: 2, z: 4, core: 2. Of those that a mesh axis runs over, the one named last changes fastest.
Arguments:
- adjoint: float32 [4, 136, 16, 512], P(None, 'lev', 'lat', 'lon'), may hold values from -6 to 6
- wind_east: float32 [136, 16, 512], P('lev', 'lat', 'lon'), may hold values from -0.48 to 0.48
- wind_north: float32 [136, 16, 512], P('lev', 'lat', 'lon'), may hold values from -0.48 to 0.48
- kz_inverse: float32 [4, 136, 136], replicated, may hold values from 0 to 1.2
- kz_regime: int32 [2, 16, 512], P(None, 'lat', 'lon'), may hold values from 0 to 3
- fp_cell: int32 [16, 2, 512], P(('lat', 'lev'), 'lon'), may hold values from 0 to 2047
- fp_owner: int32 [16, 2, 512, 1], P(('lat', 'lev'), 'lon'), may hold values from 0 to 15; in each aligned block of 512 rows (0 to 511, 512 to 1023, ..., all dimensions but the last counted through in order) at most 64 rows name the same one
- fp_station: int32 [16, 2, 512], P(('lat', 'lev'), 'lon'), may hold values from 0 to 3
- fp_weight: float32 [16, 2, 512], P(('lat', 'lev'), 'lon'), may hold values from 0.02 to 0.2
Outputs:
- final_adjoint: float32 [4, 136, 16, 512], P(None, 'lev', 'lat', 'lon')
- station_sens: float32 [2, 4, 2, 64], P(None, None, 'lon', ('lat', 'lev'))
The draws below stay inside these ranges and needn't reach their ends.
Inputs may be any that keep to these rules, and one draw needn't show every extreme that they name: `fp_owner`: among the rows of one device no region is named by more than 64 entries, a bound that some block reaches.
All inputs are finite; a program needn't handle non-finite values.
Results may differ from the reference program's by a relative error of at most 0.00014.
Values sent between devices are 32-bit elements; how exact they have to be, the bound alone decides.
No kernel may reach another device: no remote copies, remote signals or barrier semaphores. Data moves between devices by JAX's collectives and lax.ppermute only.
A program may use at most 64 MiB of HBM per device.

```python
import math
import jax
import jax.numpy as jnp
import numpy as np
from jax import lax

TRACERS = 4
LEV = 136
CLAT = 4
CLON = 256
NSUB = 4
HOURS = 2
REGIMES = 4
FOOT_LEVELS = 8
SPO = 4
ENT_DEV = 512
NLAT = 16
NLON = 512
GROUPS = 16
COLS = 256
STATIONS = 64
CAP = 64
N_LAT = 4
N_LEV = 4
N_LON = 2


def draw_wind(key, shape_dims):
    return jax.random.uniform(key, shape_dims, jnp.float32, -0.48, 0.48)


def draw_wind_east(key, part):
    return draw_wind(jax.random.fold_in(key, 11), (LEV, NLAT, NLON))


def draw_wind_north(key, part):
    return draw_wind(jax.random.fold_in(key, 23), (LEV, NLAT, NLON))


def draw_kz_inverse(key, part):
    level_ids = jnp.arange(LEV, dtype=jnp.float32)
    distance = jnp.abs(level_ids[:, None] - level_ids[None, :])
    reach_len = LEV / (2.0 + jnp.arange(REGIMES, dtype=jnp.float32))
    factor = jax.random.uniform(key, (REGIMES, LEV, LEV), jnp.float32, 0.3, 1.0)
    spread = factor * jnp.exp(-distance[None] / reach_len[:, None, None]) * (1.2 / LEV)
    return jnp.where(distance[None] == 0.0, 1.0 + 0.2 * factor, spread).astype(jnp.float32)


def place_ends(drawn, key, smallest, largest):
    spot = [jax.random.randint(jax.random.fold_in(key, axis), (), 0, length) for axis, length in enumerate(drawn.shape)]
    longest = drawn.shape.index(max(drawn.shape))
    next_to = spot[:longest] + [(spot[longest] + 1) % drawn.shape[longest]] + spot[longest + 1:]
    return drawn.at[tuple(spot)].set(smallest).at[tuple(next_to)].set(largest)


def shard_levels(own_key, shape, shards, low, high):
    level = 1.0
    for dim, parts in shards:
        draws = jax.random.uniform(jax.random.fold_in(jax.random.fold_in(own_key, 6), dim), (parts,), jnp.float32, low / len(shards), high / len(shards))
        level = level * jnp.repeat(jnp.exp(draws), shape[dim] // parts).reshape((-1,) + (1,) * (len(shape) - 1 - dim))
    return level


def routed_block(rng, own, number, rows, number_of, top, reach, lean):
    order = jax.random.permutation(rng, number_of)
    crowded, usual = shares(number_of, rows * top, reach, lean, True), shares(number_of, rows * top, reach, lean, False)
    places = jnp.arange(number_of)

    def named(lengths, turn):
        used = int((lengths > 0).sum())
        fixed = max(1, used // 4)
        shifted = fixed + (places - fixed + turn * (used - fixed)) % max(1, number_of - fixed)
        return jnp.zeros((number_of,), jnp.int32).at[order[jnp.where(places < fixed, places, shifted)]].set(jnp.asarray(lengths, jnp.int32))

    lengths = jnp.where(number % 4 == 0, named(crowded, number // 4), named(usual, number - number // 4 - 1))
    mixed = jax.random.permutation(jax.random.fold_in(own, 3), number_of)
    giver, sink = mixed[0:number_of // 2 * 2:2], mixed[1:number_of // 2 * 2:2]
    room = jnp.minimum(lengths[giver] - 1, reach - lengths[sink]) // 2
    room = jnp.where((giver == order[0]) | (sink == order[0]) | (lengths[sink] == 0), 0, jnp.maximum(room, 0))
    shifted = jax.random.randint(jax.random.fold_in(own, 4), (number_of // 2,), 0, 1 << 20) % (room + 1)
    lengths = lengths.at[giver].add(-shifted).at[sink].add(shifted)
    labels = jnp.searchsorted(jnp.cumsum(lengths), jnp.arange(rows * top), side="right").astype(jnp.int32)
    listing = labels.reshape(top, rows).T
    listing = listing[jax.random.permutation(jax.random.fold_in(own, 1), rows)]
    turn = jax.random.randint(jax.random.fold_in(own, 2), (rows, 1), 0, top)
    return jnp.take_along_axis(listing, (jnp.arange(top)[None, :] + turn) % top, axis=1)


def shares(amount, total, reach, lean, full):
    loads = [(1 << 20) // math.isqrt(grade ** lean) + 1 for grade in range(1, amount + 1)]
    largest = reach if full else min(reach, max(-(-total // amount), total * loads[0] // sum(loads)))
    least = 1 if total - largest >= amount - 1 else 0
    holding, surplus = [largest] + [least] * (amount - 1), total - largest - least * (amount - 1)
    while surplus > 0:
        free = [i for i in range(1, amount) if holding[i] < largest] or [i for i in range(1, amount) if holding[i] < reach]
        whole, remaining = sum([loads[i] for i in free]), surplus
        for i in free:
            extra = min(reach - holding[i], max(1, remaining * loads[i] // whole), surplus)
            holding[i] = holding[i] + extra
            surplus = surplus - extra
    return np.array(holding)


def normal_values(rng, shape, width, bound, shards=(), held_as=jnp.bfloat16):
    gain = shard_levels(rng, shape, shards, -0.22, 0.18) if shards else 1.0
    array = jax.random.normal(rng, shape, jnp.float32) * width * gain
    return jnp.minimum(jnp.maximum(array, -bound), bound).astype(held_as)


def setup_inputs(seed: int = 0) -> dict:
    key_list = jax.random.split(jax.random.key(seed), 10)
    adjoint = normal_values(key_list[0], (TRACERS, LEV, NLAT, NLON), 1.0, 6.0, ((1, 4), (2, 4), (3, 2)), jnp.float32)
    wind_east = draw_wind_east(jax.random.fold_in(key_list[9], 71), 0)
    wind_north = draw_wind_north(jax.random.fold_in(key_list[9], 71), 0)
    kz_inverse = draw_kz_inverse(jax.random.fold_in(key_list[9], 71), 0)
    kz_regime = place_ends(jax.random.randint(key_list[4], (HOURS, NLAT, NLON), 0, REGIMES), jax.random.fold_in(key_list[4], 1), 0, REGIMES - 1).astype(jnp.int32)
    fp_cell = place_ends(jax.random.randint(key_list[5], (GROUPS, N_LON, ENT_DEV), 0, FOOT_LEVELS * COLS), jax.random.fold_in(key_list[5], 1), 0, (FOOT_LEVELS * COLS) - 1).astype(jnp.int32)
    fp_owner_keys = jax.random.split(jax.random.fold_in(key_list[6], 1), GROUPS * N_LON * ENT_DEV // ENT_DEV)
    fp_owner_turns = jax.random.permutation(jax.random.fold_in(key_list[6], 3), GROUPS * N_LON * ENT_DEV // ENT_DEV)
    fp_owner = jax.vmap(lambda own, number: routed_block(jax.random.fold_in(key_list[6], 2), own, number, ENT_DEV, GROUPS, 1, CAP, 2))(fp_owner_keys, fp_owner_turns).reshape((GROUPS, N_LON, ENT_DEV, 1))
    fp_station = place_ends(jax.random.randint(key_list[7], (GROUPS, N_LON, ENT_DEV), 0, SPO), jax.random.fold_in(key_list[7], 1), 0, SPO - 1).astype(jnp.int32)
    fp_weight = jnp.clip(jnp.exp(math.log(0.2) - 2.3025851 * jax.random.uniform(key_list[8], (GROUPS, N_LON, ENT_DEV), jnp.float32) ** shard_levels(key_list[8], (GROUPS, N_LON, ENT_DEV), ((0, 16), (1, 2)), -0.2, 0.2)), 0.02, 0.2)
    return {"adjoint": adjoint, "wind_east": wind_east, "wind_north": wind_north, "kz_inverse": kz_inverse, "kz_regime": kz_regime, "fp_cell": fp_cell, "fp_owner": fp_owner, "fp_station": fp_station, "fp_weight": fp_weight}


def lat_sweep(padded, north_face, south_face):
    middle = padded[:, :, 1:-1]
    return middle + jnp.maximum(north_face, 0.0) * (padded[:, :, 2:] - middle) - jnp.minimum(south_face, 0.0) * (padded[:, :, :-2] - middle)


def lon_sweep(padded, east_face, west_face):
    middle = padded[:, :, :, 1:-1]
    return middle + jnp.maximum(east_face, 0.0) * (padded[:, :, :, 2:] - middle) - jnp.minimum(west_face, 0.0) * (padded[:, :, :, :-2] - middle)


def reference(adjoint, wind_east, wind_north, kz_inverse, kz_regime, fp_cell, fp_owner, fp_station, fp_weight):
    lat_total = adjoint.shape[2]
    row_index = jnp.arange(lat_total)[None, :, None]
    north_face = jnp.where(row_index == lat_total - 1, jnp.zeros_like(wind_north), wind_north)
    south_face = jnp.pad(north_face, ((0, 0), (1, 0), (0, 0)))[:, :-1]
    west_face = jnp.roll(wind_east, 1, axis=2)
    group_ids = jnp.arange(N_LAT * N_LEV, dtype=jnp.int32)[:, None, None]
    lon_ids = jnp.arange(N_LON, dtype=jnp.int32)[None, :, None]
    level_ids = fp_cell // COLS
    flat_cell = (group_ids % N_LEV) * COLS + fp_cell % COLS
    lat_ids = (group_ids // N_LEV) * CLAT + flat_cell // CLON
    lon_full = lon_ids * CLON + flat_cell % CLON
    targets = (lon_ids * STATIONS + fp_owner[..., 0] * SPO + fp_station).reshape(-1).astype(jnp.int32)
    adjoint_field = adjoint
    outputs = []
    for hour_step in range(HOURS):
        regime_map = kz_regime[hour_step]
        solved = jnp.zeros_like(adjoint_field)
        for regime in range(REGIMES):
            product = jnp.einsum("ji,tjab->tiab", kz_inverse[regime], adjoint_field, precision=lax.Precision.HIGHEST)
            solved = jnp.where(regime_map[None, None] == regime, product, solved)
        picked = solved[:, level_ids, lat_ids, lon_full] * fp_weight[None]
        totals = jax.ops.segment_sum(picked.reshape(TRACERS, -1).T, targets, num_segments=N_LON * STATIONS)
        outputs.append(totals.T.reshape(TRACERS, N_LON, STATIONS))
        adjoint_field = solved
        for substep in range(NSUB):
            padded = jnp.pad(adjoint_field, ((0, 0), (0, 0), (1, 1), (0, 0)))
            adjoint_field = lat_sweep(padded, north_face, south_face)
            padded = jnp.concatenate([adjoint_field[..., -1:], adjoint_field, adjoint_field[..., :1]], axis=3)
            adjoint_field = lon_sweep(padded, wind_east, west_face)
    return adjoint_field, jnp.stack(outputs)
```

```python
import functools
import jax
import jax.numpy as jnp
from jax import lax
from jax.experimental import pallas as pl
from jax.experimental.pallas import tpu as pltpu
from jax.sharding import PartitionSpec as P

NSUB = 4
HOURS = 2
REGIMES = 4
FOOT_LEVELS = 8
SPO = 4
LANES = 128
GRAIN = 16
F32 = jnp.float32
BF16 = jnp.bfloat16
AXES = ("lat", "lev")
RING = ("lat", "lev", "lon")


def chunk_owner(n_lat, n_lev):
    place = [0] * (n_lat * n_lev)
    for a in range(n_lat):
        for z in range(n_lev):
            chip, core = divmod(a, 2)
            step = z if chip % 2 == 0 else n_lev - 1 - z
            place[(chip * n_lev + step) * 2 + core] = a * n_lev + z
    return place


def ring_perm(n_lat, n_lev, n_lon, shift):
    place = chunk_owner(n_lat, n_lev)
    ring = [place[d] * n_lon + o for o in range(n_lon) for d in range(len(place))]
    count = len(ring)
    return [(ring[i], ring[(i + shift) % count]) for i in range(count)]


def lane_ids(rows):
    return lax.broadcasted_iota(jnp.int32, (rows, LANES), 1)


def swap_grains(blocks):
    blocks = list(blocks)
    grain = lane_ids(blocks[0].shape[0]) // GRAIN
    bit = len(blocks) // 2
    while bit:
        low = (grain & bit) == 0
        for i in range(len(blocks)):
            if i & bit == 0:
                a, b = blocks[i], blocks[i | bit]
                blocks[i] = jnp.where(low, a, pltpu.roll(b, bit * GRAIN, 1))
                blocks[i | bit] = jnp.where(low, pltpu.roll(a, LANES - bit * GRAIN, 1), b)
        bit //= 2
    return blocks


def swap_halves(a, b):
    low = lane_ids(a.shape[0]) < LANES // 2
    return (
        jnp.where(low, a, pltpu.roll(b, LANES // 2, 1)),
        jnp.where(low, pltpu.roll(a, LANES // 2, 1), b),
    )


def transpose_matrix():
    i = lax.broadcasted_iota(jnp.int32, (256, 256), 0)
    j = lax.broadcasted_iota(jnp.int32, (256, 256), 1)
    return ((i // 16 == j % 16) & (i % 16 == j // 16)).astype(F32).astype(BF16)


def split_two(x):
    high = x.astype(BF16)
    return high, (x - high.astype(F32)).astype(BF16)


def split_three(x):
    high, _ = split_two(x)
    rest = x - high.astype(F32)
    middle = rest.astype(BF16)
    return high, middle, (rest - middle.astype(F32)).astype(BF16)


def mm(a, b):
    return jnp.dot(a, b, preferred_element_type=F32)


def move_lanes(x, matrix):
    high, middle, low = split_three(x)
    return (mm(high, matrix) + mm(middle, matrix)) + mm(low, matrix)


def pack_kernel(place, adj, east, north, regime, cell, owner, station, weight, out):
    levels = adj.shape[1]
    rows = adj.shape[2]
    for pair in range(3):
        if pair < 2:
            srcs = [adj[2 * pair + k, :, r, :] for k in range(2) for r in range(rows)]
        else:
            srcs = [w[:, r, :] for w in (east, north) for r in range(rows)]
        for half in range(2):
            lanes = slice(half * LANES, (half + 1) * LANES)
            for j, piece in enumerate(swap_grains([s[:, lanes] for s in srcs])):
                out[place[half * 8 + j], pair * levels : (pair + 1) * levels, :] = piece
    first = 3 * levels
    srcs = [regime[h, r : r + 1, :].astype(F32) for h in range(HOURS) for r in range(rows)]
    cells = cell[0]
    level, lon = cells // 256, cells % 256
    stations = (owner[...] * SPO + station[0]).astype(F32)
    weights = weight[0]
    for half in range(2):
        lanes = slice(half * LANES, (half + 1) * LANES)
        for j, piece in enumerate(swap_grains([s[:, lanes] for s in srcs])):
            d = half * 8 + j
            g = place[d]
            out[g, first : first + 1, :] = piece
            here = lon - d * GRAIN
            code = jnp.where((here >= 0) & (here < GRAIN), here * FOOT_LEVELS + level, -1).astype(F32)
            for k in range(4):
                part = slice(k * LANES, (k + 1) * LANES)
                out[g, first + 2 + k : first + 3 + k, :] = code[:, part]
                out[g, first + 6 + k : first + 7 + k, :] = stations[:, part]
                out[g, first + 10 + k : first + 11 + k, :] = weights[:, part]


def solve_columns(high, low, kz_high, kz_low, regime, levels):
    product = mm(kz_high, high) + (mm(kz_low, high) + mm(kz_high, low))
    result = product[:levels]
    for k in range(1, REGIMES):
        result = jnp.where(regime == float(k), product[k * levels : (k + 1) * levels], result)
    return result


def mixing(kz):
    stacked = jnp.concatenate([kz[k].T for k in range(REGIMES)], axis=0)
    return split_two(stacked)


def rim_messages(top, bottom, first, last, rows):
    half = LANES // 2
    low = lane_ids(top.shape[0]) < half
    first[rows, :] = jnp.where(low, top[:, :LANES], pltpu.roll(bottom[:, :LANES], half, 1))
    last[rows, :] = jnp.where(low, pltpu.roll(top[:, LANES:], half, 1), bottom[:, LANES:])


def unpack_solve_kernel(n_lev, recv, kz, solved, winds, regimes, first, last, field):
    per = recv.shape[0] // n_lev
    total = kz.shape[1]
    levels = total // n_lev
    for pair in range(3):
        for z in range(n_lev):
            for half in range(2):
                lanes = slice(half * LANES, (half + 1) * LANES)
                a, b = [
                    recv[(2 * half + k) * n_lev + z, pair * levels : (pair + 1) * levels, :]
                    for k in range(2)
                ]
                for k, value in enumerate(swap_halves(a, b)):
                    base = (2 * pair + k) * total + z * levels
                    field[base : base + levels, lanes] = value
    base = 6 * total
    field[base : base + 8, :] = jnp.zeros((8, 256), F32)
    for half in range(2):
        lanes = slice(half * LANES, (half + 1) * LANES)
        a, b = [
            recv[(2 * half + k) * n_lev, 3 * levels : 3 * levels + 1, :] for k in range(2)
        ]
        for k, value in enumerate(swap_halves(a, b)):
            field[base + k : base + k + 1, lanes] = value
    matrix = transpose_matrix()
    regime = mm(field[base : base + 8, :].astype(BF16), matrix)
    regimes[...] = regime
    kz_high, kz_low = mixing(kz)
    for k in range(2):
        winds[k * total : (k + 1) * total, :] = move_lanes(
            field[(4 + k) * total : (5 + k) * total, :], matrix
        )
    for t in range(4):
        high, low = split_two(field[t * total : (t + 1) * total, :])
        high = mm(high, matrix).astype(BF16)
        low = mm(low, matrix).astype(BF16)
        solved[t * total : (t + 1) * total, :] = solve_columns(
            high, low, kz_high, kz_low, regime[0:1], total
        )
    rim_messages(
        solved[0 : 2 * total, :], solved[2 * total :, :], first, last, slice(0, 2 * total)
    )
    rim_messages(
        winds[0:total, :], winds[total:, :], first, last, slice(2 * total, 3 * total)
    )


def with_rims(main, from_east, from_west, upper):
    half = LANES // 2
    low = lane_ids(main.shape[0]) < half
    if upper:
        rim = jnp.where(low, pltpu.roll(from_east, half, 1), from_west)
    else:
        rim = jnp.where(low, from_east, pltpu.roll(from_west, half, 1))
    return jnp.concatenate([main, rim], axis=1)


def face_weights(lat_count, winds, from_east, from_west, total, faces):
    width = 384
    rims = slice(2 * total, 3 * total)
    east = with_rims(winds[0:total, :], from_east[rims, :], from_west[rims, :], False)
    north = with_rims(winds[total:, :], from_east[rims, :], from_west[rims, :], True)
    lat = lax.broadcasted_iota(jnp.int32, (total, width), 1) % lat_count
    north = jnp.where(lat == lat_count - 1, 0.0, north)
    south = pltpu.roll(north, 1, 1)
    west = pltpu.roll(east, lat_count, 1)
    faces[0] = jnp.maximum(north, 0.0)
    faces[1] = -jnp.minimum(south, 0.0)
    faces[2] = jnp.maximum(east, 0.0)
    faces[3] = -jnp.minimum(west, 0.0)


def transport(lat_count, field, east_rows, west_rows, faces, total, result):
    width = 384
    block = 8

    @pl.loop(0, total // block)
    def _(step):
        rows = pl.ds(pl.multiple_of(step * block, block), block)
        up, down, right, left = [faces[k, rows, :] for k in range(4)]
        for t in range(4):
            own = pl.ds(pl.multiple_of(t * total + step * block, block), block)
            rim = pl.ds(pl.multiple_of((t % 2) * total + step * block, block), block)
            f = with_rims(field[own, :], east_rows[rim, :], west_rows[rim, :], t >= 2)
            for _ in range(NSUB):
                f = (
                    f
                    + up * (pltpu.roll(f, width - 1, 1) - f)
                    + down * (pltpu.roll(f, 1, 1) - f)
                )
                f = (
                    f
                    + right * (pltpu.roll(f, width - lat_count, 1) - f)
                    + left * (pltpu.roll(f, lat_count, 1) - f)
                )
            result[own, :] = f[:, :256]


def transport_solve_kernel(
    lat_count, field, winds, regimes, kz, from_east, from_west, solved, first, last, faces, moved
):
    total = kz.shape[1]
    face_weights(lat_count, winds, from_east, from_west, total, faces)
    transport(lat_count, field, from_east, from_west, faces, total, moved)
    kz_high, kz_low = mixing(kz)
    for t in range(4):
        high, low = split_two(moved[t * total : (t + 1) * total, :])
        solved[t * total : (t + 1) * total, :] = solve_columns(
            high, low, kz_high, kz_low, regimes[1:2, :], total
        )
    rim_messages(
        solved[0 : 2 * total, :], solved[2 * total :, :], first, last, slice(0, 2 * total)
    )


def footprint_kernel(entry_row, recv, hour_0, hour_1, sums):
    total = hour_0.shape[0] // 4
    matrix = transpose_matrix()
    low = jnp.concatenate(
        [h[t * total : t * total + FOOT_LEVELS, :] for h in (hour_0, hour_1) for t in range(4)],
        axis=0,
    )
    parts = mm(jnp.concatenate(split_three(low), axis=0), matrix).astype(BF16)
    count = low.shape[0]
    acc = jnp.zeros((count, 64), F32)
    cell_ids = lax.broadcasted_iota(jnp.int32, (GRAIN, 512), 0)
    level_ids = lax.broadcasted_iota(jnp.int32, (FOOT_LEVELS, 512), 0)
    station_ids = lax.broadcasted_iota(jnp.int32, (64, 512), 0)
    for row in range(recv.shape[0]):
        def entries(at):
            return jnp.concatenate(
                [recv[row, at + k : at + k + 1, :] for k in range(4)], axis=1
            )

        code = entries(entry_row).astype(jnp.int32)
        station = entries(entry_row + 4).astype(jnp.int32)
        weight = entries(entry_row + 8)
        cells = ((code >> 3) == cell_ids).astype(F32).astype(BF16)
        picked = mm(parts[:, row * GRAIN : (row + 1) * GRAIN], cells)
        picked = (picked[:count] + picked[count : 2 * count]) + picked[2 * count :]
        level = jnp.where((code & 7) == level_ids, weight, 0.0)
        picked = picked * jnp.concatenate([level] * (count // FOOT_LEVELS), axis=0)
        named = (station == station_ids).astype(F32).astype(BF16)
        high, rest = split_two(picked)
        both = jnp.concatenate([high, rest], axis=0)
        both = lax.dot_general(both, named, (((1,), (1,)), ((), ())), preferred_element_type=F32)
        acc = acc + (both[:count] + both[count:])
    sums[...] = jnp.sum(acc.reshape(count // FOOT_LEVELS, FOOT_LEVELS, 64), axis=1)


def transport_pack_kernel(
    lat_count, n_lev, field, winds, from_east_0, from_west_0, from_east, from_west, sums, out,
    faces, moved,
):
    total = winds.shape[0] // 2
    levels = total // n_lev
    face_weights(lat_count, winds, from_east_0, from_west_0, total, faces)
    transport(lat_count, field, from_east, from_west, faces, total, moved)
    matrix = transpose_matrix()
    for pair in range(2):
        for k in range(2):
            rows = slice((2 * pair + k) * total, (2 * pair + k + 1) * total)
            moved[rows, :] = move_lanes(moved[rows, :], matrix)
        for z in range(n_lev):
            for half in range(2):
                lanes = slice(half * LANES, (half + 1) * LANES)
                a, b = [
                    moved[
                        (2 * pair + k) * total + z * levels : (2 * pair + k) * total
                        + (z + 1) * levels,
                        lanes,
                    ]
                    for k in range(2)
                ]
                for k, value in enumerate(swap_halves(a, b)):
                    out[
                        (2 * half + k) * n_lev + z, pair * levels : (pair + 1) * levels, :
                    ] = value
    wide = jnp.concatenate([sums[...], jnp.zeros((8, 64), F32)], axis=1)
    line = lax.broadcasted_iota(jnp.int32, (8, LANES), 0)
    spread = jnp.zeros((8, LANES), F32)
    for k in range(8):
        spread = jnp.where(line == k, pltpu.roll(wide, 4 * k, 1) if k else wide, spread)
    keep = lax.broadcasted_iota(jnp.int32, (8, LANES), 1) // 4 == line
    for g in range(out.shape[0]):
        value = pltpu.roll(spread, LANES - 4 * g, 1) if g else spread
        value = jnp.sum(jnp.where(keep, value, 0.0), axis=0, keepdims=True)
        out[g, 2 * levels : 2 * levels + 1, :] = value


def unpack_kernel(place, recv, final, stations):
    levels = final.shape[1]
    for pair in range(2):
        for half in range(2):
            lanes = slice(half * LANES, (half + 1) * LANES)
            blocks = [
                recv[place[half * 8 + j], pair * levels : (pair + 1) * levels, :]
                for j in range(8)
            ]
            for i, value in enumerate(swap_grains(blocks)):
                k, r = divmod(i, 4)
                final[2 * pair + k, :, r, lanes] = value
    line = recv[0, 2 * levels : 2 * levels + 1, :]
    for g in range(1, recv.shape[0]):
        line = line + recv[g, 2 * levels : 2 * levels + 1, :]
    for h in range(HOURS):
        for t in range(4):
            at = (h * 4 + t) * 4
            stations[h, t, :, :] = line[:, at : at + 4]


def call(kernel, outs, scratch=()):
    return pl.pallas_call(
        kernel,
        out_shape=[jax.ShapeDtypeStruct(s, F32) for s in outs],
        scratch_shapes=[pltpu.VMEM(s, F32) for s in scratch],
        compiler_params=pltpu.CompilerParams(vmem_limit_bytes=48 * 1024 * 1024),
    )


def regrouped(sizes, adjoint, wind_east, wind_north, kz_inverse, kz_regime, fp_cell, fp_owner, fp_station, fp_weight):
    n_lat, n_lev, n_lon = sizes
    levels = adjoint.shape[1]
    total = levels * n_lev
    group = n_lat * n_lev
    lat_count = n_lat * adjoint.shape[2]
    place = chunk_owner(n_lat, n_lev)
    to_west = ring_perm(n_lat, n_lev, n_lon, -1)
    to_east = ring_perm(n_lat, n_lev, n_lon, 1)

    def exchange(x):
        return lax.all_to_all(x, AXES, split_axis=0, concat_axis=0, tiled=True)

    def rims(first, last):
        return lax.ppermute(first, RING, to_west), lax.ppermute(last, RING, to_east)

    in_rows = 3 * levels + 14
    in_rows += -in_rows % 8
    out_rows = 2 * levels + 1
    out_rows += -out_rows % 8
    (sent,) = call(functools.partial(pack_kernel, place), [(group, in_rows, LANES)])(
        adjoint, wind_east, wind_north, kz_regime, fp_cell, fp_owner.reshape(1, -1), fp_station, fp_weight
    )
    recv = exchange(sent)
    solved_0, winds, regimes, first, last = call(
        functools.partial(unpack_solve_kernel, n_lev),
        [(4 * total, 256), (2 * total, 256), (8, 256), (3 * total, LANES), (3 * total, LANES)],
        [(6 * total + 8, 256)],
    )(recv, kz_inverse)
    east_0, west_0 = rims(first, last)
    solved_1, first, last = call(
        functools.partial(transport_solve_kernel, lat_count),
        [(4 * total, 256), (2 * total, LANES), (2 * total, LANES)],
        [(4, total, 384), (4 * total, 256)],
    )(solved_0, winds, regimes, kz_inverse, east_0, west_0)
    east_1, west_1 = rims(first, last)
    (sums,) = call(functools.partial(footprint_kernel, 3 * levels + 2), [(8, 64)])(
        recv, solved_0, solved_1
    )
    (back,) = call(
        functools.partial(transport_pack_kernel, lat_count, n_lev),
        [(group, out_rows, LANES)],
        [(4, total, 384), (4 * total, 256)],
    )(solved_1, winds, east_0, west_0, east_1, west_1, sums)
    final, stations = call(
        functools.partial(unpack_kernel, place), [adjoint.shape, (HOURS, 4, 1, SPO)]
    )(exchange(back))
    return final, stations


def padded_2(x, sides, width, wrap):
    for axis, dim in sides:
        peers, length = (lax.axis_size(axis), x.shape[dim])
        up = [(i, (i + 1) % peers) for i in range(peers if wrap else peers - 1)]
        down = [(j, i) for i, j in up]
        last = lax.slice_in_dim(x, length - width, length, axis=dim)
        initial = lax.slice_in_dim(x, 0, width, axis=dim)
        before = lax.ppermute(last, axis, up)
        after = lax.ppermute(initial, axis, down)
        x = jnp.concatenate([before, x, after], axis=dim)
    return x


def lat_rim(values, rim_width):
    return padded_2(values, (("lat", 2),), rim_width, False)


def lon_rim(values, rim_width):
    return padded_2(values, (("lon", 3),), rim_width, True)


def lat_sweep(padded, north_face, south_face):
    middle = padded[:, :, 1:-1]
    return (
        middle
        + jnp.maximum(north_face, 0.0) * (padded[:, :, 2:] - middle)
        - jnp.minimum(south_face, 0.0) * (padded[:, :, :-2] - middle)
    )


def lon_sweep(padded, east_face, west_face):
    middle = padded[:, :, :, 1:-1]
    return (
        middle
        + jnp.maximum(east_face, 0.0) * (padded[:, :, :, 2:] - middle)
        - jnp.minimum(west_face, 0.0) * (padded[:, :, :, :-2] - middle)
    )


def shards(
    adjoint, wind_east, wind_north, kz_inverse, kz_regime, fp_cell, fp_owner, fp_station, fp_weight
):
    tracers, levels_dev, lat_rows, lon_cells = adjoint.shape
    row_index = lax.axis_index("lat") * lat_rows + lax.broadcasted_iota(
        jnp.int32, (1, lat_rows, 1), 1
    )
    last_row = lat_rows * lax.axis_size("lat") - 1
    north_face = jnp.where(row_index == last_row, jnp.zeros_like(wind_north), wind_north)
    south_face = lat_rim(north_face[None], 1)[0][:, :-2]
    west_face = lon_rim(wind_east[None], 1)[0][:, :, :-2]
    groups = lax.axis_size("lat") * lax.axis_size("lev")
    column_count = lat_rows * lon_cells // lax.axis_size("lev")
    first_column = lax.axis_index("lev") * column_count
    regime_rows = kz_regime.reshape(HOURS, lat_rows * lon_cells)
    cell_ids = fp_cell.reshape(-1)
    owners = fp_owner.reshape(-1)
    stations = fp_station.reshape(-1)
    weights = fp_weight.reshape(-1)
    entries = cell_ids.shape[0]
    adjoint_field = adjoint
    outputs = []
    for hour_step in range(HOURS):
        chosen = lax.dynamic_slice_in_dim(regime_rows[hour_step], first_column, column_count, 0)

        def column_solve(columns, chosen=chosen):
            result = jnp.zeros_like(columns)
            for regime in range(REGIMES):
                product = jnp.einsum(
                    "ji,tjp->tip", kz_inverse[regime], columns, precision=lax.Precision.HIGHEST
                )
                result = jnp.where(chosen[None, None, :] == regime, product, result)
            returned = lax.all_to_all(result, "lev", split_axis=1, concat_axis=2, tiled=True)
            return (returned, result)

        flat_field = adjoint_field.reshape(tracers, levels_dev, lat_rows * lon_cells)
        returned, solved = column_solve(
            lax.all_to_all(flat_field, "lev", split_axis=2, concat_axis=1, tiled=True)
        )
        lowest = solved[:, :FOOT_LEVELS, :].reshape(tracers, -1)
        picked = jnp.take(lowest, cell_ids, axis=1) * weights[None, :]
        capacity = 2 * entries // groups
        owner_hits = (owners[:, None] == jnp.arange(groups, dtype=jnp.int32)[None, :]).astype(
            jnp.int32
        )
        bucket_rank = jnp.sum(jnp.cumsum(owner_hits, axis=0) * owner_hits, axis=1) - 1
        slot_pos = owners * capacity + bucket_rank
        send_values = (
            jnp.zeros((tracers, groups * capacity), jnp.float32).at[:, slot_pos].set(picked)
        )
        send_ids = jnp.full((groups * capacity,), -1, jnp.int32).at[slot_pos].set(stations)
        arrived_values, arrived_ids = (
            lax.all_to_all(
                send_values.reshape(tracers, groups, capacity),
                ("lat", "lev"),
                split_axis=1,
                concat_axis=1,
                tiled=True,
            ),
            lax.all_to_all(
                send_ids.reshape(1, groups, capacity),
                ("lat", "lev"),
                split_axis=1,
                concat_axis=1,
                tiled=True,
            ),
        )
        matches = (
            arrived_ids[0][:, :, None] == jnp.arange(SPO, dtype=jnp.int32)[None, None, :]
        ).astype(jnp.float32)
        station_sums = jnp.einsum(
            "tgc,gcs->ts", arrived_values, matches, precision=lax.Precision.HIGHEST
        )
        outputs.append(station_sums)
        adjoint_field = returned.reshape(tracers, levels_dev, lat_rows, lon_cells)
        for substep in range(NSUB):
            adjoint_field = lat_sweep(lat_rim(adjoint_field, 1), north_face, south_face)
            adjoint_field = lon_sweep(lon_rim(adjoint_field, 1), wind_east, west_face)
    return (adjoint_field, jnp.stack(outputs)[:, :, None, :])


def fits(mesh_sizes, shape, kz_shape, entries):
    n_lat, n_lev, n_lon = mesh_sizes
    tracers, levels, rows, cells = shape
    return (
        tracers == 4
        and rows == 4
        and cells == 256
        and n_lat == 4
        and n_lat * n_lev == 16
        and levels * n_lev == kz_shape[1]
        and kz_shape[1] % 8 == 0
        and entries == 512
    )


def device_part(sizes, *arrays):
    if fits(sizes, arrays[0].shape, arrays[3].shape, arrays[5].shape[-1]):
        return regrouped(sizes, *arrays)
    return shards(*arrays)


def solution(mesh):
    sizes = tuple(mesh.shape[name] for name in RING)
    in_specs = (
        P(None, "lev", "lat", "lon"),
        P("lev", "lat", "lon"),
        P("lev", "lat", "lon"),
        P(),
        P(None, "lat", "lon"),
        P(AXES, "lon", None),
        P(AXES, "lon", None, None),
        P(AXES, "lon", None),
        P(AXES, "lon", None),
    )
    out_specs = (P(None, "lev", "lat", "lon"), P(None, None, "lon", AXES))
    return jax.shard_map(
        functools.partial(device_part, sizes),
        mesh=mesh,
        in_specs=in_specs,
        out_specs=out_specs,
        check_vma=False,
    )
```

```python
import functools
import jax
import jax.numpy as jnp
from jax import lax
from jax.experimental import pallas as pl
from jax.experimental.pallas import tpu as pltpu
from jax.sharding import PartitionSpec as P

NSUB = 4
HOURS = 2
REGIMES = 4
FOOT_LEVELS = 8
SPO = 4
LANES = 128
GRAIN = 16
F32 = jnp.float32
BF16 = jnp.bfloat16
AXES = ("lat", "lev")
RING = ("lat", "lev", "lon")


def chunk_owner(n_lat, n_lev):
    place = [0] * (n_lat * n_lev)
    for a in range(n_lat):
        for z in range(n_lev):
            chip, core = divmod(a, 2)
            step = z if chip % 2 == 0 else n_lev - 1 - z
            place[(chip * n_lev + step) * 2 + core] = a * n_lev + z
    return place


def ring_perm(n_lat, n_lev, n_lon, shift):
    place = chunk_owner(n_lat, n_lev)
    ring = [place[d] * n_lon + o for o in range(n_lon) for d in range(len(place))]
    count = len(ring)
    return [(ring[i], ring[(i + shift) % count]) for i in range(count)]


def lane_ids(rows):
    return lax.broadcasted_iota(jnp.int32, (rows, LANES), 1)


def swap_grains(blocks):
    blocks = list(blocks)
    grain = lane_ids(blocks[0].shape[0]) // GRAIN
    bit = len(blocks) // 2
    while bit:
        low = (grain & bit) == 0
        for i in range(len(blocks)):
            if i & bit == 0:
                a, b = blocks[i], blocks[i | bit]
                blocks[i] = jnp.where(low, a, pltpu.roll(b, bit * GRAIN, 1))
                blocks[i | bit] = jnp.where(low, pltpu.roll(a, LANES - bit * GRAIN, 1), b)
        bit //= 2
    return blocks


def swap_halves(a, b):
    low = lane_ids(a.shape[0]) < LANES // 2
    return (
        jnp.where(low, a, pltpu.roll(b, LANES // 2, 1)),
        jnp.where(low, pltpu.roll(a, LANES // 2, 1), b),
    )


def transpose_matrix():
    i = lax.broadcasted_iota(jnp.int32, (256, 256), 0)
    j = lax.broadcasted_iota(jnp.int32, (256, 256), 1)
    return ((i // 16 == j % 16) & (i % 16 == j // 16)).astype(F32).astype(BF16)


def split_two(x):
    high = x.astype(BF16)
    return high, (x - high.astype(F32)).astype(BF16)


def split_three(x):
    high, _ = split_two(x)
    rest = x - high.astype(F32)
    middle = rest.astype(BF16)
    return high, middle, (rest - middle.astype(F32)).astype(BF16)


def mm(a, b):
    return jnp.dot(a, b, preferred_element_type=F32)


def move_lanes(x, matrix):
    high, middle, low = split_three(x)
    return (mm(high, matrix) + mm(middle, matrix)) + mm(low, matrix)


def pack_kernel(place, *refs):
    count = (len(refs) - 2) // 2
    given, out, held, sems = refs[:count], refs[count], refs[count + 1 : -1], refs[-1]
    copies = [
        pltpu.make_async_copy(a, b, sems.at[i]) for i, (a, b) in enumerate(zip(given, held))
    ]
    for copy in copies:
        copy.start()
    for copy in copies:
        copy.wait()
    pack(place, *held, out)


def pack(place, adj, east, north, regime, cell, owner, station, weight, out):
    levels = adj.shape[1]
    rows = adj.shape[2]
    for pair in range(3):
        if pair < 2:
            srcs = [adj[2 * pair + k, :, r, :] for k in range(2) for r in range(rows)]
        else:
            srcs = [w[:, r, :] for w in (east, north) for r in range(rows)]
        for half in range(2):
            lanes = slice(half * LANES, (half + 1) * LANES)
            for j, piece in enumerate(swap_grains([s[:, lanes] for s in srcs])):
                out[place[half * 8 + j], pair * levels : (pair + 1) * levels, :] = piece
    first = 3 * levels
    srcs = [regime[h, r : r + 1, :].astype(F32) for h in range(HOURS) for r in range(rows)]
    cells = cell[0]
    level, lon = cells // 256, cells % 256
    stations = (owner[...] * SPO + station[0]).astype(F32)
    weights = weight[0]
    for half in range(2):
        lanes = slice(half * LANES, (half + 1) * LANES)
        for j, piece in enumerate(swap_grains([s[:, lanes] for s in srcs])):
            d = half * 8 + j
            g = place[d]
            out[g, first : first + 1, :] = piece
            here = lon - d * GRAIN
            code = jnp.where((here >= 0) & (here < GRAIN), here * FOOT_LEVELS + level, -1).astype(F32)
            for k in range(4):
                part = slice(k * LANES, (k + 1) * LANES)
                out[g, first + 2 + k : first + 3 + k, :] = code[:, part]
                out[g, first + 6 + k : first + 7 + k, :] = stations[:, part]
                out[g, first + 10 + k : first + 11 + k, :] = weights[:, part]


def solve_columns(high, low, kz_high, kz_low, regime, levels):
    product = mm(kz_high, high) + (mm(kz_low, high) + mm(kz_high, low))
    result = product[:levels]
    for k in range(1, REGIMES):
        result = jnp.where(regime == float(k), product[k * levels : (k + 1) * levels], result)
    return result


def mixing(kz):
    stacked = jnp.concatenate([kz[k].T for k in range(REGIMES)], axis=0)
    return split_two(stacked)


def rim_messages(top, bottom, first, last, rows):
    half = LANES // 2
    low = lane_ids(top.shape[0]) < half
    first[rows, :] = jnp.where(low, top[:, :LANES], pltpu.roll(bottom[:, :LANES], half, 1))
    last[rows, :] = jnp.where(low, pltpu.roll(top[:, LANES:], half, 1), bottom[:, LANES:])


def unpack_solve_kernel(n_lev, recv, kz, solved, winds, regimes, first, last, field):
    per = recv.shape[0] // n_lev
    total = kz.shape[1]
    levels = total // n_lev
    for pair in range(3):
        for z in range(n_lev):
            for half in range(2):
                lanes = slice(half * LANES, (half + 1) * LANES)
                a, b = [
                    recv[(2 * half + k) * n_lev + z, pair * levels : (pair + 1) * levels, :]
                    for k in range(2)
                ]
                for k, value in enumerate(swap_halves(a, b)):
                    base = (2 * pair + k) * total + z * levels
                    field[base : base + levels, lanes] = value
    base = 6 * total
    field[base : base + 8, :] = jnp.zeros((8, 256), F32)
    for half in range(2):
        lanes = slice(half * LANES, (half + 1) * LANES)
        a, b = [
            recv[(2 * half + k) * n_lev, 3 * levels : 3 * levels + 1, :] for k in range(2)
        ]
        for k, value in enumerate(swap_halves(a, b)):
            field[base + k : base + k + 1, lanes] = value
    matrix = transpose_matrix()
    regime = mm(field[base : base + 8, :].astype(BF16), matrix)
    regimes[...] = regime
    kz_high, kz_low = mixing(kz)
    for k in range(2):
        winds[k * total : (k + 1) * total, :] = move_lanes(
            field[(4 + k) * total : (5 + k) * total, :], matrix
        )
    for t in range(4):
        high, low = split_two(field[t * total : (t + 1) * total, :])
        high = mm(high, matrix).astype(BF16)
        low = mm(low, matrix).astype(BF16)
        solved[t * total : (t + 1) * total, :] = solve_columns(
            high, low, kz_high, kz_low, regime[0:1], total
        )
    rim_messages(
        solved[0 : 2 * total, :], solved[2 * total :, :], first, last, slice(0, 2 * total)
    )
    rim_messages(
        winds[0:total, :], winds[total:, :], first, last, slice(2 * total, 3 * total)
    )


def rim_lanes(from_east, from_west, rows, upper):
    half = LANES // 2
    east, west = from_east[rows, :], from_west[rows, :]
    low = lane_ids(east.shape[0]) < half
    if upper:
        return jnp.where(low, pltpu.roll(east, half, 1), west)
    return jnp.where(low, east, pltpu.roll(west, half, 1))


def columns(ref, rows):
    return [ref[rows, i * LANES : (i + 1) * LANES] for i in range(3)]


def pair_columns(ref, rows):
    return [ref[rows, i * LANES : (i + 1) * LANES] for i in range(2)]


def turned(x, shift):
    return pltpu.roll(x, shift % LANES, 1)


def stepped(blocks, shift):
    count = len(blocks)
    lane = lane_ids(blocks[0].shape[0])
    moved = [turned(x, shift) for x in blocks]
    if shift > 0:
        return [jnp.where(lane < shift, moved[i - 1], moved[i]) for i in range(count)]
    return [
        jnp.where(lane >= LANES + shift, moved[(i + 1) % count], moved[i]) for i in range(count)
    ]


def face_weights(lat_count, winds, from_east, from_west, total, faces):
    rims = slice(2 * total, 3 * total)
    east = pair_columns(winds, slice(0, total)) + [rim_lanes(from_east, from_west, rims, False)]
    north = pair_columns(winds, slice(total, 2 * total)) + [
        rim_lanes(from_east, from_west, rims, True)
    ]
    lat = lane_ids(total) % lat_count
    north = [jnp.where(lat == lat_count - 1, 0.0, x) for x in north]
    west = stepped(east, lat_count)
    for i in range(3):
        lanes = slice(i * LANES, (i + 1) * LANES)
        after = jnp.maximum(north[i], 0.0)
        before = -jnp.minimum(jnp.where(lat == 0, 0.0, turned(north[i], 1)), 0.0)
        faces[0, :, lanes] = 1.0 - after - before
        faces[1, :, lanes] = after
        faces[2, :, lanes] = before
        after = jnp.maximum(east[i], 0.0)
        before = -jnp.minimum(west[i], 0.0)
        faces[3, :, lanes] = 1.0 - after - before
        faces[4, :, lanes] = after
        faces[5, :, lanes] = before


def transport(lat_count, field, east_rows, west_rows, faces, total, buffers, result):
    for t in range(4):
        own = slice(t * total, (t + 1) * total)
        rim = slice((t % 2) * total, (t % 2 + 1) * total)
        buffers[0, own, 0:256] = field[own, :]
        buffers[0, own, 256:384] = rim_lanes(east_rows, west_rows, rim, t >= 2)
    for step in range(2 * NSUB):
        last = step == 2 * NSUB - 1
        for t in range(4):
            own = slice(t * total, (t + 1) * total)
            f = columns(buffers.at[step % 2], own)
            if step % 2 == 0:
                after = [turned(x, -1) for x in f]
                before = [turned(x, 1) for x in f]
            else:
                after = stepped(f, -lat_count)
                before = stepped(f, lat_count)
            base = 3 * (step % 2)
            for i in range(2 if last else 3):
                lanes = slice(i * LANES, (i + 1) * LANES)
                value = (
                    faces[base, :, lanes] * f[i]
                    + faces[base + 1, :, lanes] * after[i]
                    + faces[base + 2, :, lanes] * before[i]
                )
                if last:
                    result[own, lanes] = value
                else:
                    buffers[(step + 1) % 2, own, lanes] = value


def transport_solve_kernel(
    lat_count, field, winds, regimes, kz, from_east, from_west, solved, first, last, faces, buffers, moved
):
    total = kz.shape[1]
    face_weights(lat_count, winds, from_east, from_west, total, faces)
    transport(lat_count, field, from_east, from_west, faces, total, buffers, moved)
    kz_high, kz_low = mixing(kz)
    for t in range(4):
        high, low = split_two(moved[t * total : (t + 1) * total, :])
        solved[t * total : (t + 1) * total, :] = solve_columns(
            high, low, kz_high, kz_low, regimes[1:2, :], total
        )
    rim_messages(
        solved[0 : 2 * total, :], solved[2 * total :, :], first, last, slice(0, 2 * total)
    )


def footprint_kernel(entry_row, recv, hour_0, hour_1, sums):
    total = hour_0.shape[0] // 4
    matrix = transpose_matrix()
    low = jnp.concatenate(
        [h[t * total : t * total + FOOT_LEVELS, :] for h in (hour_0, hour_1) for t in range(4)],
        axis=0,
    )
    parts = mm(jnp.concatenate(split_three(low), axis=0), matrix).astype(BF16)
    count = low.shape[0]
    acc = jnp.zeros((count, 64), F32)
    cell_ids = lax.broadcasted_iota(jnp.int32, (GRAIN, 512), 0)
    level_ids = lax.broadcasted_iota(jnp.int32, (FOOT_LEVELS, 512), 0)
    station_ids = lax.broadcasted_iota(jnp.int32, (64, 512), 0)
    for row in range(recv.shape[0]):
        def entries(at):
            return jnp.concatenate(
                [recv[row, at + k : at + k + 1, :] for k in range(4)], axis=1
            )

        code = entries(entry_row).astype(jnp.int32)
        station = entries(entry_row + 4).astype(jnp.int32)
        weight = entries(entry_row + 8)
        cells = ((code >> 3) == cell_ids).astype(F32).astype(BF16)
        picked = mm(parts[:, row * GRAIN : (row + 1) * GRAIN], cells)
        picked = (picked[:count] + picked[count : 2 * count]) + picked[2 * count :]
        level = jnp.where((code & 7) == level_ids, weight, 0.0)
        picked = picked * jnp.concatenate([level] * (count // FOOT_LEVELS), axis=0)
        named = (station == station_ids).astype(F32).astype(BF16)
        high, rest = split_two(picked)
        both = jnp.concatenate([high, rest], axis=0)
        both = lax.dot_general(both, named, (((1,), (1,)), ((), ())), preferred_element_type=F32)
        acc = acc + (both[:count] + both[count:])
    sums[...] = jnp.sum(acc.reshape(count // FOOT_LEVELS, FOOT_LEVELS, 64), axis=1)


def transport_pack_kernel(
    lat_count, n_lev, field, winds, from_east_0, from_west_0, from_east, from_west, sums, out,
    faces, buffers, moved,
):
    total = winds.shape[0] // 2
    levels = total // n_lev
    face_weights(lat_count, winds, from_east_0, from_west_0, total, faces)
    transport(lat_count, field, from_east, from_west, faces, total, buffers, moved)
    matrix = transpose_matrix()
    for pair in range(2):
        for k in range(2):
            rows = slice((2 * pair + k) * total, (2 * pair + k + 1) * total)
            moved[rows, :] = move_lanes(moved[rows, :], matrix)
        for z in range(n_lev):
            for half in range(2):
                lanes = slice(half * LANES, (half + 1) * LANES)
                a, b = [
                    moved[
                        (2 * pair + k) * total + z * levels : (2 * pair + k) * total
                        + (z + 1) * levels,
                        lanes,
                    ]
                    for k in range(2)
                ]
                for k, value in enumerate(swap_halves(a, b)):
                    out[
                        (2 * half + k) * n_lev + z, pair * levels : (pair + 1) * levels, :
                    ] = value
    wide = jnp.concatenate([sums[...], jnp.zeros((8, 64), F32)], axis=1)
    line = lax.broadcasted_iota(jnp.int32, (8, LANES), 0)
    spread = jnp.zeros((8, LANES), F32)
    for k in range(8):
        spread = jnp.where(line == k, pltpu.roll(wide, 4 * k, 1) if k else wide, spread)
    keep = lax.broadcasted_iota(jnp.int32, (8, LANES), 1) // 4 == line
    for g in range(out.shape[0]):
        value = pltpu.roll(spread, LANES - 4 * g, 1) if g else spread
        value = jnp.sum(jnp.where(keep, value, 0.0), axis=0, keepdims=True)
        out[g, 2 * levels : 2 * levels + 1, :] = value


def unpack_kernel(place, recv, final, stations):
    levels = final.shape[1]
    for pair in range(2):
        for half in range(2):
            lanes = slice(half * LANES, (half + 1) * LANES)
            blocks = [
                recv[place[half * 8 + j], pair * levels : (pair + 1) * levels, :]
                for j in range(8)
            ]
            for i, value in enumerate(swap_grains(blocks)):
                k, r = divmod(i, 4)
                final[2 * pair + k, :, r, lanes] = value
    line = recv[0, 2 * levels : 2 * levels + 1, :]
    for g in range(1, recv.shape[0]):
        line = line + recv[g, 2 * levels : 2 * levels + 1, :]
    for h in range(HOURS):
        for t in range(4):
            at = (h * 4 + t) * 4
            stations[h, t, :, :] = line[:, at : at + 4]


def call(kernel, outs, scratch=()):
    return pl.pallas_call(
        kernel,
        out_shape=[jax.ShapeDtypeStruct(s, F32) for s in outs],
        scratch_shapes=[pltpu.VMEM(s, F32) for s in scratch],
        compiler_params=pltpu.CompilerParams(vmem_limit_bytes=48 * 1024 * 1024),
    )


def regrouped(sizes, adjoint, wind_east, wind_north, kz_inverse, kz_regime, fp_cell, fp_owner, fp_station, fp_weight):
    n_lat, n_lev, n_lon = sizes
    levels = adjoint.shape[1]
    total = levels * n_lev
    group = n_lat * n_lev
    lat_count = n_lat * adjoint.shape[2]
    place = chunk_owner(n_lat, n_lev)
    to_west = ring_perm(n_lat, n_lev, n_lon, -1)
    to_east = ring_perm(n_lat, n_lev, n_lon, 1)

    def exchange(x):
        return lax.all_to_all(x, AXES, split_axis=0, concat_axis=0, tiled=True)

    def rims(first, last):
        return lax.ppermute(first, RING, to_west), lax.ppermute(last, RING, to_east)

    in_rows = 3 * levels + 14
    in_rows += -in_rows % 8
    out_rows = 2 * levels + 1
    out_rows += -out_rows % 8
    given = (
        adjoint, wind_east, wind_north, kz_regime, fp_cell, fp_owner.reshape(1, -1), fp_station, fp_weight
    )
    sent = pl.pallas_call(
        functools.partial(pack_kernel, place),
        in_specs=[pl.BlockSpec(memory_space=pltpu.HBM)] * len(given),
        out_shape=jax.ShapeDtypeStruct((group, in_rows, LANES), F32),
        scratch_shapes=[pltpu.VMEM(x.shape, x.dtype) for x in given]
        + [pltpu.SemaphoreType.DMA((len(given),))],
    )(*given)
    recv = exchange(sent)
    solved_0, winds, regimes, first, last = call(
        functools.partial(unpack_solve_kernel, n_lev),
        [(4 * total, 256), (2 * total, 256), (8, 256), (3 * total, LANES), (3 * total, LANES)],
        [(6 * total + 8, 256)],
    )(recv, kz_inverse)
    east_0, west_0 = rims(first, last)
    solved_1, first, last = call(
        functools.partial(transport_solve_kernel, lat_count),
        [(4 * total, 256), (2 * total, LANES), (2 * total, LANES)],
        [(6, total, 384), (2, 4 * total, 384), (4 * total, 256)],
    )(solved_0, winds, regimes, kz_inverse, east_0, west_0)
    east_1, west_1 = rims(first, last)
    (sums,) = call(functools.partial(footprint_kernel, 3 * levels + 2), [(8, 64)])(
        recv, solved_0, solved_1
    )
    (back,) = call(
        functools.partial(transport_pack_kernel, lat_count, n_lev),
        [(group, out_rows, LANES)],
        [(6, total, 384), (2, 4 * total, 384), (4 * total, 256)],
    )(solved_1, winds, east_0, west_0, east_1, west_1, sums)
    final, stations = call(
        functools.partial(unpack_kernel, place), [adjoint.shape, (HOURS, 4, 1, SPO)]
    )(exchange(back))
    return final, stations


def padded_2(x, sides, width, wrap):
    for axis, dim in sides:
        peers, length = (lax.axis_size(axis), x.shape[dim])
        up = [(i, (i + 1) % peers) for i in range(peers if wrap else peers - 1)]
        down = [(j, i) for i, j in up]
        last = lax.slice_in_dim(x, length - width, length, axis=dim)
        initial = lax.slice_in_dim(x, 0, width, axis=dim)
        before = lax.ppermute(last, axis, up)
        after = lax.ppermute(initial, axis, down)
        x = jnp.concatenate([before, x, after], axis=dim)
    return x


def lat_rim(values, rim_width):
    return padded_2(values, (("lat", 2),), rim_width, False)


def lon_rim(values, rim_width):
    return padded_2(values, (("lon", 3),), rim_width, True)


def lat_sweep(padded, north_face, south_face):
    middle = padded[:, :, 1:-1]
    return (
        middle
        + jnp.maximum(north_face, 0.0) * (padded[:, :, 2:] - middle)
        - jnp.minimum(south_face, 0.0) * (padded[:, :, :-2] - middle)
    )


def lon_sweep(padded, east_face, west_face):
    middle = padded[:, :, :, 1:-1]
    return (
        middle
        + jnp.maximum(east_face, 0.0) * (padded[:, :, :, 2:] - middle)
        - jnp.minimum(west_face, 0.0) * (padded[:, :, :, :-2] - middle)
    )


def shards(
    adjoint, wind_east, wind_north, kz_inverse, kz_regime, fp_cell, fp_owner, fp_station, fp_weight
):
    tracers, levels_dev, lat_rows, lon_cells = adjoint.shape
    row_index = lax.axis_index("lat") * lat_rows + lax.broadcasted_iota(
        jnp.int32, (1, lat_rows, 1), 1
    )
    last_row = lat_rows * lax.axis_size("lat") - 1
    north_face = jnp.where(row_index == last_row, jnp.zeros_like(wind_north), wind_north)
    south_face = lat_rim(north_face[None], 1)[0][:, :-2]
    west_face = lon_rim(wind_east[None], 1)[0][:, :, :-2]
    groups = lax.axis_size("lat") * lax.axis_size("lev")
    column_count = lat_rows * lon_cells // lax.axis_size("lev")
    first_column = lax.axis_index("lev") * column_count
    regime_rows = kz_regime.reshape(HOURS, lat_rows * lon_cells)
    cell_ids = fp_cell.reshape(-1)
    owners = fp_owner.reshape(-1)
    stations = fp_station.reshape(-1)
    weights = fp_weight.reshape(-1)
    entries = cell_ids.shape[0]
    adjoint_field = adjoint
    outputs = []
    for hour_step in range(HOURS):
        chosen = lax.dynamic_slice_in_dim(regime_rows[hour_step], first_column, column_count, 0)

        def column_solve(columns, chosen=chosen):
            result = jnp.zeros_like(columns)
            for regime in range(REGIMES):
                product = jnp.einsum(
                    "ji,tjp->tip", kz_inverse[regime], columns, precision=lax.Precision.HIGHEST
                )
                result = jnp.where(chosen[None, None, :] == regime, product, result)
            returned = lax.all_to_all(result, "lev", split_axis=1, concat_axis=2, tiled=True)
            return (returned, result)

        flat_field = adjoint_field.reshape(tracers, levels_dev, lat_rows * lon_cells)
        returned, solved = column_solve(
            lax.all_to_all(flat_field, "lev", split_axis=2, concat_axis=1, tiled=True)
        )
        lowest = solved[:, :FOOT_LEVELS, :].reshape(tracers, -1)
        picked = jnp.take(lowest, cell_ids, axis=1) * weights[None, :]
        capacity = 2 * entries // groups
        owner_hits = (owners[:, None] == jnp.arange(groups, dtype=jnp.int32)[None, :]).astype(
            jnp.int32
        )
        bucket_rank = jnp.sum(jnp.cumsum(owner_hits, axis=0) * owner_hits, axis=1) - 1
        slot_pos = owners * capacity + bucket_rank
        send_values = (
            jnp.zeros((tracers, groups * capacity), jnp.float32).at[:, slot_pos].set(picked)
        )
        send_ids = jnp.full((groups * capacity,), -1, jnp.int32).at[slot_pos].set(stations)
        arrived_values, arrived_ids = (
            lax.all_to_all(
                send_values.reshape(tracers, groups, capacity),
                ("lat", "lev"),
                split_axis=1,
                concat_axis=1,
                tiled=True,
            ),
            lax.all_to_all(
                send_ids.reshape(1, groups, capacity),
                ("lat", "lev"),
                split_axis=1,
                concat_axis=1,
                tiled=True,
            ),
        )
        matches = (
            arrived_ids[0][:, :, None] == jnp.arange(SPO, dtype=jnp.int32)[None, None, :]
        ).astype(jnp.float32)
        station_sums = jnp.einsum(
            "tgc,gcs->ts", arrived_values, matches, precision=lax.Precision.HIGHEST
        )
        outputs.append(station_sums)
        adjoint_field = returned.reshape(tracers, levels_dev, lat_rows, lon_cells)
        for substep in range(NSUB):
            adjoint_field = lat_sweep(lat_rim(adjoint_field, 1), north_face, south_face)
            adjoint_field = lon_sweep(lon_rim(adjoint_field, 1), wind_east, west_face)
    return (adjoint_field, jnp.stack(outputs)[:, :, None, :])


def fits(mesh_sizes, shape, kz_shape, entries):
    n_lat, n_lev, n_lon = mesh_sizes
    tracers, levels, rows, cells = shape
    return (
        tracers == 4
        and rows == 4
        and cells == 256
        and n_lat == 4
        and n_lat * n_lev == 16
        and levels * n_lev == kz_shape[1]
        and kz_shape[1] % 8 == 0
        and entries == 512
    )


def device_part(sizes, *arrays):
    if fits(sizes, arrays[0].shape, arrays[3].shape, arrays[5].shape[-1]):
        return regrouped(sizes, *arrays)
    return shards(*arrays)


def solution(mesh):
    sizes = tuple(mesh.shape[name] for name in RING)
    in_specs = (
        P(None, "lev", "lat", "lon"),
        P("lev", "lat", "lon"),
        P("lev", "lat", "lon"),
        P(),
        P(None, "lat", "lon"),
        P(AXES, "lon", None),
        P(AXES, "lon", None, None),
        P(AXES, "lon", None),
        P(AXES, "lon", None),
    )
    out_specs = (P(None, "lev", "lat", "lon"), P(None, None, "lon", AXES))
    return jax.shard_map(
        functools.partial(device_part, sizes),
        mesh=mesh,
        in_specs=in_specs,
        out_specs=out_specs,
        check_vma=False,
    )
```

```python
import functools
import jax
import jax.numpy as jnp
from jax import lax
from jax.experimental import pallas as pl
from jax.experimental.pallas import tpu as pltpu
from jax.sharding import PartitionSpec as P

NSUB = 4
HOURS = 2
REGIMES = 4
FOOT_LEVELS = 8
SPO = 4
LANES = 128
GRAIN = 16
ENTRY_ROWS = 16
F32 = jnp.float32
BF16 = jnp.bfloat16
AXES = ("lat", "lev")
RING = ("lat", "lev", "lon")


def chunk_owner(n_lat, n_lev):
    place = [0] * (n_lat * n_lev)
    for a in range(n_lat):
        for z in range(n_lev):
            chip, core = divmod(a, 2)
            step = z if chip % 2 == 0 else n_lev - 1 - z
            place[(chip * n_lev + step) * 2 + core] = a * n_lev + z
    return place


def ring_perm(n_lat, n_lev, n_lon, shift):
    place = chunk_owner(n_lat, n_lev)
    ring = [
        (place[::-1] if o % 2 else place)[d] * n_lon + o
        for o in range(n_lon)
        for d in range(len(place))
    ]
    count = len(ring)
    return [(ring[i], ring[(i + shift) % count]) for i in range(count)]


def owners(place):
    odd = lax.axis_index("lon") % 2 == 1
    return [jnp.where(odd, there, here) for here, there in zip(place, place[::-1])]


def lane_ids(rows):
    return lax.broadcasted_iota(jnp.int32, (rows, LANES), 1)


def swap_grains(blocks):
    blocks = list(blocks)
    grain = lane_ids(blocks[0].shape[0]) // GRAIN
    bit = len(blocks) // 2
    while bit:
        low = (grain & bit) == 0
        for i in range(len(blocks)):
            if i & bit == 0:
                a, b = blocks[i], blocks[i | bit]
                blocks[i] = jnp.where(low, a, pltpu.roll(b, bit * GRAIN, 1))
                blocks[i | bit] = jnp.where(low, pltpu.roll(a, LANES - bit * GRAIN, 1), b)
        bit //= 2
    return blocks


def swap_halves(a, b):
    low = lane_ids(a.shape[0]) < LANES // 2
    return (
        jnp.where(low, a, pltpu.roll(b, LANES // 2, 1)),
        jnp.where(low, pltpu.roll(a, LANES // 2, 1), b),
    )


def transpose_matrix():
    i = lax.broadcasted_iota(jnp.int32, (256, 256), 0)
    j = lax.broadcasted_iota(jnp.int32, (256, 256), 1)
    return ((i // 16 == j % 16) & (i % 16 == j // 16)).astype(F32).astype(BF16)


def split_two(x):
    high = x.astype(BF16)
    return high, (x - high.astype(F32)).astype(BF16)


def split_three(x):
    high, _ = split_two(x)
    rest = x - high.astype(F32)
    middle = rest.astype(BF16)
    return high, middle, (rest - middle.astype(F32)).astype(BF16)


def mm(a, b):
    return jnp.dot(a, b, preferred_element_type=F32)


def move_lanes(x, matrix):
    high, middle, low = split_three(x)
    return (mm(high, matrix) + mm(middle, matrix)) + mm(low, matrix)


def pack_kernel(place, *refs):
    count = (len(refs) - 4) // 2
    given, outs = refs[:count], refs[count : count + 3]
    held, sems = refs[count + 3 : -1], refs[-1]
    place = owners(place)
    copies = [
        pltpu.make_async_copy(a, b, sems.at[i]) for i, (a, b) in enumerate(zip(given, held))
    ]
    for copy in copies:
        copy.start()
    adj, east, north, regime, cell, owner, station, weight = held
    fields, winds, entries = outs
    levels = adj.shape[1]
    rows = adj.shape[2]

    def place_pieces(srcs, out, first, count):
        for half in range(2):
            lanes = slice(half * LANES, (half + 1) * LANES)
            for j, piece in enumerate(swap_grains([s[:, lanes] for s in srcs])):
                out[place[half * 8 + j], first : first + count, :] = piece

    copies[0].wait()
    for pair in range(2):
        srcs = [adj[2 * pair + k, :, r, :] for k in range(2) for r in range(rows)]
        place_pieces(srcs, fields, pair * levels, levels)
    for copy in copies[1:]:
        copy.wait()
    srcs = [w[:, r, :] for w in (east, north) for r in range(rows)]
    place_pieces(srcs, winds, 0, levels)
    srcs = [regime[h, r : r + 1, :].astype(F32) for h in range(HOURS) for r in range(rows)]
    place_pieces(srcs, fields, 2 * levels, 1)
    cells = cell[0].astype(F32)
    stations = (owner[...] * SPO + station[0]).astype(F32)
    for k in range(4):
        part = slice(k * LANES, (k + 1) * LANES)
        entries[k : k + 1, :] = cells[:, part]
        entries[4 + k : 5 + k, :] = stations[:, part]
        entries[8 + k : 9 + k, :] = weight[0][:, part]


def solve_columns(high, low, kz_high, kz_low, regime, levels):
    product = mm(kz_high, high) + (mm(kz_low, high) + mm(kz_high, low))
    result = product[:levels]
    for k in range(1, REGIMES):
        result = jnp.where(regime == float(k), product[k * levels : (k + 1) * levels], result)
    return result


def mixing(kz):
    stacked = jnp.concatenate([kz[k].T for k in range(REGIMES)], axis=0)
    return split_two(stacked)


def rim_messages(top, bottom, first, last, rows):
    half = LANES // 2
    low = lane_ids(top.shape[0]) < half
    first[rows, :] = jnp.where(low, top[:, :LANES], pltpu.roll(bottom[:, :LANES], half, 1))
    last[rows, :] = jnp.where(low, pltpu.roll(top[:, LANES:], half, 1), bottom[:, LANES:])


def unpack_solve_kernel(n_lev, recv, kz, solved, regimes, first, last, field):
    total = kz.shape[1]
    levels = total // n_lev
    for pair in range(2):
        for z in range(n_lev):
            for half in range(2):
                lanes = slice(half * LANES, (half + 1) * LANES)
                a, b = [
                    recv[(2 * half + k) * n_lev + z, pair * levels : (pair + 1) * levels, :]
                    for k in range(2)
                ]
                for k, value in enumerate(swap_halves(a, b)):
                    base = (2 * pair + k) * total + z * levels
                    field[base : base + levels, lanes] = value
    base = 4 * total
    field[base : base + 8, :] = jnp.zeros((8, 256), F32)
    for half in range(2):
        lanes = slice(half * LANES, (half + 1) * LANES)
        a, b = [
            recv[(2 * half + k) * n_lev, 2 * levels : 2 * levels + 1, :] for k in range(2)
        ]
        for k, value in enumerate(swap_halves(a, b)):
            field[base + k : base + k + 1, lanes] = value
    matrix = transpose_matrix()
    regime = mm(field[base : base + 8, :].astype(BF16), matrix)
    regimes[...] = regime
    kz_high, kz_low = mixing(kz)
    for t in range(4):
        high, low = split_two(field[t * total : (t + 1) * total, :])
        high = mm(high, matrix).astype(BF16)
        low = mm(low, matrix).astype(BF16)
        solved[t * total : (t + 1) * total, :] = solve_columns(
            high, low, kz_high, kz_low, regime[0:1], total
        )
    rim_messages(
        solved[0 : 2 * total, :], solved[2 * total :, :], first, last, slice(0, 2 * total)
    )


def unpack_winds_kernel(n_lev, others, winds, first, last, field):
    total = winds.shape[0] // 2
    levels = total // n_lev
    own_lat, own_lev = lax.axis_index("lat"), lax.axis_index("lev")
    for z in range(n_lev):
        for half in range(2):
            lanes = slice(half * LANES, (half + 1) * LANES)
            a, b = [
                others[z ^ own_lev, (2 * half + k) ^ own_lat, 0:levels, :] for k in range(2)
            ]
            for k, value in enumerate(swap_halves(a, b)):
                base = k * total + z * levels
                field[base : base + levels, lanes] = value
    winds[...] = move_lanes(field[...], transpose_matrix())
    rim_messages(winds[0:total, :], winds[total:, :], first, last, slice(0, total))


def rim_lanes(from_east, from_west, rows, upper):
    half = LANES // 2
    east, west = from_east[rows, :], from_west[rows, :]
    low = lane_ids(east.shape[0]) < half
    if upper:
        return jnp.where(low, pltpu.roll(east, half, 1), west)
    return jnp.where(low, east, pltpu.roll(west, half, 1))


def columns(ref, rows):
    return [ref[rows, i * LANES : (i + 1) * LANES] for i in range(3)]


def pair_columns(ref, rows):
    return [ref[rows, i * LANES : (i + 1) * LANES] for i in range(2)]


def turned(x, shift):
    return pltpu.roll(x, shift % LANES, 1)


def stepped(blocks, shift):
    count = len(blocks)
    lane = lane_ids(blocks[0].shape[0])
    moved = [turned(x, shift) for x in blocks]
    if shift > 0:
        return [jnp.where(lane < shift, moved[i - 1], moved[i]) for i in range(count)]
    return [
        jnp.where(lane >= LANES + shift, moved[(i + 1) % count], moved[i]) for i in range(count)
    ]


def face_weights(lat_count, winds, from_east, from_west, total, faces):
    rims = slice(0, total)
    east = pair_columns(winds, slice(0, total)) + [rim_lanes(from_east, from_west, rims, False)]
    north = pair_columns(winds, slice(total, 2 * total)) + [
        rim_lanes(from_east, from_west, rims, True)
    ]
    lat = lane_ids(total) % lat_count
    north = [jnp.where(lat == lat_count - 1, 0.0, x) for x in north]
    west = stepped(east, lat_count)
    for i in range(3):
        lanes = slice(i * LANES, (i + 1) * LANES)
        after = jnp.maximum(north[i], 0.0)
        before = -jnp.minimum(jnp.where(lat == 0, 0.0, turned(north[i], 1)), 0.0)
        faces[0, :, lanes] = 1.0 - after - before
        faces[1, :, lanes] = after
        faces[2, :, lanes] = before
        after = jnp.maximum(east[i], 0.0)
        before = -jnp.minimum(west[i], 0.0)
        faces[3, :, lanes] = 1.0 - after - before
        faces[4, :, lanes] = after
        faces[5, :, lanes] = before


def transport(lat_count, field, east_rows, west_rows, faces, total, buffers, result):
    for t in range(4):
        own = slice(t * total, (t + 1) * total)
        rim = slice((t % 2) * total, (t % 2 + 1) * total)
        buffers[0, own, 0:256] = field[own, :]
        buffers[0, own, 256:384] = rim_lanes(east_rows, west_rows, rim, t >= 2)
    for step in range(2 * NSUB):
        last = step == 2 * NSUB - 1
        for t in range(4):
            own = slice(t * total, (t + 1) * total)
            f = columns(buffers.at[step % 2], own)
            if step % 2 == 0:
                after = [turned(x, -1) for x in f]
                before = [turned(x, 1) for x in f]
            else:
                after = stepped(f, -lat_count)
                before = stepped(f, lat_count)
            base = 3 * (step % 2)
            for i in range(2 if last else 3):
                lanes = slice(i * LANES, (i + 1) * LANES)
                value = (
                    faces[base, :, lanes] * f[i]
                    + faces[base + 1, :, lanes] * after[i]
                    + faces[base + 2, :, lanes] * before[i]
                )
                if last:
                    result[own, lanes] = value
                else:
                    buffers[(step + 1) % 2, own, lanes] = value


def transport_solve_kernel(
    lat_count, field, winds, regimes, kz, wind_east, wind_west, from_east, from_west, solved, first, last, faces, buffers, moved
):
    total = kz.shape[1]
    face_weights(lat_count, winds, wind_east, wind_west, total, faces)
    transport(lat_count, field, from_east, from_west, faces, total, buffers, moved)
    kz_high, kz_low = mixing(kz)
    for t in range(4):
        high, low = split_two(moved[t * total : (t + 1) * total, :])
        solved[t * total : (t + 1) * total, :] = solve_columns(
            high, low, kz_high, kz_low, regimes[1:2, :], total
        )
    rim_messages(
        solved[0 : 2 * total, :], solved[2 * total :, :], first, last, slice(0, 2 * total)
    )


def footprint_kernel(n_lev, entry_row, others, hour_0, hour_1, sums):
    own_lat, own_lev = lax.axis_index("lat"), lax.axis_index("lev")
    chip, core = own_lat // 2, own_lat % 2
    step = jnp.where(chip % 2 == 0, own_lev, n_lev - 1 - own_lev)
    chunk = (chip * n_lev + step) * 2 + core
    odd = lax.axis_index("lon") % 2 == 1
    first_lon = jnp.where(odd, others.shape[0] * others.shape[1] - 1 - chunk, chunk) * GRAIN
    total = hour_0.shape[0] // 4
    matrix = transpose_matrix()
    low = jnp.concatenate(
        [h[t * total : t * total + FOOT_LEVELS, :] for h in (hour_0, hour_1) for t in range(4)],
        axis=0,
    )
    parts = mm(jnp.concatenate(split_three(low), axis=0), matrix).astype(BF16)
    count = low.shape[0]
    acc = jnp.zeros((count, 64), F32)
    cell_ids = lax.broadcasted_iota(jnp.int32, (GRAIN, 512), 0)
    level_ids = lax.broadcasted_iota(jnp.int32, (FOOT_LEVELS, 512), 0)
    station_ids = lax.broadcasted_iota(jnp.int32, (64, 512), 0)
    for row in range(others.shape[0] * others.shape[1]):
        z, a = (row % n_lev) ^ own_lev, (row // n_lev) ^ own_lat

        def entries(at):
            return jnp.concatenate(
                [others[z, a, at + k : at + k + 1, :] for k in range(4)], axis=1
            )

        code = entries(entry_row).astype(jnp.int32)
        station = entries(entry_row + 4).astype(jnp.int32)
        weight = entries(entry_row + 8)
        cells = ((code & 255) - first_lon == cell_ids).astype(F32).astype(BF16)
        picked = mm(parts[:, row * GRAIN : (row + 1) * GRAIN], cells)
        picked = (picked[:count] + picked[count : 2 * count]) + picked[2 * count :]
        level = jnp.where((code >> 8) == level_ids, weight, 0.0)
        picked = picked * jnp.concatenate([level] * (count // FOOT_LEVELS), axis=0)
        named = (station == station_ids).astype(F32).astype(BF16)
        high, rest = split_two(picked)
        both = jnp.concatenate([high, rest], axis=0)
        both = lax.dot_general(both, named, (((1,), (1,)), ((), ())), preferred_element_type=F32)
        acc = acc + (both[:count] + both[count:])
    sums[...] = jnp.sum(acc.reshape(count // FOOT_LEVELS, FOOT_LEVELS, 64), axis=1)


def transport_pack_kernel(
    lat_count, n_lev, field, winds, from_east_0, from_west_0, from_east, from_west, sums, out,
    faces, buffers, moved,
):
    total = winds.shape[0] // 2
    levels = total // n_lev
    face_weights(lat_count, winds, from_east_0, from_west_0, total, faces)
    transport(lat_count, field, from_east, from_west, faces, total, buffers, moved)
    matrix = transpose_matrix()
    for pair in range(2):
        for k in range(2):
            rows = slice((2 * pair + k) * total, (2 * pair + k + 1) * total)
            moved[rows, :] = move_lanes(moved[rows, :], matrix)
        for z in range(n_lev):
            for half in range(2):
                lanes = slice(half * LANES, (half + 1) * LANES)
                a, b = [
                    moved[
                        (2 * pair + k) * total + z * levels : (2 * pair + k) * total
                        + (z + 1) * levels,
                        lanes,
                    ]
                    for k in range(2)
                ]
                for k, value in enumerate(swap_halves(a, b)):
                    out[
                        (2 * half + k) * n_lev + z, pair * levels : (pair + 1) * levels, :
                    ] = value
    wide = jnp.concatenate([sums[...], jnp.zeros((8, 64), F32)], axis=1)
    line = lax.broadcasted_iota(jnp.int32, (8, LANES), 0)
    spread = jnp.zeros((8, LANES), F32)
    for k in range(8):
        spread = jnp.where(line == k, pltpu.roll(wide, 4 * k, 1) if k else wide, spread)
    keep = lax.broadcasted_iota(jnp.int32, (8, LANES), 1) // 4 == line
    for g in range(out.shape[0]):
        value = pltpu.roll(spread, LANES - 4 * g, 1) if g else spread
        value = jnp.sum(jnp.where(keep, value, 0.0), axis=0, keepdims=True)
        out[g, 2 * levels : 2 * levels + 1, :] = value


def unpack_kernel(place, recv, final, stations):
    place = owners(place)
    levels = final.shape[1]
    for pair in range(2):
        for half in range(2):
            lanes = slice(half * LANES, (half + 1) * LANES)
            blocks = [
                recv[place[half * 8 + j], pair * levels : (pair + 1) * levels, :]
                for j in range(8)
            ]
            for i, value in enumerate(swap_grains(blocks)):
                k, r = divmod(i, 4)
                final[2 * pair + k, :, r, lanes] = value
    line = recv[0, 2 * levels : 2 * levels + 1, :]
    for g in range(1, recv.shape[0]):
        line = line + recv[g, 2 * levels : 2 * levels + 1, :]
    for h in range(HOURS):
        for t in range(4):
            at = (h * 4 + t) * 4
            stations[h, t, :, :] = line[:, at : at + 4]


def gather_others(sizes, winds, entries):
    n_lat, n_lev, n_lon = sizes
    own_lat, own_lev = lax.axis_index("lat"), lax.axis_index("lev")
    pieces = winds.reshape(n_lat, n_lev, *winds.shape[1:])

    def swap(x, axis, count, k):
        return lax.ppermute(x, axis, [(i, i ^ k) for i in range(count)])

    def for_lat(k):
        piece = lax.dynamic_index_in_dim(pieces, own_lat ^ k, 0, keepdims=False)
        return jnp.concatenate([piece.reshape(-1, LANES), entries], axis=0)

    here = jnp.stack([for_lat(0)] + [swap(for_lat(k), "lat", n_lat, k) for k in range(1, n_lat)])
    split = n_lev * winds.shape[1]
    pieces = here[:, :split].reshape(n_lat, n_lev, *winds.shape[1:])

    def for_lev(k):
        piece = lax.dynamic_index_in_dim(pieces, own_lev ^ k, 1, keepdims=False)
        return jnp.concatenate([piece, here[:, split:]], axis=1)

    return jnp.stack(
        [for_lev(0)] + [swap(for_lev(k), "lev", n_lev, k) for k in range(1, n_lev)]
    )


def call(kernel, outs, scratch=()):
    return pl.pallas_call(
        kernel,
        out_shape=[jax.ShapeDtypeStruct(s, F32) for s in outs],
        scratch_shapes=[pltpu.VMEM(s, F32) for s in scratch],
        compiler_params=pltpu.CompilerParams(vmem_limit_bytes=48 * 1024 * 1024),
    )


def regrouped(sizes, adjoint, wind_east, wind_north, kz_inverse, kz_regime, fp_cell, fp_owner, fp_station, fp_weight):
    n_lat, n_lev, n_lon = sizes
    levels = adjoint.shape[1]
    total = levels * n_lev
    group = n_lat * n_lev
    lat_count = n_lat * adjoint.shape[2]
    place = chunk_owner(n_lat, n_lev)
    to_west = ring_perm(n_lat, n_lev, n_lon, -1)
    to_east = ring_perm(n_lat, n_lev, n_lon, 1)

    def exchange(x):
        return lax.all_to_all(x, AXES, split_axis=0, concat_axis=0, tiled=True)

    def rims(first, last):
        return lax.ppermute(first, RING, to_west), lax.ppermute(last, RING, to_east)

    out_rows = 2 * levels + 1
    out_rows += -out_rows % 8
    wind_rows = levels + -levels % 8
    given = (
        adjoint, wind_east, wind_north, kz_regime, fp_cell, fp_owner.reshape(1, -1), fp_station, fp_weight
    )
    fields, winds, entries = pl.pallas_call(
        functools.partial(pack_kernel, place),
        in_specs=[pl.BlockSpec(memory_space=pltpu.HBM)] * len(given),
        out_shape=[
            jax.ShapeDtypeStruct(shape, F32)
            for shape in (
                (group, out_rows, LANES), (group, wind_rows, LANES), (ENTRY_ROWS, LANES)
            )
        ],
        scratch_shapes=[pltpu.VMEM(x.shape, x.dtype) for x in given]
        + [pltpu.SemaphoreType.DMA((len(given),))],
    )(*given)
    recv = exchange(fields)
    others = gather_others(sizes, winds, entries)
    solved_0, regimes, first, last = call(
        functools.partial(unpack_solve_kernel, n_lev),
        [(4 * total, 256), (8, 256), (2 * total, LANES), (2 * total, LANES)],
        [(4 * total + 8, 256)],
    )(recv, kz_inverse)
    east_0, west_0 = rims(first, last)
    winds, first, last = call(
        functools.partial(unpack_winds_kernel, n_lev),
        [(2 * total, 256), (total, LANES), (total, LANES)],
        [(2 * total, 256)],
    )(others)
    wind_rims = rims(first, last)
    solved_1, first, last = call(
        functools.partial(transport_solve_kernel, lat_count),
        [(4 * total, 256), (2 * total, LANES), (2 * total, LANES)],
        [(6, total, 384), (2, 4 * total, 384), (4 * total, 256)],
    )(solved_0, winds, regimes, kz_inverse, *wind_rims, east_0, west_0)
    east_1, west_1 = rims(first, last)
    (sums,) = call(functools.partial(footprint_kernel, n_lev, wind_rows), [(8, 64)])(
        others, solved_0, solved_1
    )
    (back,) = call(
        functools.partial(transport_pack_kernel, lat_count, n_lev),
        [(group, out_rows, LANES)],
        [(6, total, 384), (2, 4 * total, 384), (4 * total, 256)],
    )(solved_1, winds, *wind_rims, east_1, west_1, sums)
    final, stations = call(
        functools.partial(unpack_kernel, place), [adjoint.shape, (HOURS, 4, 1, SPO)]
    )(exchange(back))
    return final, stations


def padded_2(x, sides, width, wrap):
    for axis, dim in sides:
        peers, length = (lax.axis_size(axis), x.shape[dim])
        up = [(i, (i + 1) % peers) for i in range(peers if wrap else peers - 1)]
        down = [(j, i) for i, j in up]
        last = lax.slice_in_dim(x, length - width, length, axis=dim)
        initial = lax.slice_in_dim(x, 0, width, axis=dim)
        before = lax.ppermute(last, axis, up)
        after = lax.ppermute(initial, axis, down)
        x = jnp.concatenate([before, x, after], axis=dim)
    return x


def lat_rim(values, rim_width):
    return padded_2(values, (("lat", 2),), rim_width, False)


def lon_rim(values, rim_width):
    return padded_2(values, (("lon", 3),), rim_width, True)


def lat_sweep(padded, north_face, south_face):
    middle = padded[:, :, 1:-1]
    return (
        middle
        + jnp.maximum(north_face, 0.0) * (padded[:, :, 2:] - middle)
        - jnp.minimum(south_face, 0.0) * (padded[:, :, :-2] - middle)
    )


def lon_sweep(padded, east_face, west_face):
    middle = padded[:, :, :, 1:-1]
    return (
        middle
        + jnp.maximum(east_face, 0.0) * (padded[:, :, :, 2:] - middle)
        - jnp.minimum(west_face, 0.0) * (padded[:, :, :, :-2] - middle)
    )


def shards(
    adjoint, wind_east, wind_north, kz_inverse, kz_regime, fp_cell, fp_owner, fp_station, fp_weight
):
    tracers, levels_dev, lat_rows, lon_cells = adjoint.shape
    row_index = lax.axis_index("lat") * lat_rows + lax.broadcasted_iota(
        jnp.int32, (1, lat_rows, 1), 1
    )
    last_row = lat_rows * lax.axis_size("lat") - 1
    north_face = jnp.where(row_index == last_row, jnp.zeros_like(wind_north), wind_north)
    south_face = lat_rim(north_face[None], 1)[0][:, :-2]
    west_face = lon_rim(wind_east[None], 1)[0][:, :, :-2]
    groups = lax.axis_size("lat") * lax.axis_size("lev")
    column_count = lat_rows * lon_cells // lax.axis_size("lev")
    first_column = lax.axis_index("lev") * column_count
    regime_rows = kz_regime.reshape(HOURS, lat_rows * lon_cells)
    cell_ids = fp_cell.reshape(-1)
    owners = fp_owner.reshape(-1)
    stations = fp_station.reshape(-1)
    weights = fp_weight.reshape(-1)
    entries = cell_ids.shape[0]
    adjoint_field = adjoint
    outputs = []
    for hour_step in range(HOURS):
        chosen = lax.dynamic_slice_in_dim(regime_rows[hour_step], first_column, column_count, 0)

        def column_solve(columns, chosen=chosen):
            result = jnp.zeros_like(columns)
            for regime in range(REGIMES):
                product = jnp.einsum(
                    "ji,tjp->tip", kz_inverse[regime], columns, precision=lax.Precision.HIGHEST
                )
                result = jnp.where(chosen[None, None, :] == regime, product, result)
            returned = lax.all_to_all(result, "lev", split_axis=1, concat_axis=2, tiled=True)
            return (returned, result)

        flat_field = adjoint_field.reshape(tracers, levels_dev, lat_rows * lon_cells)
        returned, solved = column_solve(
            lax.all_to_all(flat_field, "lev", split_axis=2, concat_axis=1, tiled=True)
        )
        lowest = solved[:, :FOOT_LEVELS, :].reshape(tracers, -1)
        picked = jnp.take(lowest, cell_ids, axis=1) * weights[None, :]
        capacity = 2 * entries // groups
        owner_hits = (owners[:, None] == jnp.arange(groups, dtype=jnp.int32)[None, :]).astype(
            jnp.int32
        )
        bucket_rank = jnp.sum(jnp.cumsum(owner_hits, axis=0) * owner_hits, axis=1) - 1
        slot_pos = owners * capacity + bucket_rank
        send_values = (
            jnp.zeros((tracers, groups * capacity), jnp.float32).at[:, slot_pos].set(picked)
        )
        send_ids = jnp.full((groups * capacity,), -1, jnp.int32).at[slot_pos].set(stations)
        arrived_values, arrived_ids = (
            lax.all_to_all(
                send_values.reshape(tracers, groups, capacity),
                ("lat", "lev"),
                split_axis=1,
                concat_axis=1,
                tiled=True,
            ),
            lax.all_to_all(
                send_ids.reshape(1, groups, capacity),
                ("lat", "lev"),
                split_axis=1,
                concat_axis=1,
                tiled=True,
            ),
        )
        matches = (
            arrived_ids[0][:, :, None] == jnp.arange(SPO, dtype=jnp.int32)[None, None, :]
        ).astype(jnp.float32)
        station_sums = jnp.einsum(
            "tgc,gcs->ts", arrived_values, matches, precision=lax.Precision.HIGHEST
        )
        outputs.append(station_sums)
        adjoint_field = returned.reshape(tracers, levels_dev, lat_rows, lon_cells)
        for substep in range(NSUB):
            adjoint_field = lat_sweep(lat_rim(adjoint_field, 1), north_face, south_face)
            adjoint_field = lon_sweep(lon_rim(adjoint_field, 1), wind_east, west_face)
    return (adjoint_field, jnp.stack(outputs)[:, :, None, :])


def fits(mesh_sizes, shape, kz_shape, entries):
    n_lat, n_lev, n_lon = mesh_sizes
    tracers, levels, rows, cells = shape
    return (
        tracers == 4
        and rows == 4
        and cells == 256
        and n_lat == 4
        and n_lat * n_lev == 16
        and levels * n_lev == kz_shape[1]
        and kz_shape[1] % 8 == 0
        and entries == 512
    )


def device_part(sizes, *arrays):
    if fits(sizes, arrays[0].shape, arrays[3].shape, arrays[5].shape[-1]):
        return regrouped(sizes, *arrays)
    return shards(*arrays)


def solution(mesh):
    sizes = tuple(mesh.shape[name] for name in RING)
    in_specs = (
        P(None, "lev", "lat", "lon"),
        P("lev", "lat", "lon"),
        P("lev", "lat", "lon"),
        P(),
        P(None, "lat", "lon"),
        P(AXES, "lon", None),
        P(AXES, "lon", None, None),
        P(AXES, "lon", None),
        P(AXES, "lon", None),
    )
    out_specs = (P(None, "lev", "lat", "lon"), P(None, None, "lon", AXES))
    return jax.shard_map(
        functools.partial(device_part, sizes),
        mesh=mesh,
        in_specs=in_specs,
        out_specs=out_specs,
        check_vma=False,
    )
```

```python
import functools
import jax
import jax.numpy as jnp
from jax import lax
from jax.experimental import pallas as pl
from jax.experimental.pallas import tpu as pltpu
from jax.sharding import PartitionSpec as P

NSUB = 4
HOURS = 2
REGIMES = 4
FOOT_LEVELS = 8
SPO = 4
LANES = 128
GRAIN = 16
ENTRY_ROWS = 12
F32 = jnp.float32
BF16 = jnp.bfloat16
AXES = ("lat", "lev")
RING = ("lat", "lev", "lon")


def chunk_owner(n_lat, n_lev):
    place = [0] * (n_lat * n_lev)
    for a in range(n_lat):
        for z in range(n_lev):
            chip, core = divmod(a, 2)
            step = z if chip % 2 == 0 else n_lev - 1 - z
            place[(chip * n_lev + step) * 2 + core] = a * n_lev + z
    return place


def ring_perm(n_lat, n_lev, n_lon, shift):
    place = chunk_owner(n_lat, n_lev)
    ring = [
        (place[::-1] if o % 2 else place)[d] * n_lon + o
        for o in range(n_lon)
        for d in range(len(place))
    ]
    count = len(ring)
    return [(ring[i], ring[(i + shift) % count]) for i in range(count)]


def owners(place):
    odd = lax.axis_index("lon") % 2 == 1
    return [jnp.where(odd, there, here) for here, there in zip(place, place[::-1])]


def lane_ids(rows):
    return lax.broadcasted_iota(jnp.int32, (rows, LANES), 1)


def swap_grains(blocks):
    blocks = list(blocks)
    grain = lane_ids(blocks[0].shape[0]) // GRAIN
    bit = len(blocks) // 2
    while bit:
        low = (grain & bit) == 0
        for i in range(len(blocks)):
            if i & bit == 0:
                a, b = blocks[i], blocks[i | bit]
                blocks[i] = jnp.where(low, a, pltpu.roll(b, bit * GRAIN, 1))
                blocks[i | bit] = jnp.where(low, pltpu.roll(a, LANES - bit * GRAIN, 1), b)
        bit //= 2
    return blocks


def swap_halves(a, b):
    low = lane_ids(a.shape[0]) < LANES // 2
    return (
        jnp.where(low, a, pltpu.roll(b, LANES // 2, 1)),
        jnp.where(low, pltpu.roll(a, LANES // 2, 1), b),
    )


def transpose_matrix():
    i = lax.broadcasted_iota(jnp.int32, (256, 256), 0)
    j = lax.broadcasted_iota(jnp.int32, (256, 256), 1)
    return ((i // 16 == j % 16) & (i % 16 == j // 16)).astype(F32).astype(BF16)


def split_two(x):
    high = x.astype(BF16)
    return high, (x - high.astype(F32)).astype(BF16)


def split_three(x):
    high, _ = split_two(x)
    rest = x - high.astype(F32)
    middle = rest.astype(BF16)
    return high, middle, (rest - middle.astype(F32)).astype(BF16)


def mm(a, b):
    return jnp.dot(a, b, preferred_element_type=F32)


def move_lanes(x, matrix):
    high, middle, low = split_three(x)
    return (mm(high, matrix) + mm(middle, matrix)) + mm(low, matrix)


def pack_kernel(place, *refs):
    count = (len(refs) - 4) // 2
    given, outs = refs[:count], refs[count : count + 3]
    held, sems = refs[count + 3 : -1], refs[-1]
    place = owners(place)
    copies = [
        pltpu.make_async_copy(a, b, sems.at[i]) for i, (a, b) in enumerate(zip(given, held))
    ]
    for copy in copies:
        copy.start()
    adj, east, north, regime, cell, owner, station, weight = held
    fields, winds, entries = outs
    levels = adj.shape[1]
    rows = adj.shape[2]

    def place_pieces(srcs, out, first, count):
        for half in range(2):
            lanes = slice(half * LANES, (half + 1) * LANES)
            for j, piece in enumerate(swap_grains([s[:, lanes] for s in srcs])):
                out[place[half * 8 + j], first : first + count, :] = piece

    copies[0].wait()
    for pair in range(2):
        srcs = [adj[2 * pair + k, :, r, :] for k in range(2) for r in range(rows)]
        place_pieces(srcs, fields, pair * levels, levels)
    for copy in copies[1:]:
        copy.wait()
    srcs = [w[:, r, :] for w in (east, north) for r in range(rows)]
    place_pieces(srcs, winds, 0, levels)
    srcs = [regime[h, r : r + 1, :].astype(F32) for h in range(HOURS) for r in range(rows)]
    place_pieces(srcs, fields, 2 * levels, 1)
    cells = cell[0].astype(F32)
    stations = (owner[...] * SPO + station[0]).astype(F32)
    for k in range(4):
        part = slice(k * LANES, (k + 1) * LANES)
        entries[k : k + 1, :] = cells[:, part]
        entries[4 + k : 5 + k, :] = stations[:, part]
        entries[8 + k : 9 + k, :] = weight[0][:, part]


def solve_columns(high, low, kz_high, kz_low, regime, levels):
    product = mm(kz_high, high) + (mm(kz_low, high) + mm(kz_high, low))
    result = product[:levels]
    for k in range(1, REGIMES):
        result = jnp.where(regime == float(k), product[k * levels : (k + 1) * levels], result)
    return result


def mixing(kz):
    stacked = jnp.concatenate([kz[k].T for k in range(REGIMES)], axis=0)
    return split_two(stacked)


def rim_messages(top, bottom, first, last, rows):
    half = LANES // 2
    low = lane_ids(top.shape[0]) < half
    first[rows, :] = jnp.where(low, top[:, :LANES], pltpu.roll(bottom[:, :LANES], half, 1))
    last[rows, :] = jnp.where(low, pltpu.roll(top[:, LANES:], half, 1), bottom[:, LANES:])


def unpack_solve_kernel(n_lev, recv, kz, solved, regimes, first, last, field):
    total = kz.shape[1]
    levels = total // n_lev
    for pair in range(2):
        for z in range(n_lev):
            for half in range(2):
                lanes = slice(half * LANES, (half + 1) * LANES)
                a, b = [
                    recv[(2 * half + k) * n_lev + z, pair * levels : (pair + 1) * levels, :]
                    for k in range(2)
                ]
                for k, value in enumerate(swap_halves(a, b)):
                    base = (2 * pair + k) * total + z * levels
                    field[base : base + levels, lanes] = value
    base = 4 * total
    field[base : base + 8, :] = jnp.zeros((8, 256), F32)
    for half in range(2):
        lanes = slice(half * LANES, (half + 1) * LANES)
        a, b = [
            recv[(2 * half + k) * n_lev, 2 * levels : 2 * levels + 1, :] for k in range(2)
        ]
        for k, value in enumerate(swap_halves(a, b)):
            field[base + k : base + k + 1, lanes] = value
    matrix = transpose_matrix()
    regime = mm(field[base : base + 8, :].astype(BF16), matrix)
    regimes[...] = regime
    kz_high, kz_low = mixing(kz)
    for t in range(4):
        high, low = split_two(field[t * total : (t + 1) * total, :])
        high = mm(high, matrix).astype(BF16)
        low = mm(low, matrix).astype(BF16)
        solved[t * total : (t + 1) * total, :] = solve_columns(
            high, low, kz_high, kz_low, regime[0:1], total
        )
    rim_messages(
        solved[0 : 2 * total, :], solved[2 * total :, :], first, last, slice(0, 2 * total)
    )


def unpack_winds_kernel(n_lev, others, winds, first, last, field):
    total = winds.shape[0] // 2
    levels = total // n_lev
    own_lat, own_lev = lax.axis_index("lat"), lax.axis_index("lev")
    for z in range(n_lev):
        for half in range(2):
            lanes = slice(half * LANES, (half + 1) * LANES)
            a, b = [
                others[z ^ own_lev, (2 * half + k) ^ own_lat, 0:levels, :] for k in range(2)
            ]
            for k, value in enumerate(swap_halves(a, b)):
                base = k * total + z * levels
                field[base : base + levels, lanes] = value
    winds[...] = move_lanes(field[...], transpose_matrix())
    rim_messages(winds[0:total, :], winds[total:, :], first, last, slice(0, total))


def rim_lanes(from_east, from_west, rows, upper):
    half = LANES // 2
    east, west = from_east[rows, :], from_west[rows, :]
    low = lane_ids(east.shape[0]) < half
    if upper:
        return jnp.where(low, pltpu.roll(east, half, 1), west)
    return jnp.where(low, east, pltpu.roll(west, half, 1))


def columns(ref, rows):
    return [ref[rows, i * LANES : (i + 1) * LANES] for i in range(3)]


def pair_columns(ref, rows):
    return [ref[rows, i * LANES : (i + 1) * LANES] for i in range(2)]


def turned(x, shift):
    return pltpu.roll(x, shift % LANES, 1)


def stepped(blocks, shift):
    count = len(blocks)
    lane = lane_ids(blocks[0].shape[0])
    moved = [turned(x, shift) for x in blocks]
    if shift > 0:
        return [jnp.where(lane < shift, moved[i - 1], moved[i]) for i in range(count)]
    return [
        jnp.where(lane >= LANES + shift, moved[(i + 1) % count], moved[i]) for i in range(count)
    ]


def face_weights(lat_count, winds, from_east, from_west, total, faces):
    rims = slice(0, total)
    east = pair_columns(winds, slice(0, total)) + [rim_lanes(from_east, from_west, rims, False)]
    north = pair_columns(winds, slice(total, 2 * total)) + [
        rim_lanes(from_east, from_west, rims, True)
    ]
    lat = lane_ids(total) % lat_count
    north = [jnp.where(lat == lat_count - 1, 0.0, x) for x in north]
    west = stepped(east, lat_count)
    for i in range(3):
        lanes = slice(i * LANES, (i + 1) * LANES)
        after = jnp.maximum(north[i], 0.0)
        before = -jnp.minimum(jnp.where(lat == 0, 0.0, turned(north[i], 1)), 0.0)
        faces[0, :, lanes] = 1.0 - after - before
        faces[1, :, lanes] = after
        faces[2, :, lanes] = before
        after = jnp.maximum(east[i], 0.0)
        before = -jnp.minimum(west[i], 0.0)
        faces[3, :, lanes] = 1.0 - after - before
        faces[4, :, lanes] = after
        faces[5, :, lanes] = before


def transport(lat_count, field, east_rows, west_rows, faces, total, buffers, result):
    for t in range(4):
        own = slice(t * total, (t + 1) * total)
        rim = slice((t % 2) * total, (t % 2 + 1) * total)
        buffers[0, own, 0:256] = field[own, :]
        buffers[0, own, 256:384] = rim_lanes(east_rows, west_rows, rim, t >= 2)
    for step in range(2 * NSUB):
        last = step == 2 * NSUB - 1
        for t in range(4):
            own = slice(t * total, (t + 1) * total)
            f = columns(buffers.at[step % 2], own)
            if step % 2 == 0:
                after = [turned(x, -1) for x in f]
                before = [turned(x, 1) for x in f]
            else:
                after = stepped(f, -lat_count)
                before = stepped(f, lat_count)
            base = 3 * (step % 2)
            for i in range(2 if last else 3):
                lanes = slice(i * LANES, (i + 1) * LANES)
                value = (
                    faces[base, :, lanes] * f[i]
                    + faces[base + 1, :, lanes] * after[i]
                    + faces[base + 2, :, lanes] * before[i]
                )
                if last:
                    result[own, lanes] = value
                else:
                    buffers[(step + 1) % 2, own, lanes] = value


def transport_solve_kernel(
    lat_count, field, winds, regimes, kz, wind_east, wind_west, from_east, from_west, solved, first, last, faces, buffers, moved
):
    total = kz.shape[1]
    face_weights(lat_count, winds, wind_east, wind_west, total, faces)
    transport(lat_count, field, from_east, from_west, faces, total, buffers, moved)
    kz_high, kz_low = mixing(kz)
    for t in range(4):
        high, low = split_two(moved[t * total : (t + 1) * total, :])
        solved[t * total : (t + 1) * total, :] = solve_columns(
            high, low, kz_high, kz_low, regimes[1:2, :], total
        )
    rim_messages(
        solved[0 : 2 * total, :], solved[2 * total :, :], first, last, slice(0, 2 * total)
    )


def footprint_kernel(n_lev, entry_row, others, hour_0, hour_1, sums):
    own_lat, own_lev = lax.axis_index("lat"), lax.axis_index("lev")
    chip, core = own_lat // 2, own_lat % 2
    step = jnp.where(chip % 2 == 0, own_lev, n_lev - 1 - own_lev)
    chunk = (chip * n_lev + step) * 2 + core
    odd = lax.axis_index("lon") % 2 == 1
    first_lon = jnp.where(odd, others.shape[0] * others.shape[1] - 1 - chunk, chunk) * GRAIN
    total = hour_0.shape[0] // 4
    matrix = transpose_matrix()
    low = jnp.concatenate(
        [h[t * total : t * total + FOOT_LEVELS, :] for h in (hour_0, hour_1) for t in range(4)],
        axis=0,
    )
    parts = mm(jnp.concatenate(split_three(low), axis=0), matrix).astype(BF16)
    count = low.shape[0]
    acc = jnp.zeros((count, 64), F32)
    cell_ids = lax.broadcasted_iota(jnp.int32, (GRAIN, 512), 0)
    level_ids = lax.broadcasted_iota(jnp.int32, (FOOT_LEVELS, 512), 0)
    station_ids = lax.broadcasted_iota(jnp.int32, (64, 512), 0)
    for row in range(others.shape[0] * others.shape[1]):
        z, a = (row % n_lev) ^ own_lev, (row // n_lev) ^ own_lat

        def entries(at):
            return jnp.concatenate(
                [others[z, a, at + k : at + k + 1, :] for k in range(4)], axis=1
            )

        code = entries(entry_row).astype(jnp.int32)
        station = entries(entry_row + 4).astype(jnp.int32)
        weight = entries(entry_row + 8)
        cells = ((code & 255) - first_lon == cell_ids).astype(F32).astype(BF16)
        picked = mm(parts[:, row * GRAIN : (row + 1) * GRAIN], cells)
        picked = (picked[:count] + picked[count : 2 * count]) + picked[2 * count :]
        level = jnp.where((code >> 8) == level_ids, weight, 0.0)
        picked = picked * jnp.concatenate([level] * (count // FOOT_LEVELS), axis=0)
        named = (station == station_ids).astype(F32).astype(BF16)
        high, rest = split_two(picked)
        both = jnp.concatenate([high, rest], axis=0)
        both = lax.dot_general(both, named, (((1,), (1,)), ((), ())), preferred_element_type=F32)
        acc = acc + (both[:count] + both[count:])
    sums[...] = jnp.sum(acc.reshape(count // FOOT_LEVELS, FOOT_LEVELS, 64), axis=1)


def transport_pack_kernel(
    lat_count, n_lev, field, winds, from_east_0, from_west_0, from_east, from_west, sums, out,
    faces, buffers, moved,
):
    total = winds.shape[0] // 2
    levels = total // n_lev
    face_weights(lat_count, winds, from_east_0, from_west_0, total, faces)
    transport(lat_count, field, from_east, from_west, faces, total, buffers, moved)
    matrix = transpose_matrix()
    for pair in range(2):
        for k in range(2):
            rows = slice((2 * pair + k) * total, (2 * pair + k + 1) * total)
            moved[rows, :] = move_lanes(moved[rows, :], matrix)
        for z in range(n_lev):
            for half in range(2):
                lanes = slice(half * LANES, (half + 1) * LANES)
                a, b = [
                    moved[
                        (2 * pair + k) * total + z * levels : (2 * pair + k) * total
                        + (z + 1) * levels,
                        lanes,
                    ]
                    for k in range(2)
                ]
                for k, value in enumerate(swap_halves(a, b)):
                    out[
                        (2 * half + k) * n_lev + z, pair * levels : (pair + 1) * levels, :
                    ] = value
    wide = jnp.concatenate([sums[...], jnp.zeros((8, 64), F32)], axis=1)
    line = lax.broadcasted_iota(jnp.int32, (8, LANES), 0)
    spread = jnp.zeros((8, LANES), F32)
    for k in range(8):
        spread = jnp.where(line == k, pltpu.roll(wide, 4 * k, 1) if k else wide, spread)
    keep = lax.broadcasted_iota(jnp.int32, (8, LANES), 1) // 4 == line
    for g in range(out.shape[0]):
        value = pltpu.roll(spread, LANES - 4 * g, 1) if g else spread
        value = jnp.sum(jnp.where(keep, value, 0.0), axis=0, keepdims=True)
        out[g, 2 * levels : 2 * levels + 1, :] = value


def unpack_kernel(place, recv, final, stations):
    place = owners(place)
    levels = final.shape[1]
    for pair in range(2):
        for half in range(2):
            lanes = slice(half * LANES, (half + 1) * LANES)
            blocks = [
                recv[place[half * 8 + j], pair * levels : (pair + 1) * levels, :]
                for j in range(8)
            ]
            for i, value in enumerate(swap_grains(blocks)):
                k, r = divmod(i, 4)
                final[2 * pair + k, :, r, lanes] = value
    line = recv[0, 2 * levels : 2 * levels + 1, :]
    for g in range(1, recv.shape[0]):
        line = line + recv[g, 2 * levels : 2 * levels + 1, :]
    for h in range(HOURS):
        for t in range(4):
            at = (h * 4 + t) * 4
            stations[h, t, :, :] = line[:, at : at + 4]


def gather_others(sizes, winds, entries):
    n_lat, n_lev, _ = sizes
    own_lat, own_lev = lax.axis_index("lat"), lax.axis_index("lev")
    levels = winds.shape[1]
    pieces = winds.reshape(n_lat, n_lev * levels, LANES)

    def swap(x, axis, count, k):
        return lax.ppermute(x, axis, [(i, i ^ k) for i in range(count)])

    def for_lat(k):
        piece = lax.dynamic_index_in_dim(pieces, own_lat ^ k, 0, keepdims=False)
        return jnp.concatenate([piece, entries], axis=0)

    here = jnp.stack([for_lat(0)] + [swap(for_lat(k), "lat", n_lat, k) for k in range(1, n_lat)])
    pieces = here[:, : n_lev * levels].reshape(n_lat, n_lev, levels, LANES)
    entries = here[:, n_lev * levels :].reshape(-1, LANES)

    def for_lev(k):
        piece = lax.dynamic_index_in_dim(pieces, own_lev ^ k, 1, keepdims=False)
        return jnp.concatenate([piece.reshape(-1, LANES), entries], axis=0)

    both = jnp.stack([for_lev(0)] + [swap(for_lev(k), "lev", n_lev, k) for k in range(1, n_lev)])
    split = n_lat * levels
    return (
        both[:, :split].reshape(n_lev, n_lat, levels, LANES),
        both[:, split:].reshape(n_lev, n_lat, -1, LANES),
    )


def call(kernel, outs, scratch=()):
    return pl.pallas_call(
        kernel,
        out_shape=[jax.ShapeDtypeStruct(s, F32) for s in outs],
        scratch_shapes=[pltpu.VMEM(s, F32) for s in scratch],
        compiler_params=pltpu.CompilerParams(vmem_limit_bytes=48 * 1024 * 1024),
    )


def regrouped(sizes, adjoint, wind_east, wind_north, kz_inverse, kz_regime, fp_cell, fp_owner, fp_station, fp_weight):
    n_lat, n_lev, n_lon = sizes
    levels = adjoint.shape[1]
    total = levels * n_lev
    group = n_lat * n_lev
    lat_count = n_lat * adjoint.shape[2]
    place = chunk_owner(n_lat, n_lev)
    to_west = ring_perm(n_lat, n_lev, n_lon, -1)
    to_east = ring_perm(n_lat, n_lev, n_lon, 1)

    def exchange(x):
        return lax.all_to_all(x, AXES, split_axis=0, concat_axis=0, tiled=True)

    def rims(first, last):
        return lax.ppermute(first, RING, to_west), lax.ppermute(last, RING, to_east)

    out_rows = 2 * levels + 1
    out_rows += -out_rows % 8
    wind_rows = levels + -levels % 8
    given = (
        adjoint, wind_east, wind_north, kz_regime, fp_cell, fp_owner.reshape(1, -1), fp_station, fp_weight
    )
    fields, winds, entries = pl.pallas_call(
        functools.partial(pack_kernel, place),
        in_specs=[pl.BlockSpec(memory_space=pltpu.HBM)] * len(given),
        out_shape=[
            jax.ShapeDtypeStruct(shape, F32)
            for shape in (
                (group, out_rows, LANES), (group, wind_rows, LANES), (ENTRY_ROWS, LANES)
            )
        ],
        scratch_shapes=[pltpu.VMEM(x.shape, x.dtype) for x in given]
        + [pltpu.SemaphoreType.DMA((len(given),))],
    )(*given)
    recv = exchange(fields)
    winds, entries = gather_others(sizes, winds[:, :levels], entries)
    solved_0, regimes, first, last = call(
        functools.partial(unpack_solve_kernel, n_lev),
        [(4 * total, 256), (8, 256), (2 * total, LANES), (2 * total, LANES)],
        [(4 * total + 8, 256)],
    )(recv, kz_inverse)
    east_0, west_0 = rims(first, last)
    winds, first, last = call(
        functools.partial(unpack_winds_kernel, n_lev),
        [(2 * total, 256), (total, LANES), (total, LANES)],
        [(2 * total, 256)],
    )(winds)
    wind_rims = rims(first, last)
    solved_1, first, last = call(
        functools.partial(transport_solve_kernel, lat_count),
        [(4 * total, 256), (2 * total, LANES), (2 * total, LANES)],
        [(6, total, 384), (2, 4 * total, 384), (4 * total, 256)],
    )(solved_0, winds, regimes, kz_inverse, *wind_rims, east_0, west_0)
    east_1, west_1 = rims(first, last)
    (sums,) = call(functools.partial(footprint_kernel, n_lev, 0), [(8, 64)])(
        entries, solved_0, solved_1
    )
    (back,) = call(
        functools.partial(transport_pack_kernel, lat_count, n_lev),
        [(group, out_rows, LANES)],
        [(6, total, 384), (2, 4 * total, 384), (4 * total, 256)],
    )(solved_1, winds, *wind_rims, east_1, west_1, sums)
    final, stations = call(
        functools.partial(unpack_kernel, place), [adjoint.shape, (HOURS, 4, 1, SPO)]
    )(exchange(back))
    return final, stations


def padded_2(x, sides, width, wrap):
    for axis, dim in sides:
        peers, length = (lax.axis_size(axis), x.shape[dim])
        up = [(i, (i + 1) % peers) for i in range(peers if wrap else peers - 1)]
        down = [(j, i) for i, j in up]
        last = lax.slice_in_dim(x, length - width, length, axis=dim)
        initial = lax.slice_in_dim(x, 0, width, axis=dim)
        before = lax.ppermute(last, axis, up)
        after = lax.ppermute(initial, axis, down)
        x = jnp.concatenate([before, x, after], axis=dim)
    return x


def lat_rim(values, rim_width):
    return padded_2(values, (("lat", 2),), rim_width, False)


def lon_rim(values, rim_width):
    return padded_2(values, (("lon", 3),), rim_width, True)


def lat_sweep(padded, north_face, south_face):
    middle = padded[:, :, 1:-1]
    return (
        middle
        + jnp.maximum(north_face, 0.0) * (padded[:, :, 2:] - middle)
        - jnp.minimum(south_face, 0.0) * (padded[:, :, :-2] - middle)
    )


def lon_sweep(padded, east_face, west_face):
    middle = padded[:, :, :, 1:-1]
    return (
        middle
        + jnp.maximum(east_face, 0.0) * (padded[:, :, :, 2:] - middle)
        - jnp.minimum(west_face, 0.0) * (padded[:, :, :, :-2] - middle)
    )


def shards(
    adjoint, wind_east, wind_north, kz_inverse, kz_regime, fp_cell, fp_owner, fp_station, fp_weight
):
    tracers, levels_dev, lat_rows, lon_cells = adjoint.shape
    row_index = lax.axis_index("lat") * lat_rows + lax.broadcasted_iota(
        jnp.int32, (1, lat_rows, 1), 1
    )
    last_row = lat_rows * lax.axis_size("lat") - 1
    north_face = jnp.where(row_index == last_row, jnp.zeros_like(wind_north), wind_north)
    south_face = lat_rim(north_face[None], 1)[0][:, :-2]
    west_face = lon_rim(wind_east[None], 1)[0][:, :, :-2]
    groups = lax.axis_size("lat") * lax.axis_size("lev")
    column_count = lat_rows * lon_cells // lax.axis_size("lev")
    first_column = lax.axis_index("lev") * column_count
    regime_rows = kz_regime.reshape(HOURS, lat_rows * lon_cells)
    cell_ids = fp_cell.reshape(-1)
    owners = fp_owner.reshape(-1)
    stations = fp_station.reshape(-1)
    weights = fp_weight.reshape(-1)
    entries = cell_ids.shape[0]
    adjoint_field = adjoint
    outputs = []
    for hour_step in range(HOURS):
        chosen = lax.dynamic_slice_in_dim(regime_rows[hour_step], first_column, column_count, 0)

        def column_solve(columns, chosen=chosen):
            result = jnp.zeros_like(columns)
            for regime in range(REGIMES):
                product = jnp.einsum(
                    "ji,tjp->tip", kz_inverse[regime], columns, precision=lax.Precision.HIGHEST
                )
                result = jnp.where(chosen[None, None, :] == regime, product, result)
            returned = lax.all_to_all(result, "lev", split_axis=1, concat_axis=2, tiled=True)
            return (returned, result)

        flat_field = adjoint_field.reshape(tracers, levels_dev, lat_rows * lon_cells)
        returned, solved = column_solve(
            lax.all_to_all(flat_field, "lev", split_axis=2, concat_axis=1, tiled=True)
        )
        lowest = solved[:, :FOOT_LEVELS, :].reshape(tracers, -1)
        picked = jnp.take(lowest, cell_ids, axis=1) * weights[None, :]
        capacity = 2 * entries // groups
        owner_hits = (owners[:, None] == jnp.arange(groups, dtype=jnp.int32)[None, :]).astype(
            jnp.int32
        )
        bucket_rank = jnp.sum(jnp.cumsum(owner_hits, axis=0) * owner_hits, axis=1) - 1
        slot_pos = owners * capacity + bucket_rank
        send_values = (
            jnp.zeros((tracers, groups * capacity), jnp.float32).at[:, slot_pos].set(picked)
        )
        send_ids = jnp.full((groups * capacity,), -1, jnp.int32).at[slot_pos].set(stations)
        arrived_values, arrived_ids = (
            lax.all_to_all(
                send_values.reshape(tracers, groups, capacity),
                ("lat", "lev"),
                split_axis=1,
                concat_axis=1,
                tiled=True,
            ),
            lax.all_to_all(
                send_ids.reshape(1, groups, capacity),
                ("lat", "lev"),
                split_axis=1,
                concat_axis=1,
                tiled=True,
            ),
        )
        matches = (
            arrived_ids[0][:, :, None] == jnp.arange(SPO, dtype=jnp.int32)[None, None, :]
        ).astype(jnp.float32)
        station_sums = jnp.einsum(
            "tgc,gcs->ts", arrived_values, matches, precision=lax.Precision.HIGHEST
        )
        outputs.append(station_sums)
        adjoint_field = returned.reshape(tracers, levels_dev, lat_rows, lon_cells)
        for substep in range(NSUB):
            adjoint_field = lat_sweep(lat_rim(adjoint_field, 1), north_face, south_face)
            adjoint_field = lon_sweep(lon_rim(adjoint_field, 1), wind_east, west_face)
    return (adjoint_field, jnp.stack(outputs)[:, :, None, :])


def fits(mesh_sizes, shape, kz_shape, entries):
    n_lat, n_lev, n_lon = mesh_sizes
    tracers, levels, rows, cells = shape
    return (
        tracers == 4
        and rows == 4
        and cells == 256
        and n_lat == 4
        and n_lat * n_lev == 16
        and levels * n_lev == kz_shape[1]
        and kz_shape[1] % 8 == 0
        and entries == 512
    )


def device_part(sizes, *arrays):
    if fits(sizes, arrays[0].shape, arrays[3].shape, arrays[5].shape[-1]):
        return regrouped(sizes, *arrays)
    return shards(*arrays)


def solution(mesh):
    sizes = tuple(mesh.shape[name] for name in RING)
    in_specs = (
        P(None, "lev", "lat", "lon"),
        P("lev", "lat", "lon"),
        P("lev", "lat", "lon"),
        P(),
        P(None, "lat", "lon"),
        P(AXES, "lon", None),
        P(AXES, "lon", None, None),
        P(AXES, "lon", None),
        P(AXES, "lon", None),
    )
    out_specs = (P(None, "lev", "lat", "lon"), P(None, None, "lon", AXES))
    return jax.shard_map(
        functools.partial(device_part, sizes),
        mesh=mesh,
        in_specs=in_specs,
        out_specs=out_specs,
        check_vma=False,
    )
```

```python
import functools
import jax
import jax.numpy as jnp
from jax import lax
from jax.experimental import pallas as pl
from jax.experimental.pallas import tpu as pltpu
from jax.sharding import PartitionSpec as P

NSUB = 4
HOURS = 2
REGIMES = 4
FOOT_LEVELS = 8
SPO = 4
LANES = 128
GRAIN = 16
F32 = jnp.float32
BF16 = jnp.bfloat16
AXES = ("lat", "lev")
RING = ("lat", "lev", "lon")


def chunk_owner(n_lat, n_lev):
    place = [0] * (n_lat * n_lev)
    for a in range(n_lat):
        for z in range(n_lev):
            chip, core = divmod(a, 2)
            step = z if chip % 2 == 0 else n_lev - 1 - z
            place[(chip * n_lev + step) * 2 + core] = a * n_lev + z
    return place


def ring_perm(n_lat, n_lev, n_lon, shift):
    place = chunk_owner(n_lat, n_lev)
    ring = [
        (place[::-1] if o % 2 else place)[d] * n_lon + o
        for o in range(n_lon)
        for d in range(len(place))
    ]
    count = len(ring)
    return [(ring[i], ring[(i + shift) % count]) for i in range(count)]


def owners(place):
    odd = lax.axis_index("lon") % 2 == 1
    return [jnp.where(odd, there, here) for here, there in zip(place, place[::-1])]


def lane_ids(rows):
    return lax.broadcasted_iota(jnp.int32, (rows, LANES), 1)


def swap_grains(blocks):
    blocks = list(blocks)
    grain = lane_ids(blocks[0].shape[0]) // GRAIN
    bit = len(blocks) // 2
    while bit:
        low = (grain & bit) == 0
        for i in range(len(blocks)):
            if i & bit == 0:
                a, b = blocks[i], blocks[i | bit]
                blocks[i] = jnp.where(low, a, pltpu.roll(b, bit * GRAIN, 1))
                blocks[i | bit] = jnp.where(low, pltpu.roll(a, LANES - bit * GRAIN, 1), b)
        bit //= 2
    return blocks


def swap_halves(a, b):
    low = lane_ids(a.shape[0]) < LANES // 2
    return (
        jnp.where(low, a, pltpu.roll(b, LANES // 2, 1)),
        jnp.where(low, pltpu.roll(a, LANES // 2, 1), b),
    )


def transpose_matrix():
    i = lax.broadcasted_iota(jnp.int32, (256, 256), 0)
    j = lax.broadcasted_iota(jnp.int32, (256, 256), 1)
    return ((i // 16 == j % 16) & (i % 16 == j // 16)).astype(F32).astype(BF16)


def split_two(x):
    high = x.astype(BF16)
    return high, (x - high.astype(F32)).astype(BF16)


def split_three(x):
    high, _ = split_two(x)
    rest = x - high.astype(F32)
    middle = rest.astype(BF16)
    return high, middle, (rest - middle.astype(F32)).astype(BF16)


def mm(a, b):
    return jnp.dot(a, b, preferred_element_type=F32)


def move_lanes(x, matrix):
    high, middle, low = split_three(x)
    return (mm(high, matrix) + mm(middle, matrix)) + mm(low, matrix)


def pack_kernel(place, *refs):
    count = (len(refs) - 3) // 2
    given, outs = refs[:count], refs[count : count + 2]
    held, sems = refs[count + 2 : -1], refs[-1]
    place = owners(place)
    copies = [
        pltpu.make_async_copy(a, b, sems.at[i]) for i, (a, b) in enumerate(zip(given, held))
    ]
    for copy in copies:
        copy.start()
    adj, east, north, regime, cell, owner, station, weight = held
    fields, winds = outs
    levels = adj.shape[1]
    rows = adj.shape[2]

    def place_pieces(srcs, out, first, count):
        for half in range(2):
            lanes = slice(half * LANES, (half + 1) * LANES)
            for j, piece in enumerate(swap_grains([s[:, lanes] for s in srcs])):
                out[place[half * 8 + j], first : first + count, :] = piece

    copies[0].wait()
    for pair in range(2):
        srcs = [adj[2 * pair + k, :, r, :] for k in range(2) for r in range(rows)]
        place_pieces(srcs, fields, pair * levels, levels)
    for copy in copies[1:]:
        copy.wait()
    srcs = [w[:, r, :] for w in (east, north) for r in range(rows)]
    place_pieces(srcs, winds, 0, levels)
    srcs = [regime[h, r : r + 1, :].astype(F32) for h in range(HOURS) for r in range(rows)]
    place_pieces(srcs, fields, 2 * levels, 1)
    cells = cell[0].astype(F32)
    stations = (owner[...] * SPO + station[0]).astype(F32)
    for g in range(fields.shape[0]):
        k = g // (fields.shape[0] // 4)
        for at, value in enumerate((cells, stations, weight[0])):
            row = 2 * levels + 1 + at
            fields[g, row : row + 1, :] = value[:, k * LANES : (k + 1) * LANES]


def solve_columns(high, low, kz_high, kz_low, regime, levels):
    product = mm(kz_high, high) + (mm(kz_low, high) + mm(kz_high, low))
    result = product[:levels]
    for k in range(1, REGIMES):
        result = jnp.where(regime == float(k), product[k * levels : (k + 1) * levels], result)
    return result


def mixing(kz):
    stacked = jnp.concatenate([kz[k].T for k in range(REGIMES)], axis=0)
    return split_two(stacked)


def rim_messages(top, bottom, first, last, rows):
    half = LANES // 2
    low = lane_ids(top.shape[0]) < half
    first[rows, :] = jnp.where(low, top[:, :LANES], pltpu.roll(bottom[:, :LANES], half, 1))
    last[rows, :] = jnp.where(low, pltpu.roll(top[:, LANES:], half, 1), bottom[:, LANES:])


def unpack_solve_kernel(n_lev, recv, kz, solved, regimes, first, last, field):
    total = kz.shape[1]
    levels = total // n_lev
    for pair in range(2):
        for z in range(n_lev):
            for half in range(2):
                lanes = slice(half * LANES, (half + 1) * LANES)
                a, b = [
                    recv[(2 * half + k) * n_lev + z, pair * levels : (pair + 1) * levels, :]
                    for k in range(2)
                ]
                for k, value in enumerate(swap_halves(a, b)):
                    base = (2 * pair + k) * total + z * levels
                    field[base : base + levels, lanes] = value
    base = 4 * total
    field[base : base + 8, :] = jnp.zeros((8, 256), F32)
    for half in range(2):
        lanes = slice(half * LANES, (half + 1) * LANES)
        a, b = [
            recv[(2 * half + k) * n_lev, 2 * levels : 2 * levels + 1, :] for k in range(2)
        ]
        for k, value in enumerate(swap_halves(a, b)):
            field[base + k : base + k + 1, lanes] = value
    matrix = transpose_matrix()
    regime = mm(field[base : base + 8, :].astype(BF16), matrix)
    regimes[...] = regime
    kz_high, kz_low = mixing(kz)
    for t in range(4):
        high, low = split_two(field[t * total : (t + 1) * total, :])
        high = mm(high, matrix).astype(BF16)
        low = mm(low, matrix).astype(BF16)
        solved[t * total : (t + 1) * total, :] = solve_columns(
            high, low, kz_high, kz_low, regime[0:1], total
        )
    rim_messages(
        solved[0 : 2 * total, :], solved[2 * total :, :], first, last, slice(0, 2 * total)
    )


def unpack_winds_kernel(n_lev, *refs):
    pieces, (winds, first, last, field, others) = refs[:n_lev], refs[n_lev + 1 :]
    total = winds.shape[0] // 2
    levels = total // n_lev
    for m in range(n_lev):
        for k in range(others.shape[1]):
            others[m, k] = pieces[m][k * levels : (k + 1) * levels, :]
    own_lat, own_lev = lax.axis_index("lat"), lax.axis_index("lev")
    for z in range(n_lev):
        for half in range(2):
            lanes = slice(half * LANES, (half + 1) * LANES)
            a, b = [
                others[z ^ own_lev, (2 * half + k) ^ own_lat, 0:levels, :] for k in range(2)
            ]
            for k, value in enumerate(swap_halves(a, b)):
                base = k * total + z * levels
                field[base : base + levels, lanes] = value
    winds[...] = move_lanes(field[...], transpose_matrix())
    rim_messages(winds[0:total, :], winds[total:, :], first, last, slice(0, total))


def rim_lanes(from_east, from_west, rows, upper):
    half = LANES // 2
    east, west = from_east[rows, :], from_west[rows, :]
    low = lane_ids(east.shape[0]) < half
    if upper:
        return jnp.where(low, pltpu.roll(east, half, 1), west)
    return jnp.where(low, east, pltpu.roll(west, half, 1))


def columns(ref, rows):
    return [ref[rows, i * LANES : (i + 1) * LANES] for i in range(3)]


def pair_columns(ref, rows):
    return [ref[rows, i * LANES : (i + 1) * LANES] for i in range(2)]


def turned(x, shift):
    return pltpu.roll(x, shift % LANES, 1)


def stepped(blocks, shift):
    count = len(blocks)
    lane = lane_ids(blocks[0].shape[0])
    moved = [turned(x, shift) for x in blocks]
    if shift > 0:
        return [jnp.where(lane < shift, moved[i - 1], moved[i]) for i in range(count)]
    return [
        jnp.where(lane >= LANES + shift, moved[(i + 1) % count], moved[i]) for i in range(count)
    ]


def face_weights(lat_count, winds, from_east, from_west, total, faces):
    rims = slice(0, total)
    east = pair_columns(winds, slice(0, total)) + [rim_lanes(from_east, from_west, rims, False)]
    north = pair_columns(winds, slice(total, 2 * total)) + [
        rim_lanes(from_east, from_west, rims, True)
    ]
    lat = lane_ids(total) % lat_count
    north = [jnp.where(lat == lat_count - 1, 0.0, x) for x in north]
    west = stepped(east, lat_count)
    for i in range(3):
        lanes = slice(i * LANES, (i + 1) * LANES)
        after = jnp.maximum(north[i], 0.0)
        before = -jnp.minimum(jnp.where(lat == 0, 0.0, turned(north[i], 1)), 0.0)
        faces[0, :, lanes] = 1.0 - after - before
        faces[1, :, lanes] = after
        faces[2, :, lanes] = before
        after = jnp.maximum(east[i], 0.0)
        before = -jnp.minimum(west[i], 0.0)
        faces[3, :, lanes] = 1.0 - after - before
        faces[4, :, lanes] = after
        faces[5, :, lanes] = before


def transport(lat_count, field, east_rows, west_rows, faces, total, buffers, result):
    for t in range(4):
        own = slice(t * total, (t + 1) * total)
        rim = slice((t % 2) * total, (t % 2 + 1) * total)
        buffers[0, own, 0:256] = field[own, :]
        buffers[0, own, 256:384] = rim_lanes(east_rows, west_rows, rim, t >= 2)
    for step in range(2 * NSUB):
        last = step == 2 * NSUB - 1
        for t in range(4):
            own = slice(t * total, (t + 1) * total)
            f = columns(buffers.at[step % 2], own)
            if step % 2 == 0:
                after = [turned(x, -1) for x in f]
                before = [turned(x, 1) for x in f]
            else:
                after = stepped(f, -lat_count)
                before = stepped(f, lat_count)
            base = 3 * (step % 2)
            for i in range(2 if last else 3):
                lanes = slice(i * LANES, (i + 1) * LANES)
                value = (
                    faces[base, :, lanes] * f[i]
                    + faces[base + 1, :, lanes] * after[i]
                    + faces[base + 2, :, lanes] * before[i]
                )
                if last:
                    result[own, lanes] = value
                else:
                    buffers[(step + 1) % 2, own, lanes] = value


def transport_solve_kernel(
    lat_count, field, winds, regimes, kz, wind_east, wind_west, from_east, from_west, solved, first, last, faces, buffers, moved
):
    total = kz.shape[1]
    face_weights(lat_count, winds, wind_east, wind_west, total, faces)
    transport(lat_count, field, from_east, from_west, faces, total, buffers, moved)
    kz_high, kz_low = mixing(kz)
    for t in range(4):
        high, low = split_two(moved[t * total : (t + 1) * total, :])
        solved[t * total : (t + 1) * total, :] = solve_columns(
            high, low, kz_high, kz_low, regimes[1:2, :], total
        )
    rim_messages(
        solved[0 : 2 * total, :], solved[2 * total :, :], first, last, slice(0, 2 * total)
    )


def footprint_kernel(n_lev, quarters, hour_0, hour_1, sums):
    own_lat, own_lev = lax.axis_index("lat"), lax.axis_index("lev")
    chip, core = own_lat // 2, own_lat % 2
    step = jnp.where(chip % 2 == 0, own_lev, n_lev - 1 - own_lev)
    chunk = (chip * n_lev + step) * 2 + core
    odd = lax.axis_index("lon") % 2 == 1
    group = quarters.shape[1] // 3
    first_lon = jnp.where(odd, group - 1 - chunk, chunk) * GRAIN
    total = hour_0.shape[0] // 4
    matrix = transpose_matrix()
    low = jnp.concatenate(
        [h[t * total : t * total + FOOT_LEVELS, :] for h in (hour_0, hour_1) for t in range(4)],
        axis=0,
    )
    parts = mm(jnp.concatenate(split_three(low), axis=0), matrix).astype(BF16)
    count = low.shape[0]
    acc = jnp.zeros((count, 64), F32)
    cell_ids = lax.broadcasted_iota(jnp.int32, (GRAIN, 512), 0)
    level_ids = lax.broadcasted_iota(jnp.int32, (FOOT_LEVELS, 512), 0)
    station_ids = lax.broadcasted_iota(jnp.int32, (64, 512), 0)
    for row in range(group):

        def entries(at):
            return jnp.concatenate(
                [quarters[k, 3 * row + at : 3 * row + at + 1, :] for k in range(4)], axis=1
            )

        code = entries(0).astype(jnp.int32)
        station = entries(1).astype(jnp.int32)
        weight = entries(2)
        cells = ((code & 255) - first_lon == cell_ids).astype(F32).astype(BF16)
        picked = mm(parts[:, row * GRAIN : (row + 1) * GRAIN], cells)
        picked = (picked[:count] + picked[count : 2 * count]) + picked[2 * count :]
        level = jnp.where((code >> 8) == level_ids, weight, 0.0)
        picked = picked * jnp.concatenate([level] * (count // FOOT_LEVELS), axis=0)
        named = (station == station_ids).astype(F32).astype(BF16)
        high, rest = split_two(picked)
        both = jnp.concatenate([high, rest], axis=0)
        both = lax.dot_general(both, named, (((1,), (1,)), ((), ())), preferred_element_type=F32)
        acc = acc + (both[:count] + both[count:])
    sums[...] = jnp.sum(acc.reshape(count // FOOT_LEVELS, FOOT_LEVELS, 64), axis=1)


def transport_pack_kernel(
    lat_count, n_lev, field, winds, from_east_0, from_west_0, from_east, from_west, sums, out,
    faces, buffers, moved,
):
    total = winds.shape[0] // 2
    levels = total // n_lev
    face_weights(lat_count, winds, from_east_0, from_west_0, total, faces)
    transport(lat_count, field, from_east, from_west, faces, total, buffers, moved)
    matrix = transpose_matrix()
    for pair in range(2):
        for k in range(2):
            rows = slice((2 * pair + k) * total, (2 * pair + k + 1) * total)
            moved[rows, :] = move_lanes(moved[rows, :], matrix)
        for z in range(n_lev):
            for half in range(2):
                lanes = slice(half * LANES, (half + 1) * LANES)
                a, b = [
                    moved[
                        (2 * pair + k) * total + z * levels : (2 * pair + k) * total
                        + (z + 1) * levels,
                        lanes,
                    ]
                    for k in range(2)
                ]
                for k, value in enumerate(swap_halves(a, b)):
                    out[
                        (2 * half + k) * n_lev + z, pair * levels : (pair + 1) * levels, :
                    ] = value
    wide = jnp.concatenate([sums[...], jnp.zeros((8, 64), F32)], axis=1)
    line = lax.broadcasted_iota(jnp.int32, (8, LANES), 0)
    spread = jnp.zeros((8, LANES), F32)
    for k in range(8):
        spread = jnp.where(line == k, pltpu.roll(wide, 4 * k, 1) if k else wide, spread)
    keep = lax.broadcasted_iota(jnp.int32, (8, LANES), 1) // 4 == line
    for g in range(out.shape[0]):
        value = pltpu.roll(spread, LANES - 4 * g, 1) if g else spread
        value = jnp.sum(jnp.where(keep, value, 0.0), axis=0, keepdims=True)
        out[g, 2 * levels : 2 * levels + 1, :] = value


def unpack_kernel(place, recv, final, stations):
    place = owners(place)
    levels = final.shape[1]
    for pair in range(2):
        for half in range(2):
            lanes = slice(half * LANES, (half + 1) * LANES)
            blocks = [
                recv[place[half * 8 + j], pair * levels : (pair + 1) * levels, :]
                for j in range(8)
            ]
            for i, value in enumerate(swap_grains(blocks)):
                k, r = divmod(i, 4)
                final[2 * pair + k, :, r, lanes] = value
    line = recv[0, 2 * levels : 2 * levels + 1, :]
    for g in range(1, recv.shape[0]):
        line = line + recv[g, 2 * levels : 2 * levels + 1, :]
    for h in range(HOURS):
        for t in range(4):
            at = (h * 4 + t) * 4
            stations[h, t, :, :] = line[:, at : at + 4]


def swaps(x, axis, count, piece):
    return [piece(x, 0)] + [
        lax.ppermute(piece(x, k), axis, [(i, i ^ k) for i in range(count)])
        for k in range(1, count)
    ]


def gather_winds(sizes, winds):
    n_lat, n_lev, _ = sizes
    own_lat, own_lev = lax.axis_index("lat"), lax.axis_index("lev")
    levels = winds.shape[1]

    def for_lat(x, k):
        return lax.dynamic_index_in_dim(x, own_lat ^ k, 0, keepdims=False)

    def for_lev(x, k):
        return lax.dynamic_index_in_dim(x, own_lev ^ k, 1, keepdims=False).reshape(-1, LANES)

    here = swaps(winds.reshape(n_lat, n_lev * levels, LANES), "lat", n_lat, for_lat)
    here = jnp.stack(here).reshape(n_lat, n_lev, levels, LANES)
    return swaps(here, "lev", n_lev, for_lev)


def call(kernel, outs, scratch=()):
    return pl.pallas_call(
        kernel,
        out_shape=[jax.ShapeDtypeStruct(s, F32) for s in outs],
        scratch_shapes=[pltpu.VMEM(s, F32) for s in scratch],
        compiler_params=pltpu.CompilerParams(vmem_limit_bytes=48 * 1024 * 1024),
    )


def regrouped(sizes, adjoint, wind_east, wind_north, kz_inverse, kz_regime, fp_cell, fp_owner, fp_station, fp_weight):
    n_lat, n_lev, n_lon = sizes
    levels = adjoint.shape[1]
    total = levels * n_lev
    group = n_lat * n_lev
    lat_count = n_lat * adjoint.shape[2]
    place = chunk_owner(n_lat, n_lev)
    to_west = ring_perm(n_lat, n_lev, n_lon, -1)
    to_east = ring_perm(n_lat, n_lev, n_lon, 1)

    def exchange(x):
        return lax.all_to_all(x, AXES, split_axis=0, concat_axis=0, tiled=True)

    def rims(first, last):
        return lax.ppermute(first, RING, to_west), lax.ppermute(last, RING, to_east)

    out_rows = 2 * levels + 1
    out_rows += -out_rows % 8
    in_rows = 2 * levels + 4
    in_rows += -in_rows % 8
    wind_rows = levels + -levels % 8
    given = (
        adjoint, wind_east, wind_north, kz_regime, fp_cell, fp_owner.reshape(1, -1), fp_station, fp_weight
    )
    fields, winds = pl.pallas_call(
        functools.partial(pack_kernel, place),
        in_specs=[pl.BlockSpec(memory_space=pltpu.HBM)] * len(given),
        out_shape=[
            jax.ShapeDtypeStruct(shape, F32)
            for shape in (
                (group, in_rows, LANES), (group, wind_rows, LANES)
            )
        ],
        scratch_shapes=[pltpu.VMEM(x.shape, x.dtype) for x in given]
        + [pltpu.SemaphoreType.DMA((len(given),))],
    )(*given)
    recv = exchange(fields)
    winds = gather_winds(sizes, winds[:, :levels])
    solved_0, regimes, first, last = call(
        functools.partial(unpack_solve_kernel, n_lev),
        [(4 * total, 256), (8, 256), (2 * total, LANES), (2 * total, LANES)],
        [(4 * total + 8, 256)],
    )(recv, kz_inverse)
    east_0, west_0 = rims(first, last)
    winds, first, last = call(
        functools.partial(unpack_winds_kernel, n_lev),
        [(2 * total, 256), (total, LANES), (total, LANES)],
        [(2 * total, 256), (n_lev, n_lat, levels, LANES)],
    )(*winds, regimes)
    wind_rims = rims(first, last)
    entries = recv[:, 2 * levels + 1 : 2 * levels + 4].reshape(-1, LANES)
    entries = jnp.stack(swaps(entries, "lat", n_lat, lambda x, k: x))
    solved_1, first, last = call(
        functools.partial(transport_solve_kernel, lat_count),
        [(4 * total, 256), (2 * total, LANES), (2 * total, LANES)],
        [(6, total, 384), (2, 4 * total, 384), (4 * total, 256)],
    )(solved_0, winds, regimes, kz_inverse, *wind_rims, east_0, west_0)
    east_1, west_1 = rims(first, last)
    (sums,) = call(functools.partial(footprint_kernel, n_lev), [(8, 64)])(
        entries, solved_0, solved_1
    )
    (back,) = call(
        functools.partial(transport_pack_kernel, lat_count, n_lev),
        [(group, out_rows, LANES)],
        [(6, total, 384), (2, 4 * total, 384), (4 * total, 256)],
    )(solved_1, winds, *wind_rims, east_1, west_1, sums)
    final, stations = call(
        functools.partial(unpack_kernel, place), [adjoint.shape, (HOURS, 4, 1, SPO)]
    )(exchange(back))
    return final, stations


def padded_2(x, sides, width, wrap):
    for axis, dim in sides:
        peers, length = (lax.axis_size(axis), x.shape[dim])
        up = [(i, (i + 1) % peers) for i in range(peers if wrap else peers - 1)]
        down = [(j, i) for i, j in up]
        last = lax.slice_in_dim(x, length - width, length, axis=dim)
        initial = lax.slice_in_dim(x, 0, width, axis=dim)
        before = lax.ppermute(last, axis, up)
        after = lax.ppermute(initial, axis, down)
        x = jnp.concatenate([before, x, after], axis=dim)
    return x


def lat_rim(values, rim_width):
    return padded_2(values, (("lat", 2),), rim_width, False)


def lon_rim(values, rim_width):
    return padded_2(values, (("lon", 3),), rim_width, True)


def lat_sweep(padded, north_face, south_face):
    middle = padded[:, :, 1:-1]
    return (
        middle
        + jnp.maximum(north_face, 0.0) * (padded[:, :, 2:] - middle)
        - jnp.minimum(south_face, 0.0) * (padded[:, :, :-2] - middle)
    )


def lon_sweep(padded, east_face, west_face):
    middle = padded[:, :, :, 1:-1]
    return (
        middle
        + jnp.maximum(east_face, 0.0) * (padded[:, :, :, 2:] - middle)
        - jnp.minimum(west_face, 0.0) * (padded[:, :, :, :-2] - middle)
    )


def shards(
    adjoint, wind_east, wind_north, kz_inverse, kz_regime, fp_cell, fp_owner, fp_station, fp_weight
):
    tracers, levels_dev, lat_rows, lon_cells = adjoint.shape
    row_index = lax.axis_index("lat") * lat_rows + lax.broadcasted_iota(
        jnp.int32, (1, lat_rows, 1), 1
    )
    last_row = lat_rows * lax.axis_size("lat") - 1
    north_face = jnp.where(row_index == last_row, jnp.zeros_like(wind_north), wind_north)
    south_face = lat_rim(north_face[None], 1)[0][:, :-2]
    west_face = lon_rim(wind_east[None], 1)[0][:, :, :-2]
    groups = lax.axis_size("lat") * lax.axis_size("lev")
    column_count = lat_rows * lon_cells // lax.axis_size("lev")
    first_column = lax.axis_index("lev") * column_count
    regime_rows = kz_regime.reshape(HOURS, lat_rows * lon_cells)
    cell_ids = fp_cell.reshape(-1)
    owners = fp_owner.reshape(-1)
    stations = fp_station.reshape(-1)
    weights = fp_weight.reshape(-1)
    entries = cell_ids.shape[0]
    adjoint_field = adjoint
    outputs = []
    for hour_step in range(HOURS):
        chosen = lax.dynamic_slice_in_dim(regime_rows[hour_step], first_column, column_count, 0)

        def column_solve(columns, chosen=chosen):
            result = jnp.zeros_like(columns)
            for regime in range(REGIMES):
                product = jnp.einsum(
                    "ji,tjp->tip", kz_inverse[regime], columns, precision=lax.Precision.HIGHEST
                )
                result = jnp.where(chosen[None, None, :] == regime, product, result)
            returned = lax.all_to_all(result, "lev", split_axis=1, concat_axis=2, tiled=True)
            return (returned, result)

        flat_field = adjoint_field.reshape(tracers, levels_dev, lat_rows * lon_cells)
        returned, solved = column_solve(
            lax.all_to_all(flat_field, "lev", split_axis=2, concat_axis=1, tiled=True)
        )
        lowest = solved[:, :FOOT_LEVELS, :].reshape(tracers, -1)
        picked = jnp.take(lowest, cell_ids, axis=1) * weights[None, :]
        capacity = 2 * entries // groups
        owner_hits = (owners[:, None] == jnp.arange(groups, dtype=jnp.int32)[None, :]).astype(
            jnp.int32
        )
        bucket_rank = jnp.sum(jnp.cumsum(owner_hits, axis=0) * owner_hits, axis=1) - 1
        slot_pos = owners * capacity + bucket_rank
        send_values = (
            jnp.zeros((tracers, groups * capacity), jnp.float32).at[:, slot_pos].set(picked)
        )
        send_ids = jnp.full((groups * capacity,), -1, jnp.int32).at[slot_pos].set(stations)
        arrived_values, arrived_ids = (
            lax.all_to_all(
                send_values.reshape(tracers, groups, capacity),
                ("lat", "lev"),
                split_axis=1,
                concat_axis=1,
                tiled=True,
            ),
            lax.all_to_all(
                send_ids.reshape(1, groups, capacity),
                ("lat", "lev"),
                split_axis=1,
                concat_axis=1,
                tiled=True,
            ),
        )
        matches = (
            arrived_ids[0][:, :, None] == jnp.arange(SPO, dtype=jnp.int32)[None, None, :]
        ).astype(jnp.float32)
        station_sums = jnp.einsum(
            "tgc,gcs->ts", arrived_values, matches, precision=lax.Precision.HIGHEST
        )
        outputs.append(station_sums)
        adjoint_field = returned.reshape(tracers, levels_dev, lat_rows, lon_cells)
        for substep in range(NSUB):
            adjoint_field = lat_sweep(lat_rim(adjoint_field, 1), north_face, south_face)
            adjoint_field = lon_sweep(lon_rim(adjoint_field, 1), wind_east, west_face)
    return (adjoint_field, jnp.stack(outputs)[:, :, None, :])


def fits(mesh_sizes, shape, kz_shape, entries):
    n_lat, n_lev, n_lon = mesh_sizes
    tracers, levels, rows, cells = shape
    return (
        tracers == 4
        and rows == 4
        and cells == 256
        and n_lat == 4
        and n_lat * n_lev == 16
        and levels * n_lev == kz_shape[1]
        and kz_shape[1] % 8 == 0
        and levels % 2 == 0
        and entries == 512
    )


def device_part(sizes, *arrays):
    if fits(sizes, arrays[0].shape, arrays[3].shape, arrays[5].shape[-1]):
        return regrouped(sizes, *arrays)
    return shards(*arrays)


def solution(mesh):
    sizes = tuple(mesh.shape[name] for name in RING)
    in_specs = (
        P(None, "lev", "lat", "lon"),
        P("lev", "lat", "lon"),
        P("lev", "lat", "lon"),
        P(),
        P(None, "lat", "lon"),
        P(AXES, "lon", None),
        P(AXES, "lon", None, None),
        P(AXES, "lon", None),
        P(AXES, "lon", None),
    )
    out_specs = (P(None, "lev", "lat", "lon"), P(None, None, "lon", AXES))
    return jax.shard_map(
        functools.partial(device_part, sizes),
        mesh=mesh,
        in_specs=in_specs,
        out_specs=out_specs,
        check_vma=False,
    )
```

```python
import functools
import jax
import jax.numpy as jnp
from jax import lax
from jax.experimental import pallas as pl
from jax.experimental.pallas import tpu as pltpu
from jax.sharding import PartitionSpec as P

NSUB = 4
HOURS = 2
REGIMES = 4
FOOT_LEVELS = 8
SPO = 4
LANES = 128
GRAIN = 16
F32 = jnp.float32
BF16 = jnp.bfloat16
AXES = ("lat", "lev")
RING = ("lat", "lev", "lon")


def chunk_owner(n_lat, n_lev):
    place = [0] * (n_lat * n_lev)
    for a in range(n_lat):
        for z in range(n_lev):
            chip, core = divmod(a, 2)
            step = z if chip % 2 == 0 else n_lev - 1 - z
            place[(chip * n_lev + step) * 2 + core] = a * n_lev + z
    return place


def ring_perm(n_lat, n_lev, n_lon, shift):
    place = chunk_owner(n_lat, n_lev)
    ring = [
        (place[::-1] if o % 2 else place)[d] * n_lon + o
        for o in range(n_lon)
        for d in range(len(place))
    ]
    count = len(ring)
    return [(ring[i], ring[(i + shift) % count]) for i in range(count)]


def owners(place):
    odd = lax.axis_index("lon") % 2 == 1
    return [jnp.where(odd, there, here) for here, there in zip(place, place[::-1])]


def lane_ids(rows):
    return lax.broadcasted_iota(jnp.int32, (rows, LANES), 1)


def swap_grains(blocks):
    blocks = list(blocks)
    grain = lane_ids(blocks[0].shape[0]) // GRAIN
    bit = len(blocks) // 2
    while bit:
        low = (grain & bit) == 0
        for i in range(len(blocks)):
            if i & bit == 0:
                a, b = blocks[i], blocks[i | bit]
                blocks[i] = jnp.where(low, a, pltpu.roll(b, bit * GRAIN, 1))
                blocks[i | bit] = jnp.where(low, pltpu.roll(a, LANES - bit * GRAIN, 1), b)
        bit //= 2
    return blocks


def swap_halves(a, b):
    low = lane_ids(a.shape[0]) < LANES // 2
    return (
        jnp.where(low, a, pltpu.roll(b, LANES // 2, 1)),
        jnp.where(low, pltpu.roll(a, LANES // 2, 1), b),
    )


def transpose_matrix():
    i = lax.broadcasted_iota(jnp.int32, (256, 256), 0)
    j = lax.broadcasted_iota(jnp.int32, (256, 256), 1)
    return ((i // 16 == j % 16) & (i % 16 == j // 16)).astype(F32).astype(BF16)


def split_two(x):
    high = x.astype(BF16)
    return high, (x - high.astype(F32)).astype(BF16)


def split_three(x):
    high, _ = split_two(x)
    rest = x - high.astype(F32)
    middle = rest.astype(BF16)
    return high, middle, (rest - middle.astype(F32)).astype(BF16)


def mm(a, b):
    return jnp.dot(a, b, preferred_element_type=F32)


def move_lanes(x, matrix):
    high, middle, low = split_three(x)
    return (mm(high, matrix) + mm(middle, matrix)) + mm(low, matrix)


def pack_kernel(place, *refs):
    count = (len(refs) - 3) // 2
    given, outs = refs[:count], refs[count : count + 2]
    held, sems = refs[count + 2 : -1], refs[-1]
    place = owners(place)
    copies = [
        pltpu.make_async_copy(a, b, sems.at[i]) for i, (a, b) in enumerate(zip(given, held))
    ]
    halves = [
        pltpu.make_async_copy(given[0].at[part], held[0].at[part], sems.at[at])
        for part, at in ((pl.ds(0, 2), 0), (pl.ds(2, 2), count))
    ]
    for copy in halves + copies[1:]:
        copy.start()
    adj, east, north, regime, cell, owner, station, weight = held
    fields, winds = outs
    levels = adj.shape[1]
    rows = adj.shape[2]

    def place_pieces(srcs, out, first, count):
        for half in range(2):
            lanes = slice(half * LANES, (half + 1) * LANES)
            for j, piece in enumerate(swap_grains([s[:, lanes] for s in srcs])):
                out[place[half * 8 + j], first : first + count, :] = piece

    for pair in range(2):
        halves[pair].wait()
        srcs = [adj[2 * pair + k, :, r, :] for k in range(2) for r in range(rows)]
        place_pieces(srcs, fields, pair * levels, levels)
    for copy in copies[1:]:
        copy.wait()
    srcs = [w[:, r, :] for w in (east, north) for r in range(rows)]
    place_pieces(srcs, winds, 0, levels)
    srcs = [regime[h, r : r + 1, :].astype(F32) for h in range(HOURS) for r in range(rows)]
    place_pieces(srcs, fields, 2 * levels, 1)
    cells = cell[0].astype(F32)
    stations = (owner[...] * SPO + station[0]).astype(F32)
    for g in range(fields.shape[0]):
        k = g // (fields.shape[0] // 4)
        for at, value in enumerate((cells, stations, weight[0])):
            row = 2 * levels + 1 + at
            fields[g, row : row + 1, :] = value[:, k * LANES : (k + 1) * LANES]


def solve_columns(high, low, kz_high, kz_low, regime, levels):
    product = mm(kz_high, high) + (mm(kz_low, high) + mm(kz_high, low))
    result = product[:levels]
    for k in range(1, REGIMES):
        result = jnp.where(regime == float(k), product[k * levels : (k + 1) * levels], result)
    return result


def mixing(kz):
    stacked = jnp.concatenate([kz[k].T for k in range(REGIMES)], axis=0)
    return split_two(stacked)


def rim_messages(top, bottom, first, last, rows):
    half = LANES // 2
    low = lane_ids(top.shape[0]) < half
    first[rows, :] = jnp.where(low, top[:, :LANES], pltpu.roll(bottom[:, :LANES], half, 1))
    last[rows, :] = jnp.where(low, pltpu.roll(top[:, LANES:], half, 1), bottom[:, LANES:])


def unpack_solve_kernel(n_lev, recv, kz, solved, regimes, first, last, field):
    total = kz.shape[1]
    levels = total // n_lev
    for pair in range(2):
        for z in range(n_lev):
            for half in range(2):
                lanes = slice(half * LANES, (half + 1) * LANES)
                a, b = [
                    recv[(2 * half + k) * n_lev + z, pair * levels : (pair + 1) * levels, :]
                    for k in range(2)
                ]
                for k, value in enumerate(swap_halves(a, b)):
                    base = (2 * pair + k) * total + z * levels
                    field[base : base + levels, lanes] = value
    base = 4 * total
    field[base : base + 8, :] = jnp.zeros((8, 256), F32)
    for half in range(2):
        lanes = slice(half * LANES, (half + 1) * LANES)
        a, b = [
            recv[(2 * half + k) * n_lev, 2 * levels : 2 * levels + 1, :] for k in range(2)
        ]
        for k, value in enumerate(swap_halves(a, b)):
            field[base + k : base + k + 1, lanes] = value
    matrix = transpose_matrix()
    regime = mm(field[base : base + 8, :].astype(BF16), matrix)
    regimes[...] = regime
    kz_high, kz_low = mixing(kz)
    for t in range(4):
        high, low = split_two(field[t * total : (t + 1) * total, :])
        high = mm(high, matrix).astype(BF16)
        low = mm(low, matrix).astype(BF16)
        solved[t * total : (t + 1) * total, :] = solve_columns(
            high, low, kz_high, kz_low, regime[0:1], total
        )
    rim_messages(
        solved[0 : 2 * total, :], solved[2 * total :, :], first, last, slice(0, 2 * total)
    )


def unpack_winds_kernel(n_lev, *refs):
    pieces, (winds, first, last, field, others) = refs[:n_lev], refs[n_lev + 1 :]
    total = winds.shape[0] // 2
    levels = total // n_lev
    for m in range(n_lev):
        for k in range(others.shape[1]):
            others[m, k] = pieces[m][k * levels : (k + 1) * levels, :]
    own_lat, own_lev = lax.axis_index("lat"), lax.axis_index("lev")
    for z in range(n_lev):
        for half in range(2):
            lanes = slice(half * LANES, (half + 1) * LANES)
            a, b = [
                others[z ^ own_lev, (2 * half + k) ^ own_lat, 0:levels, :] for k in range(2)
            ]
            for k, value in enumerate(swap_halves(a, b)):
                base = k * total + z * levels
                field[base : base + levels, lanes] = value
    winds[...] = move_lanes(field[...], transpose_matrix())
    rim_messages(winds[0:total, :], winds[total:, :], first, last, slice(0, total))


def rim_lanes(from_east, from_west, rows, upper):
    half = LANES // 2
    east, west = from_east[rows, :], from_west[rows, :]
    low = lane_ids(east.shape[0]) < half
    if upper:
        return jnp.where(low, pltpu.roll(east, half, 1), west)
    return jnp.where(low, east, pltpu.roll(west, half, 1))


def columns(ref, rows):
    return [ref[rows, i * LANES : (i + 1) * LANES] for i in range(3)]


def pair_columns(ref, rows):
    return [ref[rows, i * LANES : (i + 1) * LANES] for i in range(2)]


def turned(x, shift):
    return pltpu.roll(x, shift % LANES, 1)


def stepped(blocks, shift):
    count = len(blocks)
    lane = lane_ids(blocks[0].shape[0])
    moved = [turned(x, shift) for x in blocks]
    if shift > 0:
        return [jnp.where(lane < shift, moved[i - 1], moved[i]) for i in range(count)]
    return [
        jnp.where(lane >= LANES + shift, moved[(i + 1) % count], moved[i]) for i in range(count)
    ]


def face_weights(lat_count, winds, from_east, from_west, total, faces):
    rims = slice(0, total)
    east = pair_columns(winds, slice(0, total)) + [rim_lanes(from_east, from_west, rims, False)]
    north = pair_columns(winds, slice(total, 2 * total)) + [
        rim_lanes(from_east, from_west, rims, True)
    ]
    lat = lane_ids(total) % lat_count
    north = [jnp.where(lat == lat_count - 1, 0.0, x) for x in north]
    west = stepped(east, lat_count)
    for i in range(3):
        lanes = slice(i * LANES, (i + 1) * LANES)
        after = jnp.maximum(north[i], 0.0)
        before = -jnp.minimum(jnp.where(lat == 0, 0.0, turned(north[i], 1)), 0.0)
        faces[0, :, lanes] = 1.0 - after - before
        faces[1, :, lanes] = after
        faces[2, :, lanes] = before
        after = jnp.maximum(east[i], 0.0)
        before = -jnp.minimum(west[i], 0.0)
        faces[3, :, lanes] = 1.0 - after - before
        faces[4, :, lanes] = after
        faces[5, :, lanes] = before


def transport(lat_count, field, east_rows, west_rows, faces, total, buffers, result):
    for t in range(4):
        own = slice(t * total, (t + 1) * total)
        rim = slice((t % 2) * total, (t % 2 + 1) * total)
        buffers[0, own, 0:256] = field[own, :]
        buffers[0, own, 256:384] = rim_lanes(east_rows, west_rows, rim, t >= 2)
    for step in range(2 * NSUB):
        last = step == 2 * NSUB - 1
        for t in range(4):
            own = slice(t * total, (t + 1) * total)
            f = columns(buffers.at[step % 2], own)
            if step % 2 == 0:
                after = [turned(x, -1) for x in f]
                before = [turned(x, 1) for x in f]
            else:
                after = stepped(f, -lat_count)
                before = stepped(f, lat_count)
            base = 3 * (step % 2)
            for i in range(2 if last else 3):
                lanes = slice(i * LANES, (i + 1) * LANES)
                value = (
                    faces[base, :, lanes] * f[i]
                    + faces[base + 1, :, lanes] * after[i]
                    + faces[base + 2, :, lanes] * before[i]
                )
                if last:
                    result[own, lanes] = value
                else:
                    buffers[(step + 1) % 2, own, lanes] = value


def transport_solve_kernel(
    lat_count, field, winds, regimes, kz, wind_east, wind_west, from_east, from_west, solved, first, last, faces, buffers, moved
):
    total = kz.shape[1]
    face_weights(lat_count, winds, wind_east, wind_west, total, faces)
    transport(lat_count, field, from_east, from_west, faces, total, buffers, moved)
    kz_high, kz_low = mixing(kz)
    for t in range(4):
        high, low = split_two(moved[t * total : (t + 1) * total, :])
        solved[t * total : (t + 1) * total, :] = solve_columns(
            high, low, kz_high, kz_low, regimes[1:2, :], total
        )
    rim_messages(
        solved[0 : 2 * total, :], solved[2 * total :, :], first, last, slice(0, 2 * total)
    )


def footprint_kernel(n_lev, quarters, hour_0, hour_1, sums):
    own_lat, own_lev = lax.axis_index("lat"), lax.axis_index("lev")
    chip, core = own_lat // 2, own_lat % 2
    step = jnp.where(chip % 2 == 0, own_lev, n_lev - 1 - own_lev)
    chunk = (chip * n_lev + step) * 2 + core
    odd = lax.axis_index("lon") % 2 == 1
    group = quarters.shape[1] // 3
    first_lon = jnp.where(odd, group - 1 - chunk, chunk) * GRAIN
    total = hour_0.shape[0] // 4
    matrix = transpose_matrix()
    low = jnp.concatenate(
        [h[t * total : t * total + FOOT_LEVELS, :] for h in (hour_0, hour_1) for t in range(4)],
        axis=0,
    )
    parts = mm(jnp.concatenate(split_three(low), axis=0), matrix).astype(BF16)
    count = low.shape[0]
    acc = jnp.zeros((count, 64), F32)
    cell_ids = lax.broadcasted_iota(jnp.int32, (GRAIN, 512), 0)
    level_ids = lax.broadcasted_iota(jnp.int32, (FOOT_LEVELS, 512), 0)
    station_ids = lax.broadcasted_iota(jnp.int32, (64, 512), 0)
    for row in range(group):

        def entries(at):
            return jnp.concatenate(
                [quarters[k, 3 * row + at : 3 * row + at + 1, :] for k in range(4)], axis=1
            )

        code = entries(0).astype(jnp.int32)
        station = entries(1).astype(jnp.int32)
        weight = entries(2)
        cells = ((code & 255) - first_lon == cell_ids).astype(F32).astype(BF16)
        picked = mm(parts[:, row * GRAIN : (row + 1) * GRAIN], cells)
        picked = (picked[:count] + picked[count : 2 * count]) + picked[2 * count :]
        level = jnp.where((code >> 8) == level_ids, weight, 0.0)
        picked = picked * jnp.concatenate([level] * (count // FOOT_LEVELS), axis=0)
        named = (station == station_ids).astype(F32).astype(BF16)
        high, rest = split_two(picked)
        both = jnp.concatenate([high, rest], axis=0)
        both = lax.dot_general(both, named, (((1,), (1,)), ((), ())), preferred_element_type=F32)
        acc = acc + (both[:count] + both[count:])
    sums[...] = jnp.sum(acc.reshape(count // FOOT_LEVELS, FOOT_LEVELS, 64), axis=1)


def face_kernel(lat_count, winds, wind_east, wind_west, _, faces):
    face_weights(lat_count, winds, wind_east, wind_west, winds.shape[0] // 2, faces)


def transport_pack_kernel(
    lat_count, n_lev, field, faces, from_east, from_west, sums, out, buffers, moved
):
    total = faces.shape[1]
    levels = total // n_lev
    transport(lat_count, field, from_east, from_west, faces, total, buffers, moved)
    matrix = transpose_matrix()
    for pair in range(2):
        for k in range(2):
            rows = slice((2 * pair + k) * total, (2 * pair + k + 1) * total)
            moved[rows, :] = move_lanes(moved[rows, :], matrix)
        for z in range(n_lev):
            for half in range(2):
                lanes = slice(half * LANES, (half + 1) * LANES)
                a, b = [
                    moved[
                        (2 * pair + k) * total + z * levels : (2 * pair + k) * total
                        + (z + 1) * levels,
                        lanes,
                    ]
                    for k in range(2)
                ]
                for k, value in enumerate(swap_halves(a, b)):
                    out[
                        (2 * half + k) * n_lev + z, pair * levels : (pair + 1) * levels, :
                    ] = value
    wide = jnp.concatenate([sums[...], jnp.zeros((8, 64), F32)], axis=1)
    line = lax.broadcasted_iota(jnp.int32, (8, LANES), 0)
    spread = jnp.zeros((8, LANES), F32)
    for k in range(8):
        spread = jnp.where(line == k, pltpu.roll(wide, 4 * k, 1) if k else wide, spread)
    keep = lax.broadcasted_iota(jnp.int32, (8, LANES), 1) // 4 == line
    for g in range(out.shape[0]):
        value = pltpu.roll(spread, LANES - 4 * g, 1) if g else spread
        value = jnp.sum(jnp.where(keep, value, 0.0), axis=0, keepdims=True)
        out[g, 2 * levels : 2 * levels + 1, :] = value


def unpack_kernel(place, recv, final, stations):
    place = owners(place)
    levels = final.shape[1]
    for pair in range(2):
        for half in range(2):
            lanes = slice(half * LANES, (half + 1) * LANES)
            blocks = [
                recv[place[half * 8 + j], pair * levels : (pair + 1) * levels, :]
                for j in range(8)
            ]
            for i, value in enumerate(swap_grains(blocks)):
                k, r = divmod(i, 4)
                final[2 * pair + k, :, r, lanes] = value
    line = recv[0, 2 * levels : 2 * levels + 1, :]
    for g in range(1, recv.shape[0]):
        line = line + recv[g, 2 * levels : 2 * levels + 1, :]
    for h in range(HOURS):
        for t in range(4):
            at = (h * 4 + t) * 4
            stations[h, t, :, :] = line[:, at : at + 4]


def swaps(x, axis, count, piece):
    return [piece(x, 0)] + [
        lax.ppermute(piece(x, k), axis, [(i, i ^ k) for i in range(count)])
        for k in range(1, count)
    ]


def gather_winds(sizes, winds):
    n_lat, n_lev, _ = sizes
    own_lat, own_lev = lax.axis_index("lat"), lax.axis_index("lev")
    levels = winds.shape[1]

    def for_lat(x, k):
        return lax.dynamic_index_in_dim(x, own_lat ^ k, 0, keepdims=False)

    def for_lev(x, k):
        return lax.dynamic_index_in_dim(x, own_lev ^ k, 1, keepdims=False).reshape(-1, LANES)

    here = swaps(winds.reshape(n_lat, n_lev * levels, LANES), "lat", n_lat, for_lat)
    here = jnp.stack(here).reshape(n_lat, n_lev, levels, LANES)
    return swaps(here, "lev", n_lev, for_lev)


def call(kernel, outs, scratch=()):
    return pl.pallas_call(
        kernel,
        out_shape=[jax.ShapeDtypeStruct(s, F32) for s in outs],
        scratch_shapes=[pltpu.VMEM(s, F32) for s in scratch],
        compiler_params=pltpu.CompilerParams(vmem_limit_bytes=48 * 1024 * 1024),
    )


def regrouped(sizes, adjoint, wind_east, wind_north, kz_inverse, kz_regime, fp_cell, fp_owner, fp_station, fp_weight):
    n_lat, n_lev, n_lon = sizes
    levels = adjoint.shape[1]
    total = levels * n_lev
    group = n_lat * n_lev
    lat_count = n_lat * adjoint.shape[2]
    place = chunk_owner(n_lat, n_lev)
    to_west = ring_perm(n_lat, n_lev, n_lon, -1)
    to_east = ring_perm(n_lat, n_lev, n_lon, 1)

    def exchange(x):
        return lax.all_to_all(x, AXES, split_axis=0, concat_axis=0, tiled=True)

    def rims(first, last):
        return lax.ppermute(first, RING, to_west), lax.ppermute(last, RING, to_east)

    out_rows = 2 * levels + 1
    out_rows += -out_rows % 8
    in_rows = 2 * levels + 4
    in_rows += -in_rows % 8
    wind_rows = levels + -levels % 8
    given = (
        adjoint, wind_east, wind_north, kz_regime, fp_cell, fp_owner.reshape(1, -1), fp_station, fp_weight
    )
    fields, winds = pl.pallas_call(
        functools.partial(pack_kernel, place),
        in_specs=[pl.BlockSpec(memory_space=pltpu.HBM)] * len(given),
        out_shape=[
            jax.ShapeDtypeStruct(shape, F32)
            for shape in (
                (group, in_rows, LANES), (group, wind_rows, LANES)
            )
        ],
        scratch_shapes=[pltpu.VMEM(x.shape, x.dtype) for x in given]
        + [pltpu.SemaphoreType.DMA((len(given) + 1,))],
        compiler_params=pltpu.CompilerParams(vmem_limit_bytes=48 * 1024 * 1024),
    )(*[pltpu.with_memory_space_constraint(x, pltpu.HBM) for x in given])
    recv = exchange(fields)
    winds = gather_winds(sizes, winds[:, :levels])
    solved_0, regimes, first, last = call(
        functools.partial(unpack_solve_kernel, n_lev),
        [(4 * total, 256), (8, 256), (2 * total, LANES), (2 * total, LANES)],
        [(4 * total + 8, 256)],
    )(recv, kz_inverse)
    east_0, west_0 = rims(first, last)
    winds, first, last = call(
        functools.partial(unpack_winds_kernel, n_lev),
        [(2 * total, 256), (total, LANES), (total, LANES)],
        [(2 * total, 256), (n_lev, n_lat, levels, LANES)],
    )(*winds, regimes)
    wind_rims = rims(first, last)
    entries = recv[:, 2 * levels + 1 : 2 * levels + 4].reshape(-1, LANES)
    entries = jnp.stack(swaps(entries, "lat", n_lat, lambda x, k: x))
    solved_1, first, last = call(
        functools.partial(transport_solve_kernel, lat_count),
        [(4 * total, 256), (2 * total, LANES), (2 * total, LANES)],
        [(6, total, 384), (2, 4 * total, 384), (4 * total, 256)],
    )(solved_0, winds, regimes, kz_inverse, *wind_rims, east_0, west_0)
    east_1, west_1 = rims(first, last)
    (sums,) = call(functools.partial(footprint_kernel, n_lev), [(8, 64)])(
        entries, solved_0, solved_1
    )
    (faces,) = call(functools.partial(face_kernel, lat_count), [(6, total, 384)])(
        winds, *wind_rims, first
    )
    (back,) = call(
        functools.partial(transport_pack_kernel, lat_count, n_lev),
        [(group, out_rows, LANES)],
        [(2, 4 * total, 384), (4 * total, 256)],
    )(solved_1, faces, east_1, west_1, sums)
    final, stations = call(
        functools.partial(unpack_kernel, place), [adjoint.shape, (HOURS, 4, 1, SPO)]
    )(exchange(back))
    return final, stations


def padded_2(x, sides, width, wrap):
    for axis, dim in sides:
        peers, length = (lax.axis_size(axis), x.shape[dim])
        up = [(i, (i + 1) % peers) for i in range(peers if wrap else peers - 1)]
        down = [(j, i) for i, j in up]
        last = lax.slice_in_dim(x, length - width, length, axis=dim)
        initial = lax.slice_in_dim(x, 0, width, axis=dim)
        before = lax.ppermute(last, axis, up)
        after = lax.ppermute(initial, axis, down)
        x = jnp.concatenate([before, x, after], axis=dim)
    return x


def lat_rim(values, rim_width):
    return padded_2(values, (("lat", 2),), rim_width, False)


def lon_rim(values, rim_width):
    return padded_2(values, (("lon", 3),), rim_width, True)


def lat_sweep(padded, north_face, south_face):
    middle = padded[:, :, 1:-1]
    return (
        middle
        + jnp.maximum(north_face, 0.0) * (padded[:, :, 2:] - middle)
        - jnp.minimum(south_face, 0.0) * (padded[:, :, :-2] - middle)
    )


def lon_sweep(padded, east_face, west_face):
    middle = padded[:, :, :, 1:-1]
    return (
        middle
        + jnp.maximum(east_face, 0.0) * (padded[:, :, :, 2:] - middle)
        - jnp.minimum(west_face, 0.0) * (padded[:, :, :, :-2] - middle)
    )


def shards(
    adjoint, wind_east, wind_north, kz_inverse, kz_regime, fp_cell, fp_owner, fp_station, fp_weight
):
    tracers, levels_dev, lat_rows, lon_cells = adjoint.shape
    row_index = lax.axis_index("lat") * lat_rows + lax.broadcasted_iota(
        jnp.int32, (1, lat_rows, 1), 1
    )
    last_row = lat_rows * lax.axis_size("lat") - 1
    north_face = jnp.where(row_index == last_row, jnp.zeros_like(wind_north), wind_north)
    south_face = lat_rim(north_face[None], 1)[0][:, :-2]
    west_face = lon_rim(wind_east[None], 1)[0][:, :, :-2]
    groups = lax.axis_size("lat") * lax.axis_size("lev")
    column_count = lat_rows * lon_cells // lax.axis_size("lev")
    first_column = lax.axis_index("lev") * column_count
    regime_rows = kz_regime.reshape(HOURS, lat_rows * lon_cells)
    cell_ids = fp_cell.reshape(-1)
    owners = fp_owner.reshape(-1)
    stations = fp_station.reshape(-1)
    weights = fp_weight.reshape(-1)
    entries = cell_ids.shape[0]
    adjoint_field = adjoint
    outputs = []
    for hour_step in range(HOURS):
        chosen = lax.dynamic_slice_in_dim(regime_rows[hour_step], first_column, column_count, 0)

        def column_solve(columns, chosen=chosen):
            result = jnp.zeros_like(columns)
            for regime in range(REGIMES):
                product = jnp.einsum(
                    "ji,tjp->tip", kz_inverse[regime], columns, precision=lax.Precision.HIGHEST
                )
                result = jnp.where(chosen[None, None, :] == regime, product, result)
            returned = lax.all_to_all(result, "lev", split_axis=1, concat_axis=2, tiled=True)
            return (returned, result)

        flat_field = adjoint_field.reshape(tracers, levels_dev, lat_rows * lon_cells)
        returned, solved = column_solve(
            lax.all_to_all(flat_field, "lev", split_axis=2, concat_axis=1, tiled=True)
        )
        lowest = solved[:, :FOOT_LEVELS, :].reshape(tracers, -1)
        picked = jnp.take(lowest, cell_ids, axis=1) * weights[None, :]
        capacity = 2 * entries // groups
        owner_hits = (owners[:, None] == jnp.arange(groups, dtype=jnp.int32)[None, :]).astype(
            jnp.int32
        )
        bucket_rank = jnp.sum(jnp.cumsum(owner_hits, axis=0) * owner_hits, axis=1) - 1
        slot_pos = owners * capacity + bucket_rank
        send_values = (
            jnp.zeros((tracers, groups * capacity), jnp.float32).at[:, slot_pos].set(picked)
        )
        send_ids = jnp.full((groups * capacity,), -1, jnp.int32).at[slot_pos].set(stations)
        arrived_values, arrived_ids = (
            lax.all_to_all(
                send_values.reshape(tracers, groups, capacity),
                ("lat", "lev"),
                split_axis=1,
                concat_axis=1,
                tiled=True,
            ),
            lax.all_to_all(
                send_ids.reshape(1, groups, capacity),
                ("lat", "lev"),
                split_axis=1,
                concat_axis=1,
                tiled=True,
            ),
        )
        matches = (
            arrived_ids[0][:, :, None] == jnp.arange(SPO, dtype=jnp.int32)[None, None, :]
        ).astype(jnp.float32)
        station_sums = jnp.einsum(
            "tgc,gcs->ts", arrived_values, matches, precision=lax.Precision.HIGHEST
        )
        outputs.append(station_sums)
        adjoint_field = returned.reshape(tracers, levels_dev, lat_rows, lon_cells)
        for substep in range(NSUB):
            adjoint_field = lat_sweep(lat_rim(adjoint_field, 1), north_face, south_face)
            adjoint_field = lon_sweep(lon_rim(adjoint_field, 1), wind_east, west_face)
    return (adjoint_field, jnp.stack(outputs)[:, :, None, :])


def fits(mesh_sizes, shape, kz_shape, entries):
    n_lat, n_lev, n_lon = mesh_sizes
    tracers, levels, rows, cells = shape
    return (
        tracers == 4
        and rows == 4
        and cells == 256
        and n_lat == 4
        and n_lat * n_lev == 16
        and levels * n_lev == kz_shape[1]
        and kz_shape[1] % 8 == 0
        and levels % 2 == 0
        and entries == 512
    )


def device_part(sizes, *arrays):
    if fits(sizes, arrays[0].shape, arrays[3].shape, arrays[5].shape[-1]):
        return regrouped(sizes, *arrays)
    return shards(*arrays)


def solution(mesh):
    sizes = tuple(mesh.shape[name] for name in RING)
    in_specs = (
        P(None, "lev", "lat", "lon"),
        P("lev", "lat", "lon"),
        P("lev", "lat", "lon"),
        P(),
        P(None, "lat", "lon"),
        P(AXES, "lon", None),
        P(AXES, "lon", None, None),
        P(AXES, "lon", None),
        P(AXES, "lon", None),
    )
    out_specs = (P(None, "lev", "lat", "lon"), P(None, None, "lon", AXES))
    return jax.shard_map(
        functools.partial(device_part, sizes),
        mesh=mesh,
        in_specs=in_specs,
        out_specs=out_specs,
        check_vma=False,
    )
```

```python
import functools
import jax
import jax.numpy as jnp
from jax import lax
from jax.experimental import pallas as pl
from jax.experimental.pallas import tpu as pltpu
from jax.sharding import PartitionSpec as P

NSUB = 4
HOURS = 2
REGIMES = 4
FOOT_LEVELS = 8
SPO = 4
LANES = 128
GRAIN = 16
F32 = jnp.float32
BF16 = jnp.bfloat16
AXES = ("lat", "lev")
RING = ("lat", "lev", "lon")


def chunk_owner(n_lat, n_lev):
    place = [0] * (n_lat * n_lev)
    for a in range(n_lat):
        for z in range(n_lev):
            chip, core = divmod(a, 2)
            step = z if chip % 2 == 0 else n_lev - 1 - z
            place[(chip * n_lev + step) * 2 + core] = a * n_lev + z
    return place


def ring_perm(n_lat, n_lev, n_lon, shift):
    place = chunk_owner(n_lat, n_lev)
    ring = [
        (place[::-1] if o % 2 else place)[d] * n_lon + o
        for o in range(n_lon)
        for d in range(len(place))
    ]
    count = len(ring)
    return [(ring[i], ring[(i + shift) % count]) for i in range(count)]


def owners(place):
    odd = lax.axis_index("lon") % 2 == 1
    return [jnp.where(odd, there, here) for here, there in zip(place, place[::-1])]


def lane_ids(rows):
    return lax.broadcasted_iota(jnp.int32, (rows, LANES), 1)


def swap_grains(blocks):
    blocks = list(blocks)
    grain = lane_ids(blocks[0].shape[0]) // GRAIN
    bit = len(blocks) // 2
    while bit:
        low = (grain & bit) == 0
        for i in range(len(blocks)):
            if i & bit == 0:
                a, b = blocks[i], blocks[i | bit]
                blocks[i] = jnp.where(low, a, pltpu.roll(b, bit * GRAIN, 1))
                blocks[i | bit] = jnp.where(low, pltpu.roll(a, LANES - bit * GRAIN, 1), b)
        bit //= 2
    return blocks


def swap_halves(a, b):
    low = lane_ids(a.shape[0]) < LANES // 2
    return (
        jnp.where(low, a, pltpu.roll(b, LANES // 2, 1)),
        jnp.where(low, pltpu.roll(a, LANES // 2, 1), b),
    )


def lane_matrix(back):
    major = lax.broadcasted_iota(jnp.int32, (256, 256), 1 if back else 0)
    work = lax.broadcasted_iota(jnp.int32, (256, 256), 0 if back else 1)
    lon = (work % LANES) // GRAIN * 2 + work // LANES
    return ((major // GRAIN == work % GRAIN) & (major % GRAIN == lon)).astype(F32).astype(BF16)


def split_two(x):
    high = x.astype(BF16)
    return high, (x - high.astype(F32)).astype(BF16)


def split_three(x):
    high, _ = split_two(x)
    rest = x - high.astype(F32)
    middle = rest.astype(BF16)
    return high, middle, (rest - middle.astype(F32)).astype(BF16)


def mm(a, b):
    return jnp.dot(a, b, preferred_element_type=F32)


def move_lanes(x, matrix):
    high, middle, low = split_three(x)
    return (mm(high, matrix) + mm(middle, matrix)) + mm(low, matrix)


def pack_kernel(place, *refs):
    count = (len(refs) - 3) // 2
    given, outs = refs[:count], refs[count : count + 2]
    held, sems = refs[count + 2 : -1], refs[-1]
    place = owners(place)
    copies = [
        pltpu.make_async_copy(a, b, sems.at[i]) for i, (a, b) in enumerate(zip(given, held))
    ]
    halves = [
        pltpu.make_async_copy(given[0].at[part], held[0].at[part], sems.at[at])
        for part, at in ((pl.ds(0, 2), 0), (pl.ds(2, 2), count))
    ]
    for copy in halves + copies[1:]:
        copy.start()
    adj, east, north, regime, cell, owner, station, weight = held
    fields, winds = outs
    levels = adj.shape[1]
    rows = adj.shape[2]

    def place_pieces(srcs, out, first, count):
        for half in range(2):
            lanes = slice(half * LANES, (half + 1) * LANES)
            for j, piece in enumerate(swap_grains([s[:, lanes] for s in srcs])):
                out[place[half * 8 + j], first : first + count, :] = piece

    for pair in range(2):
        halves[pair].wait()
        srcs = [adj[2 * pair + k, :, r, :] for k in range(2) for r in range(rows)]
        place_pieces(srcs, fields, pair * levels, levels)
    for copy in copies[1:]:
        copy.wait()
    srcs = [w[:, r, :] for w in (east, north) for r in range(rows)]
    place_pieces(srcs, winds, 0, levels)
    srcs = [regime[h, r : r + 1, :].astype(F32) for h in range(HOURS) for r in range(rows)]
    place_pieces(srcs, fields, 2 * levels, 1)
    cells = cell[0].astype(F32)
    stations = (owner[...] * SPO + station[0]).astype(F32)
    for g in range(fields.shape[0]):
        k = g // (fields.shape[0] // 4)
        for at, value in enumerate((cells, stations, weight[0])):
            row = 2 * levels + 1 + at
            fields[g, row : row + 1, :] = value[:, k * LANES : (k + 1) * LANES]


def solve_columns(high, low, kz_high, kz_low, regime, levels):
    product = mm(kz_high, high) + (mm(kz_low, high) + mm(kz_high, low))
    result = product[:levels]
    for k in range(1, REGIMES):
        result = jnp.where(regime == float(k), product[k * levels : (k + 1) * levels], result)
    return result


def mixing(kz):
    stacked = jnp.concatenate([kz[k].T for k in range(REGIMES)], axis=0)
    return split_two(stacked)


def rim_messages(top, bottom, first, last, rows):
    pair = lane_ids(top.shape[0]) // (2 * GRAIN)
    blocks = [top[:, :LANES], top[:, LANES:], bottom[:, :LANES], bottom[:, LANES:]]

    def gathered(offset):
        out = blocks[3] if offset == 3 else turned(blocks[3], (3 - offset) * 2 * GRAIN)
        for k in range(3):
            shift = (k - offset) * 2 * GRAIN
            out = jnp.where(pair == k, turned(blocks[k], shift) if shift else blocks[k], out)
        return out

    first[rows, :] = gathered(0)
    last[rows, :] = gathered(3)


def unpack_solve_kernel(n_lev, recv, kz, solved, regimes, first, last, field):
    total = kz.shape[1]
    levels = total // n_lev
    for pair in range(2):
        for z in range(n_lev):
            for half in range(2):
                lanes = slice(half * LANES, (half + 1) * LANES)
                a, b = [
                    recv[(2 * half + k) * n_lev + z, pair * levels : (pair + 1) * levels, :]
                    for k in range(2)
                ]
                for k, value in enumerate(swap_halves(a, b)):
                    base = (2 * pair + k) * total + z * levels
                    field[base : base + levels, lanes] = value
    base = 4 * total
    field[base : base + 8, :] = jnp.zeros((8, 256), F32)
    for half in range(2):
        lanes = slice(half * LANES, (half + 1) * LANES)
        a, b = [
            recv[(2 * half + k) * n_lev, 2 * levels : 2 * levels + 1, :] for k in range(2)
        ]
        for k, value in enumerate(swap_halves(a, b)):
            field[base + k : base + k + 1, lanes] = value
    matrix = lane_matrix(False)
    regime = mm(field[base : base + 8, :].astype(BF16), matrix)
    regimes[...] = regime
    kz_high, kz_low = mixing(kz)
    for t in range(4):
        high, low = split_two(field[t * total : (t + 1) * total, :])
        high = mm(high, matrix).astype(BF16)
        low = mm(low, matrix).astype(BF16)
        solved[t * total : (t + 1) * total, :] = solve_columns(
            high, low, kz_high, kz_low, regime[0:1], total
        )
    rim_messages(
        solved[0 : 2 * total, :], solved[2 * total :, :], first, last, slice(0, 2 * total)
    )


def unpack_winds_kernel(n_lev, *refs):
    pieces, (winds, first, last, field, others) = refs[:n_lev], refs[n_lev + 1 :]
    total = winds.shape[0] // 2
    levels = total // n_lev
    for m in range(n_lev):
        for k in range(others.shape[1]):
            others[m, k] = pieces[m][k * levels : (k + 1) * levels, :]
    own_lat, own_lev = lax.axis_index("lat"), lax.axis_index("lev")
    for z in range(n_lev):
        for half in range(2):
            lanes = slice(half * LANES, (half + 1) * LANES)
            a, b = [
                others[z ^ own_lev, (2 * half + k) ^ own_lat, 0:levels, :] for k in range(2)
            ]
            for k, value in enumerate(swap_halves(a, b)):
                base = k * total + z * levels
                field[base : base + levels, lanes] = value
    winds[...] = move_lanes(field[...], lane_matrix(False))
    rim_messages(winds[0:total, :], winds[total:, :], first, last, slice(0, total))


def rim_lanes(from_east, from_west, rows, upper):
    half = LANES // 2
    east, west = from_east[rows, :], from_west[rows, :]
    lane = lane_ids(east.shape[0])
    if upper:
        both = jnp.where(lane < half, pltpu.roll(east, half, 1), west)
    else:
        both = jnp.where(lane < half, east, pltpu.roll(west, half, 1))
    place = lane // GRAIN % 4
    both = jnp.where(place == 1, turned(both, -GRAIN), jnp.where(place == 2, turned(both, GRAIN), both))
    return both


def columns(ref, rows):
    return [ref[rows, i * LANES : (i + 1) * LANES] for i in range(3)]


def pair_columns(ref, rows):
    return [ref[rows, i * LANES : (i + 1) * LANES] for i in range(2)]


def turned(x, shift):
    return pltpu.roll(x, shift % LANES, 1)


def stepped(blocks, shift):
    even, odd, rim = blocks
    lane = lane_ids(even.shape[0])
    outer = turned(rim, shift)
    if shift > 0:
        inner, edge = turned(odd, shift), lane < shift
        return [jnp.where(edge, outer, inner), even, jnp.where(edge, inner, outer)]
    inner, edge = turned(even, shift), lane >= LANES + shift
    return [odd, jnp.where(edge, outer, inner), jnp.where(edge, inner, outer)]


def face_weights(lat_count, winds, from_east, from_west, total, faces):
    rims = slice(0, total)
    east = pair_columns(winds, slice(0, total)) + [rim_lanes(from_east, from_west, rims, False)]
    north = pair_columns(winds, slice(total, 2 * total)) + [
        rim_lanes(from_east, from_west, rims, True)
    ]
    lat = lane_ids(total) % lat_count
    north = [jnp.where(lat == lat_count - 1, 0.0, x) for x in north]
    west = stepped(east, lat_count)
    for i in range(3):
        lanes = slice(i * LANES, (i + 1) * LANES)
        after = jnp.maximum(north[i], 0.0)
        before = -jnp.minimum(jnp.where(lat == 0, 0.0, turned(north[i], 1)), 0.0)
        faces[0, :, lanes] = 1.0 - after - before
        faces[1, :, lanes] = after
        faces[2, :, lanes] = before
        after = jnp.maximum(east[i], 0.0)
        before = -jnp.minimum(west[i], 0.0)
        faces[3, :, lanes] = 1.0 - after - before
        faces[4, :, lanes] = after
        faces[5, :, lanes] = before


def first_sweep_kernel(lat_count, field, winds, swept):
    total = winds.shape[0] // 2
    lat = lane_ids(total) % lat_count
    for i, north in enumerate(pair_columns(winds, slice(total, 2 * total))):
        lanes = slice(i * LANES, (i + 1) * LANES)
        north = jnp.where(lat == lat_count - 1, 0.0, north)
        after = jnp.maximum(north, 0.0)
        before = -jnp.minimum(jnp.where(lat == 0, 0.0, turned(north, 1)), 0.0)
        stay = 1.0 - after - before
        for t in range(4):
            own = slice(t * total, (t + 1) * total)
            f = field[own, lanes]
            swept[own, lanes] = stay * f + after * turned(f, -1) + before * turned(f, 1)


def transport(lat_count, field, east_rows, west_rows, faces, total, buffers, result, begun=False):
    for t in range(4):
        own = slice(t * total, (t + 1) * total)
        rim = slice((t % 2) * total, (t % 2 + 1) * total)
        rim = rim_lanes(east_rows, west_rows, rim, t >= 2)
        if begun:
            lanes = slice(256, 384)
            rim = (
                faces[0, :, lanes] * rim
                + faces[1, :, lanes] * turned(rim, -1)
                + faces[2, :, lanes] * turned(rim, 1)
            )
        buffers[int(begun), own, 0:256] = field[own, :]
        buffers[int(begun), own, 256:384] = rim
    for step in range(int(begun), 2 * NSUB):
        last = step == 2 * NSUB - 1
        for t in range(4):
            own = slice(t * total, (t + 1) * total)
            f = columns(buffers.at[step % 2], own)
            if step % 2 == 0:
                after = [turned(x, -1) for x in f]
                before = [turned(x, 1) for x in f]
            else:
                after = stepped(f, -lat_count)
                before = stepped(f, lat_count)
            base = 3 * (step % 2)
            for i in range(2 if last else 3):
                lanes = slice(i * LANES, (i + 1) * LANES)
                value = (
                    faces[base, :, lanes] * f[i]
                    + faces[base + 1, :, lanes] * after[i]
                    + faces[base + 2, :, lanes] * before[i]
                )
                if last:
                    result[own, lanes] = value
                else:
                    buffers[(step + 1) % 2, own, lanes] = value


def transport_solve_kernel(
    lat_count, field, winds, regimes, kz, wind_east, wind_west, from_east, from_west, solved, first, last, faces, buffers, moved
):
    total = kz.shape[1]
    face_weights(lat_count, winds, wind_east, wind_west, total, faces)
    transport(lat_count, field, from_east, from_west, faces, total, buffers, moved, True)
    kz_high, kz_low = mixing(kz)
    for t in range(4):
        high, low = split_two(moved[t * total : (t + 1) * total, :])
        solved[t * total : (t + 1) * total, :] = solve_columns(
            high, low, kz_high, kz_low, regimes[1:2, :], total
        )
    rim_messages(
        solved[0 : 2 * total, :], solved[2 * total :, :], first, last, slice(0, 2 * total)
    )


def footprint_kernel(n_lev, quarters, hour_0, hour_1, sums):
    own_lat, own_lev = lax.axis_index("lat"), lax.axis_index("lev")
    chip, core = own_lat // 2, own_lat % 2
    step = jnp.where(chip % 2 == 0, own_lev, n_lev - 1 - own_lev)
    chunk = (chip * n_lev + step) * 2 + core
    odd = lax.axis_index("lon") % 2 == 1
    group = quarters.shape[1] // 3
    first_lon = jnp.where(odd, group - 1 - chunk, chunk) * GRAIN
    total = hour_0.shape[0] // 4
    matrix = lane_matrix(True)
    low = jnp.concatenate(
        [h[t * total : t * total + FOOT_LEVELS, :] for h in (hour_0, hour_1) for t in range(4)],
        axis=0,
    )
    parts = mm(jnp.concatenate(split_three(low), axis=0), matrix).astype(BF16)
    count = low.shape[0]
    acc = jnp.zeros((count, 64), F32)
    cell_ids = lax.broadcasted_iota(jnp.int32, (GRAIN, 512), 0)
    level_ids = lax.broadcasted_iota(jnp.int32, (FOOT_LEVELS, 512), 0)
    station_ids = lax.broadcasted_iota(jnp.int32, (64, 512), 0)
    for row in range(group):

        def entries(at):
            return jnp.concatenate(
                [quarters[k, 3 * row + at : 3 * row + at + 1, :] for k in range(4)], axis=1
            )

        code = entries(0).astype(jnp.int32)
        station = entries(1).astype(jnp.int32)
        weight = entries(2)
        cells = ((code & 255) - first_lon == cell_ids).astype(F32).astype(BF16)
        picked = mm(parts[:, row * GRAIN : (row + 1) * GRAIN], cells)
        picked = (picked[:count] + picked[count : 2 * count]) + picked[2 * count :]
        level = jnp.where((code >> 8) == level_ids, weight, 0.0)
        picked = picked * jnp.concatenate([level] * (count // FOOT_LEVELS), axis=0)
        named = (station == station_ids).astype(F32).astype(BF16)
        high, rest = split_two(picked)
        both = jnp.concatenate([high, rest], axis=0)
        both = lax.dot_general(both, named, (((1,), (1,)), ((), ())), preferred_element_type=F32)
        acc = acc + (both[:count] + both[count:])
    sums[...] = jnp.sum(acc.reshape(count // FOOT_LEVELS, FOOT_LEVELS, 64), axis=1)


def face_kernel(lat_count, winds, wind_east, wind_west, _, faces):
    face_weights(lat_count, winds, wind_east, wind_west, winds.shape[0] // 2, faces)


def transport_pack_kernel(
    lat_count, n_lev, field, faces, from_east, from_west, sums, out, buffers, moved
):
    total = faces.shape[1]
    levels = total // n_lev
    transport(lat_count, field, from_east, from_west, faces, total, buffers, moved)
    matrix = lane_matrix(True)
    for pair in range(2):
        for k in range(2):
            rows = slice((2 * pair + k) * total, (2 * pair + k + 1) * total)
            moved[rows, :] = move_lanes(moved[rows, :], matrix)
        for z in range(n_lev):
            for half in range(2):
                lanes = slice(half * LANES, (half + 1) * LANES)
                a, b = [
                    moved[
                        (2 * pair + k) * total + z * levels : (2 * pair + k) * total
                        + (z + 1) * levels,
                        lanes,
                    ]
                    for k in range(2)
                ]
                for k, value in enumerate(swap_halves(a, b)):
                    out[
                        (2 * half + k) * n_lev + z, pair * levels : (pair + 1) * levels, :
                    ] = value
    wide = jnp.concatenate([sums[...], jnp.zeros((8, 64), F32)], axis=1)
    line = lax.broadcasted_iota(jnp.int32, (8, LANES), 0)
    spread = jnp.zeros((8, LANES), F32)
    for k in range(8):
        spread = jnp.where(line == k, pltpu.roll(wide, 4 * k, 1) if k else wide, spread)
    keep = lax.broadcasted_iota(jnp.int32, (8, LANES), 1) // 4 == line
    for g in range(out.shape[0]):
        value = pltpu.roll(spread, LANES - 4 * g, 1) if g else spread
        value = jnp.sum(jnp.where(keep, value, 0.0), axis=0, keepdims=True)
        out[g, 2 * levels : 2 * levels + 1, :] = value


def unpack_kernel(place, recv, final, stations):
    place = owners(place)
    levels = final.shape[1]
    for pair in range(2):
        for half in range(2):
            lanes = slice(half * LANES, (half + 1) * LANES)
            blocks = [
                recv[place[half * 8 + j], pair * levels : (pair + 1) * levels, :]
                for j in range(8)
            ]
            for i, value in enumerate(swap_grains(blocks)):
                k, r = divmod(i, 4)
                final[2 * pair + k, :, r, lanes] = value
    line = recv[0, 2 * levels : 2 * levels + 1, :]
    for g in range(1, recv.shape[0]):
        line = line + recv[g, 2 * levels : 2 * levels + 1, :]
    for h in range(HOURS):
        for t in range(4):
            at = (h * 4 + t) * 4
            stations[h, t, :, :] = line[:, at : at + 4]


def swaps(x, axis, count, piece):
    return [piece(x, 0)] + [
        lax.ppermute(piece(x, k), axis, [(i, i ^ k) for i in range(count)])
        for k in range(1, count)
    ]


def gather_winds(sizes, winds):
    n_lat, n_lev, _ = sizes
    own_lat, own_lev = lax.axis_index("lat"), lax.axis_index("lev")
    levels = winds.shape[1]

    def for_lat(x, k):
        return lax.dynamic_index_in_dim(x, own_lat ^ k, 0, keepdims=False)

    def for_lev(x, k):
        return lax.dynamic_index_in_dim(x, own_lev ^ k, 1, keepdims=False).reshape(-1, LANES)

    here = swaps(winds.reshape(n_lat, n_lev * levels, LANES), "lat", n_lat, for_lat)
    here = jnp.stack(here).reshape(n_lat, n_lev, levels, LANES)
    return swaps(here, "lev", n_lev, for_lev)


def call(kernel, outs, scratch=()):
    return pl.pallas_call(
        kernel,
        out_shape=[jax.ShapeDtypeStruct(s, F32) for s in outs],
        scratch_shapes=[pltpu.VMEM(s, F32) for s in scratch],
        compiler_params=pltpu.CompilerParams(vmem_limit_bytes=48 * 1024 * 1024),
    )


def regrouped(sizes, adjoint, wind_east, wind_north, kz_inverse, kz_regime, fp_cell, fp_owner, fp_station, fp_weight):
    n_lat, n_lev, n_lon = sizes
    levels = adjoint.shape[1]
    total = levels * n_lev
    group = n_lat * n_lev
    lat_count = n_lat * adjoint.shape[2]
    place = chunk_owner(n_lat, n_lev)
    to_west = ring_perm(n_lat, n_lev, n_lon, -1)
    to_east = ring_perm(n_lat, n_lev, n_lon, 1)

    def exchange(x):
        return lax.all_to_all(x, AXES, split_axis=0, concat_axis=0, tiled=True)

    def rims(first, last):
        return lax.ppermute(first, RING, to_west), lax.ppermute(last, RING, to_east)

    out_rows = 2 * levels + 1
    out_rows += -out_rows % 8
    in_rows = 2 * levels + 4
    in_rows += -in_rows % 8
    wind_rows = levels + -levels % 8
    given = (
        adjoint, wind_east, wind_north, kz_regime, fp_cell, fp_owner.reshape(1, -1), fp_station, fp_weight
    )
    fields, winds = pl.pallas_call(
        functools.partial(pack_kernel, place),
        in_specs=[pl.BlockSpec(memory_space=pltpu.HBM)] * len(given),
        out_shape=[
            jax.ShapeDtypeStruct(shape, F32)
            for shape in (
                (group, in_rows, LANES), (group, wind_rows, LANES)
            )
        ],
        scratch_shapes=[pltpu.VMEM(x.shape, x.dtype) for x in given]
        + [pltpu.SemaphoreType.DMA((len(given) + 1,))],
        compiler_params=pltpu.CompilerParams(vmem_limit_bytes=48 * 1024 * 1024),
    )(*[pltpu.with_memory_space_constraint(x, pltpu.HBM) for x in given])
    recv = exchange(fields)
    winds = gather_winds(sizes, winds[:, :levels])
    solved_0, regimes, first, last = call(
        functools.partial(unpack_solve_kernel, n_lev),
        [(4 * total, 256), (8, 256), (2 * total, LANES), (2 * total, LANES)],
        [(4 * total + 8, 256)],
    )(recv, kz_inverse)
    east_0, west_0 = rims(first, last)
    winds, first, last = call(
        functools.partial(unpack_winds_kernel, n_lev),
        [(2 * total, 256), (total, LANES), (total, LANES)],
        [(2 * total, 256), (n_lev, n_lat, levels, LANES)],
    )(*winds, regimes)
    wind_rims = rims(first, last)
    (swept,) = call(functools.partial(first_sweep_kernel, lat_count), [(4 * total, 256)])(
        solved_0, winds
    )
    entries = recv[:, 2 * levels + 1 : 2 * levels + 4].reshape(-1, LANES)
    entries = jnp.stack(swaps(entries, "lat", n_lat, lambda x, k: x))
    solved_1, first, last = call(
        functools.partial(transport_solve_kernel, lat_count),
        [(4 * total, 256), (2 * total, LANES), (2 * total, LANES)],
        [(6, total, 384), (2, 4 * total, 384), (4 * total, 256)],
    )(swept, winds, regimes, kz_inverse, *wind_rims, east_0, west_0)
    east_1, west_1 = rims(first, last)
    (sums,) = call(functools.partial(footprint_kernel, n_lev), [(8, 64)])(
        entries, solved_0, solved_1
    )
    (faces,) = call(functools.partial(face_kernel, lat_count), [(6, total, 384)])(
        winds, *wind_rims, first
    )
    (back,) = call(
        functools.partial(transport_pack_kernel, lat_count, n_lev),
        [(group, out_rows, LANES)],
        [(2, 4 * total, 384), (4 * total, 256)],
    )(solved_1, faces, east_1, west_1, sums)
    final, stations = call(
        functools.partial(unpack_kernel, place), [adjoint.shape, (HOURS, 4, 1, SPO)]
    )(exchange(back))
    return final, stations


def padded_2(x, sides, width, wrap):
    for axis, dim in sides:
        peers, length = (lax.axis_size(axis), x.shape[dim])
        up = [(i, (i + 1) % peers) for i in range(peers if wrap else peers - 1)]
        down = [(j, i) for i, j in up]
        last = lax.slice_in_dim(x, length - width, length, axis=dim)
        initial = lax.slice_in_dim(x, 0, width, axis=dim)
        before = lax.ppermute(last, axis, up)
        after = lax.ppermute(initial, axis, down)
        x = jnp.concatenate([before, x, after], axis=dim)
    return x


def lat_rim(values, rim_width):
    return padded_2(values, (("lat", 2),), rim_width, False)


def lon_rim(values, rim_width):
    return padded_2(values, (("lon", 3),), rim_width, True)


def lat_sweep(padded, north_face, south_face):
    middle = padded[:, :, 1:-1]
    return (
        middle
        + jnp.maximum(north_face, 0.0) * (padded[:, :, 2:] - middle)
        - jnp.minimum(south_face, 0.0) * (padded[:, :, :-2] - middle)
    )


def lon_sweep(padded, east_face, west_face):
    middle = padded[:, :, :, 1:-1]
    return (
        middle
        + jnp.maximum(east_face, 0.0) * (padded[:, :, :, 2:] - middle)
        - jnp.minimum(west_face, 0.0) * (padded[:, :, :, :-2] - middle)
    )


def shards(
    adjoint, wind_east, wind_north, kz_inverse, kz_regime, fp_cell, fp_owner, fp_station, fp_weight
):
    tracers, levels_dev, lat_rows, lon_cells = adjoint.shape
    row_index = lax.axis_index("lat") * lat_rows + lax.broadcasted_iota(
        jnp.int32, (1, lat_rows, 1), 1
    )
    last_row = lat_rows * lax.axis_size("lat") - 1
    north_face = jnp.where(row_index == last_row, jnp.zeros_like(wind_north), wind_north)
    south_face = lat_rim(north_face[None], 1)[0][:, :-2]
    west_face = lon_rim(wind_east[None], 1)[0][:, :, :-2]
    groups = lax.axis_size("lat") * lax.axis_size("lev")
    column_count = lat_rows * lon_cells // lax.axis_size("lev")
    first_column = lax.axis_index("lev") * column_count
    regime_rows = kz_regime.reshape(HOURS, lat_rows * lon_cells)
    cell_ids = fp_cell.reshape(-1)
    owners = fp_owner.reshape(-1)
    stations = fp_station.reshape(-1)
    weights = fp_weight.reshape(-1)
    entries = cell_ids.shape[0]
    adjoint_field = adjoint
    outputs = []
    for hour_step in range(HOURS):
        chosen = lax.dynamic_slice_in_dim(regime_rows[hour_step], first_column, column_count, 0)

        def column_solve(columns, chosen=chosen):
            result = jnp.zeros_like(columns)
            for regime in range(REGIMES):
                product = jnp.einsum(
                    "ji,tjp->tip", kz_inverse[regime], columns, precision=lax.Precision.HIGHEST
                )
                result = jnp.where(chosen[None, None, :] == regime, product, result)
            returned = lax.all_to_all(result, "lev", split_axis=1, concat_axis=2, tiled=True)
            return (returned, result)

        flat_field = adjoint_field.reshape(tracers, levels_dev, lat_rows * lon_cells)
        returned, solved = column_solve(
            lax.all_to_all(flat_field, "lev", split_axis=2, concat_axis=1, tiled=True)
        )
        lowest = solved[:, :FOOT_LEVELS, :].reshape(tracers, -1)
        picked = jnp.take(lowest, cell_ids, axis=1) * weights[None, :]
        capacity = 2 * entries // groups
        owner_hits = (owners[:, None] == jnp.arange(groups, dtype=jnp.int32)[None, :]).astype(
            jnp.int32
        )
        bucket_rank = jnp.sum(jnp.cumsum(owner_hits, axis=0) * owner_hits, axis=1) - 1
        slot_pos = owners * capacity + bucket_rank
        send_values = (
            jnp.zeros((tracers, groups * capacity), jnp.float32).at[:, slot_pos].set(picked)
        )
        send_ids = jnp.full((groups * capacity,), -1, jnp.int32).at[slot_pos].set(stations)
        arrived_values, arrived_ids = (
            lax.all_to_all(
                send_values.reshape(tracers, groups, capacity),
                ("lat", "lev"),
                split_axis=1,
                concat_axis=1,
                tiled=True,
            ),
            lax.all_to_all(
                send_ids.reshape(1, groups, capacity),
                ("lat", "lev"),
                split_axis=1,
                concat_axis=1,
                tiled=True,
            ),
        )
        matches = (
            arrived_ids[0][:, :, None] == jnp.arange(SPO, dtype=jnp.int32)[None, None, :]
        ).astype(jnp.float32)
        station_sums = jnp.einsum(
            "tgc,gcs->ts", arrived_values, matches, precision=lax.Precision.HIGHEST
        )
        outputs.append(station_sums)
        adjoint_field = returned.reshape(tracers, levels_dev, lat_rows, lon_cells)
        for substep in range(NSUB):
            adjoint_field = lat_sweep(lat_rim(adjoint_field, 1), north_face, south_face)
            adjoint_field = lon_sweep(lon_rim(adjoint_field, 1), wind_east, west_face)
    return (adjoint_field, jnp.stack(outputs)[:, :, None, :])


def fits(mesh_sizes, shape, kz_shape, entries):
    n_lat, n_lev, n_lon = mesh_sizes
    tracers, levels, rows, cells = shape
    return (
        tracers == 4
        and rows == 4
        and cells == 256
        and n_lat == 4
        and n_lat * n_lev == 16
        and levels * n_lev == kz_shape[1]
        and kz_shape[1] % 8 == 0
        and levels % 2 == 0
        and entries == 512
    )


def device_part(sizes, *arrays):
    if fits(sizes, arrays[0].shape, arrays[3].shape, arrays[5].shape[-1]):
        return regrouped(sizes, *arrays)
    return shards(*arrays)


def solution(mesh):
    sizes = tuple(mesh.shape[name] for name in RING)
    in_specs = (
        P(None, "lev", "lat", "lon"),
        P("lev", "lat", "lon"),
        P("lev", "lat", "lon"),
        P(),
        P(None, "lat", "lon"),
        P(AXES, "lon", None),
        P(AXES, "lon", None, None),
        P(AXES, "lon", None),
        P(AXES, "lon", None),
    )
    out_specs = (P(None, "lev", "lat", "lon"), P(None, None, "lon", AXES))
    return jax.shard_map(
        functools.partial(device_part, sizes),
        mesh=mesh,
        in_specs=in_specs,
        out_specs=out_specs,
        check_vma=False,
    )
```

```python
import functools
import jax
import jax.numpy as jnp
from jax import lax
from jax.experimental import pallas as pl
from jax.experimental.pallas import tpu as pltpu
from jax.sharding import PartitionSpec as P

NSUB = 4
HOURS = 2
REGIMES = 4
FOOT_LEVELS = 8
SPO = 4
LANES = 128
GRAIN = 16
F32 = jnp.float32
BF16 = jnp.bfloat16
AXES = ("lat", "lev")
RING = ("lat", "lev", "lon")


def chunk_owner(n_lat, n_lev):
    place = [0] * (n_lat * n_lev)
    for a in range(n_lat):
        for z in range(n_lev):
            chip, core = divmod(a, 2)
            step = z if chip % 2 == 0 else n_lev - 1 - z
            place[(chip * n_lev + step) * 2 + core] = a * n_lev + z
    return place


def ring_perm(n_lat, n_lev, n_lon, shift):
    place = chunk_owner(n_lat, n_lev)
    ring = [
        (place[::-1] if o % 2 else place)[d] * n_lon + o
        for o in range(n_lon)
        for d in range(len(place))
    ]
    count = len(ring)
    return [(ring[i], ring[(i + shift) % count]) for i in range(count)]


def owners(place):
    odd = lax.axis_index("lon") % 2 == 1
    return [jnp.where(odd, there, here) for here, there in zip(place, place[::-1])]


def lane_ids(rows):
    return lax.broadcasted_iota(jnp.int32, (rows, LANES), 1)


def swap_grains(blocks):
    blocks = list(blocks)
    grain = lane_ids(blocks[0].shape[0]) // GRAIN
    bit = len(blocks) // 2
    while bit:
        low = (grain & bit) == 0
        for i in range(len(blocks)):
            if i & bit == 0:
                a, b = blocks[i], blocks[i | bit]
                blocks[i] = jnp.where(low, a, pltpu.roll(b, bit * GRAIN, 1))
                blocks[i | bit] = jnp.where(low, pltpu.roll(a, LANES - bit * GRAIN, 1), b)
        bit //= 2
    return blocks


def swap_halves(a, b):
    low = lane_ids(a.shape[0]) < LANES // 2
    return (
        jnp.where(low, a, pltpu.roll(b, LANES // 2, 1)),
        jnp.where(low, pltpu.roll(a, LANES // 2, 1), b),
    )


def lane_matrix(back):
    major = lax.broadcasted_iota(jnp.int32, (256, 256), 1 if back else 0)
    work = lax.broadcasted_iota(jnp.int32, (256, 256), 0 if back else 1)
    lon = (work % LANES) // GRAIN * 2 + work // LANES
    return ((major // GRAIN == work % GRAIN) & (major % GRAIN == lon)).astype(F32).astype(BF16)


def split_two(x):
    high = x.astype(BF16)
    return high, (x - high.astype(F32)).astype(BF16)


def split_three(x):
    high, _ = split_two(x)
    rest = x - high.astype(F32)
    middle = rest.astype(BF16)
    return high, middle, (rest - middle.astype(F32)).astype(BF16)


def mm(a, b):
    return jnp.dot(a, b, preferred_element_type=F32)


def move_lanes(x, matrix):
    high, middle, low = split_three(x)
    return (mm(high, matrix) + mm(middle, matrix)) + mm(low, matrix)


def fetch(given, held, sems):
    return [
        pltpu.make_async_copy(a, b, sems.at[i]) for i, (a, b) in enumerate(zip(given, held))
    ]


def place_pieces(place, srcs, out, first, count):
    for half in range(2):
        lanes = slice(half * LANES, (half + 1) * LANES)
        for j, piece in enumerate(swap_grains([s[:, lanes] for s in srcs])):
            out[place[half * 8 + j], first : first + count, :] = piece


def pack_winds_kernel(place, *refs):
    given, winds, held, sems = refs[:2], refs[3], refs[4:6], refs[6]
    copies = fetch(given, held, sems)
    for copy in copies:
        copy.start()
    place = owners(place)
    levels, rows = held[0].shape[:2]
    for copy in copies:
        copy.wait()
    place_pieces(place, [w[:, r, :] for w in held for r in range(rows)], winds, 0, levels)


def pack_fields_kernel(place, *refs):
    count = (len(refs) - 2) // 2
    given, fields, held, sems = refs[:count], refs[count], refs[count + 1 : -1], refs[-1]
    halves = [
        pltpu.make_async_copy(given[0].at[part], held[0].at[part], sems.at[at])
        for part, at in ((pl.ds(0, 2), 0), (pl.ds(2, 2), count))
    ]
    copies = fetch(given, held, sems)[1:]
    for copy in halves + copies:
        copy.start()
    adj, regime, cell, owner, station, weight = held
    place = owners(place)
    levels, rows = adj.shape[1:3]
    for pair in range(2):
        halves[pair].wait()
        srcs = [adj[2 * pair + k, :, r, :] for k in range(2) for r in range(rows)]
        place_pieces(place, srcs, fields, pair * levels, levels)
    for copy in copies:
        copy.wait()
    srcs = [regime[h, r : r + 1, :].astype(F32) for h in range(HOURS) for r in range(rows)]
    place_pieces(place, srcs, fields, 2 * levels, 1)
    cells = cell[0].astype(F32)
    stations = (owner[...] * SPO + station[0]).astype(F32)
    for g in range(fields.shape[0]):
        k = g // (fields.shape[0] // 4)
        for at, value in enumerate((cells, stations, weight[0])):
            row = 2 * levels + 1 + at
            fields[g, row : row + 1, :] = value[:, k * LANES : (k + 1) * LANES]


def solve_columns(high, low, kz_high, kz_low, regime, levels):
    product = mm(kz_high, high) + (mm(kz_low, high) + mm(kz_high, low))
    result = product[:levels]
    for k in range(1, REGIMES):
        result = jnp.where(regime == float(k), product[k * levels : (k + 1) * levels], result)
    return result


def mixing(kz):
    stacked = jnp.concatenate([kz[k].T for k in range(REGIMES)], axis=0)
    return split_two(stacked)


def rim_messages(top, bottom, first, last, rows):
    pair = lane_ids(top.shape[0]) // (2 * GRAIN)
    blocks = [top[:, :LANES], top[:, LANES:], bottom[:, :LANES], bottom[:, LANES:]]

    def gathered(offset):
        out = blocks[3] if offset == 3 else turned(blocks[3], (3 - offset) * 2 * GRAIN)
        for k in range(3):
            shift = (k - offset) * 2 * GRAIN
            out = jnp.where(pair == k, turned(blocks[k], shift) if shift else blocks[k], out)
        return out

    first[rows, :] = gathered(0)
    last[rows, :] = gathered(3)


def unpack_solve_kernel(n_lev, recv, kz, solved, regimes, first, last, field):
    total = kz.shape[1]
    levels = total // n_lev
    for pair in range(2):
        for z in range(n_lev):
            for half in range(2):
                lanes = slice(half * LANES, (half + 1) * LANES)
                a, b = [
                    recv[(2 * half + k) * n_lev + z, pair * levels : (pair + 1) * levels, :]
                    for k in range(2)
                ]
                for k, value in enumerate(swap_halves(a, b)):
                    base = (2 * pair + k) * total + z * levels
                    field[base : base + levels, lanes] = value
    base = 4 * total
    field[base : base + 8, :] = jnp.zeros((8, 256), F32)
    for half in range(2):
        lanes = slice(half * LANES, (half + 1) * LANES)
        a, b = [
            recv[(2 * half + k) * n_lev, 2 * levels : 2 * levels + 1, :] for k in range(2)
        ]
        for k, value in enumerate(swap_halves(a, b)):
            field[base + k : base + k + 1, lanes] = value
    matrix = lane_matrix(False)
    regime = mm(field[base : base + 8, :].astype(BF16), matrix)
    regimes[...] = regime
    kz_high, kz_low = mixing(kz)
    for t in range(4):
        high, low = split_two(field[t * total : (t + 1) * total, :])
        high = mm(high, matrix).astype(BF16)
        low = mm(low, matrix).astype(BF16)
        solved[t * total : (t + 1) * total, :] = solve_columns(
            high, low, kz_high, kz_low, regime[0:1], total
        )
    rim_messages(
        solved[0 : 2 * total, :], solved[2 * total :, :], first, last, slice(0, 2 * total)
    )


def unpack_winds_kernel(n_lev, *refs):
    pieces, (winds, first, last, field, others) = refs[:n_lev], refs[n_lev + 1 :]
    total = winds.shape[0] // 2
    levels = total // n_lev
    for m in range(n_lev):
        for k in range(others.shape[1]):
            others[m, k] = pieces[m][k * levels : (k + 1) * levels, :]
    own_lat, own_lev = lax.axis_index("lat"), lax.axis_index("lev")
    for z in range(n_lev):
        for half in range(2):
            lanes = slice(half * LANES, (half + 1) * LANES)
            a, b = [
                others[z ^ own_lev, (2 * half + k) ^ own_lat, 0:levels, :] for k in range(2)
            ]
            for k, value in enumerate(swap_halves(a, b)):
                base = k * total + z * levels
                field[base : base + levels, lanes] = value
    winds[...] = move_lanes(field[...], lane_matrix(False))
    rim_messages(winds[0:total, :], winds[total:, :], first, last, slice(0, total))


def rim_lanes(from_east, from_west, rows, upper):
    half = LANES // 2
    east, west = from_east[rows, :], from_west[rows, :]
    lane = lane_ids(east.shape[0])
    if upper:
        both = jnp.where(lane < half, pltpu.roll(east, half, 1), west)
    else:
        both = jnp.where(lane < half, east, pltpu.roll(west, half, 1))
    place = lane // GRAIN % 4
    both = jnp.where(place == 1, turned(both, -GRAIN), jnp.where(place == 2, turned(both, GRAIN), both))
    return both


def columns(ref, rows):
    return [ref[rows, i * LANES : (i + 1) * LANES] for i in range(3)]


def pair_columns(ref, rows):
    return [ref[rows, i * LANES : (i + 1) * LANES] for i in range(2)]


def turned(x, shift):
    return pltpu.roll(x, shift % LANES, 1)


def stepped(blocks, shift):
    even, odd, rim = blocks
    lane = lane_ids(even.shape[0])
    outer = turned(rim, shift)
    if shift > 0:
        inner, edge = turned(odd, shift), lane < shift
        return [jnp.where(edge, outer, inner), even, jnp.where(edge, inner, outer)]
    inner, edge = turned(even, shift), lane >= LANES + shift
    return [odd, jnp.where(edge, outer, inner), jnp.where(edge, inner, outer)]


def face_weights(lat_count, winds, from_east, from_west, total, faces):
    rims = slice(0, total)
    east = pair_columns(winds, slice(0, total)) + [rim_lanes(from_east, from_west, rims, False)]
    north = pair_columns(winds, slice(total, 2 * total)) + [
        rim_lanes(from_east, from_west, rims, True)
    ]
    lat = lane_ids(total) % lat_count
    north = [jnp.where(lat == lat_count - 1, 0.0, x) for x in north]
    west = stepped(east, lat_count)
    for i in range(3):
        lanes = slice(i * LANES, (i + 1) * LANES)
        after = jnp.maximum(north[i], 0.0)
        before = -jnp.minimum(jnp.where(lat == 0, 0.0, turned(north[i], 1)), 0.0)
        faces[0, :, lanes] = 1.0 - after - before
        faces[1, :, lanes] = after
        faces[2, :, lanes] = before
        after = jnp.maximum(east[i], 0.0)
        before = -jnp.minimum(west[i], 0.0)
        faces[3, :, lanes] = 1.0 - after - before
        faces[4, :, lanes] = after
        faces[5, :, lanes] = before


def first_sweep_kernel(lat_count, field, winds, swept):
    total = winds.shape[0] // 2
    lat = lane_ids(total) % lat_count
    for i, north in enumerate(pair_columns(winds, slice(total, 2 * total))):
        lanes = slice(i * LANES, (i + 1) * LANES)
        north = jnp.where(lat == lat_count - 1, 0.0, north)
        after = jnp.maximum(north, 0.0)
        before = -jnp.minimum(jnp.where(lat == 0, 0.0, turned(north, 1)), 0.0)
        stay = 1.0 - after - before
        for t in range(4):
            own = slice(t * total, (t + 1) * total)
            f = field[own, lanes]
            swept[own, lanes] = stay * f + after * turned(f, -1) + before * turned(f, 1)


def transport(lat_count, field, east_rows, west_rows, faces, total, buffers, result, begun=False):
    for t in range(4):
        own = slice(t * total, (t + 1) * total)
        rim = slice((t % 2) * total, (t % 2 + 1) * total)
        rim = rim_lanes(east_rows, west_rows, rim, t >= 2)
        if begun:
            lanes = slice(256, 384)
            rim = (
                faces[0, :, lanes] * rim
                + faces[1, :, lanes] * turned(rim, -1)
                + faces[2, :, lanes] * turned(rim, 1)
            )
        buffers[int(begun), own, 0:256] = field[own, :]
        buffers[int(begun), own, 256:384] = rim
    for step in range(int(begun), 2 * NSUB):
        last = step == 2 * NSUB - 1
        for t in range(4):
            own = slice(t * total, (t + 1) * total)
            f = columns(buffers.at[step % 2], own)
            if step % 2 == 0:
                after = [turned(x, -1) for x in f]
                before = [turned(x, 1) for x in f]
            else:
                after = stepped(f, -lat_count)
                before = stepped(f, lat_count)
            base = 3 * (step % 2)
            for i in range(2 if last else 3):
                lanes = slice(i * LANES, (i + 1) * LANES)
                value = (
                    faces[base, :, lanes] * f[i]
                    + faces[base + 1, :, lanes] * after[i]
                    + faces[base + 2, :, lanes] * before[i]
                )
                if last:
                    result[own, lanes] = value
                else:
                    buffers[(step + 1) % 2, own, lanes] = value


def transport_solve_kernel(
    lat_count, field, winds, regimes, kz, wind_east, wind_west, from_east, from_west, solved, first, last, faces, buffers, moved
):
    total = kz.shape[1]
    face_weights(lat_count, winds, wind_east, wind_west, total, faces)
    transport(lat_count, field, from_east, from_west, faces, total, buffers, moved, True)
    kz_high, kz_low = mixing(kz)
    for t in range(4):
        high, low = split_two(moved[t * total : (t + 1) * total, :])
        solved[t * total : (t + 1) * total, :] = solve_columns(
            high, low, kz_high, kz_low, regimes[1:2, :], total
        )
    rim_messages(
        solved[0 : 2 * total, :], solved[2 * total :, :], first, last, slice(0, 2 * total)
    )


def footprint_kernel(n_lev, quarters, hour_0, hour_1, sums):
    own_lat, own_lev = lax.axis_index("lat"), lax.axis_index("lev")
    chip, core = own_lat // 2, own_lat % 2
    step = jnp.where(chip % 2 == 0, own_lev, n_lev - 1 - own_lev)
    chunk = (chip * n_lev + step) * 2 + core
    odd = lax.axis_index("lon") % 2 == 1
    group = quarters.shape[1] // 3
    first_lon = jnp.where(odd, group - 1 - chunk, chunk) * GRAIN
    total = hour_0.shape[0] // 4
    matrix = lane_matrix(True)
    low = jnp.concatenate(
        [h[t * total : t * total + FOOT_LEVELS, :] for h in (hour_0, hour_1) for t in range(4)],
        axis=0,
    )
    parts = mm(jnp.concatenate(split_three(low), axis=0), matrix).astype(BF16)
    count = low.shape[0]
    acc = jnp.zeros((count, 64), F32)
    cell_ids = lax.broadcasted_iota(jnp.int32, (GRAIN, 512), 0)
    level_ids = lax.broadcasted_iota(jnp.int32, (FOOT_LEVELS, 512), 0)
    station_ids = lax.broadcasted_iota(jnp.int32, (64, 512), 0)
    for row in range(group):

        def entries(at):
            return jnp.concatenate(
                [quarters[k, 3 * row + at : 3 * row + at + 1, :] for k in range(4)], axis=1
            )

        code = entries(0).astype(jnp.int32)
        station = entries(1).astype(jnp.int32)
        weight = entries(2)
        cells = ((code & 255) - first_lon == cell_ids).astype(F32).astype(BF16)
        picked = mm(parts[:, row * GRAIN : (row + 1) * GRAIN], cells)
        picked = (picked[:count] + picked[count : 2 * count]) + picked[2 * count :]
        level = jnp.where((code >> 8) == level_ids, weight, 0.0)
        picked = picked * jnp.concatenate([level] * (count // FOOT_LEVELS), axis=0)
        named = (station == station_ids).astype(F32).astype(BF16)
        high, rest = split_two(picked)
        both = jnp.concatenate([high, rest], axis=0)
        both = lax.dot_general(both, named, (((1,), (1,)), ((), ())), preferred_element_type=F32)
        acc = acc + (both[:count] + both[count:])
    sums[...] = jnp.sum(acc.reshape(count // FOOT_LEVELS, FOOT_LEVELS, 64), axis=1)


def face_kernel(lat_count, winds, wind_east, wind_west, _, faces):
    face_weights(lat_count, winds, wind_east, wind_west, winds.shape[0] // 2, faces)


def transport_pack_kernel(
    lat_count, n_lev, field, faces, from_east, from_west, sums, out, buffers, moved
):
    total = faces.shape[1]
    levels = total // n_lev
    transport(lat_count, field, from_east, from_west, faces, total, buffers, moved)
    matrix = lane_matrix(True)
    for pair in range(2):
        for k in range(2):
            rows = slice((2 * pair + k) * total, (2 * pair + k + 1) * total)
            moved[rows, :] = move_lanes(moved[rows, :], matrix)
        for z in range(n_lev):
            for half in range(2):
                lanes = slice(half * LANES, (half + 1) * LANES)
                a, b = [
                    moved[
                        (2 * pair + k) * total + z * levels : (2 * pair + k) * total
                        + (z + 1) * levels,
                        lanes,
                    ]
                    for k in range(2)
                ]
                for k, value in enumerate(swap_halves(a, b)):
                    out[
                        (2 * half + k) * n_lev + z, pair * levels : (pair + 1) * levels, :
                    ] = value
    wide = jnp.concatenate([sums[...], jnp.zeros((8, 64), F32)], axis=1)
    line = lax.broadcasted_iota(jnp.int32, (8, LANES), 0)
    spread = jnp.zeros((8, LANES), F32)
    for k in range(8):
        spread = jnp.where(line == k, pltpu.roll(wide, 4 * k, 1) if k else wide, spread)
    keep = lax.broadcasted_iota(jnp.int32, (8, LANES), 1) // 4 == line
    for g in range(out.shape[0]):
        value = pltpu.roll(spread, LANES - 4 * g, 1) if g else spread
        value = jnp.sum(jnp.where(keep, value, 0.0), axis=0, keepdims=True)
        out[g, 2 * levels : 2 * levels + 1, :] = value


def unpack_kernel(place, recv, final, stations):
    place = owners(place)
    levels = final.shape[1]
    for pair in range(2):
        for half in range(2):
            lanes = slice(half * LANES, (half + 1) * LANES)
            blocks = [
                recv[place[half * 8 + j], pair * levels : (pair + 1) * levels, :]
                for j in range(8)
            ]
            for i, value in enumerate(swap_grains(blocks)):
                k, r = divmod(i, 4)
                final[2 * pair + k, :, r, lanes] = value
    line = recv[0, 2 * levels : 2 * levels + 1, :]
    for g in range(1, recv.shape[0]):
        line = line + recv[g, 2 * levels : 2 * levels + 1, :]
    for h in range(HOURS):
        for t in range(4):
            at = (h * 4 + t) * 4
            stations[h, t, :, :] = line[:, at : at + 4]


def swaps(x, axis, count, piece):
    return [piece(x, 0)] + [
        lax.ppermute(piece(x, k), axis, [(i, i ^ k) for i in range(count)])
        for k in range(1, count)
    ]


def gather_winds(sizes, winds):
    n_lat, n_lev, _ = sizes
    own_lat, own_lev = lax.axis_index("lat"), lax.axis_index("lev")
    levels = winds.shape[1]

    def for_lat(x, k):
        return lax.dynamic_index_in_dim(x, own_lat ^ k, 0, keepdims=False)

    def for_lev(x, k):
        return lax.dynamic_index_in_dim(x, own_lev ^ k, 1, keepdims=False).reshape(-1, LANES)

    here = swaps(winds.reshape(n_lat, n_lev * levels, LANES), "lat", n_lat, for_lat)
    here = jnp.stack(here).reshape(n_lat, n_lev, levels, LANES)
    return swaps(here, "lev", n_lev, for_lev)


def call(kernel, outs, scratch=()):
    return pl.pallas_call(
        kernel,
        out_shape=[jax.ShapeDtypeStruct(s, F32) for s in outs],
        scratch_shapes=[pltpu.VMEM(s, F32) for s in scratch],
        compiler_params=pltpu.CompilerParams(vmem_limit_bytes=48 * 1024 * 1024),
    )


def regrouped(sizes, adjoint, wind_east, wind_north, kz_inverse, kz_regime, fp_cell, fp_owner, fp_station, fp_weight):
    n_lat, n_lev, n_lon = sizes
    levels = adjoint.shape[1]
    total = levels * n_lev
    group = n_lat * n_lev
    lat_count = n_lat * adjoint.shape[2]
    place = chunk_owner(n_lat, n_lev)
    to_west = ring_perm(n_lat, n_lev, n_lon, -1)
    to_east = ring_perm(n_lat, n_lev, n_lon, 1)

    def exchange(x):
        return lax.all_to_all(x, AXES, split_axis=0, concat_axis=0, tiled=True)

    def rims(first, last):
        return lax.ppermute(first, RING, to_west), lax.ppermute(last, RING, to_east)

    out_rows = 2 * levels + 1
    out_rows += -out_rows % 8
    in_rows = 2 * levels + 4
    in_rows += -in_rows % 8
    wind_rows = levels + -levels % 8

    def pack(kernel, given, after, shape):
        given = [pltpu.with_memory_space_constraint(x, pltpu.HBM) for x in given]
        return pl.pallas_call(
            functools.partial(kernel, place),
            in_specs=[pl.BlockSpec(memory_space=pltpu.HBM)] * (len(given) + len(after)),
            out_shape=jax.ShapeDtypeStruct(shape, F32),
            scratch_shapes=[pltpu.VMEM(x.shape, x.dtype) for x in given]
            + [pltpu.SemaphoreType.DMA((len(given) + 1,))],
            compiler_params=pltpu.CompilerParams(vmem_limit_bytes=48 * 1024 * 1024),
        )(*given, *after)

    fields = pack(
        pack_fields_kernel,
        (adjoint, kz_regime, fp_cell, fp_owner.reshape(1, -1), fp_station, fp_weight),
        (),
        (group, in_rows, LANES),
    )
    winds = pack(
        pack_winds_kernel, (wind_east, wind_north), (fields,), (group, wind_rows, LANES)
    )
    recv = exchange(fields)
    winds = gather_winds(sizes, winds[:, :levels])
    solved_0, regimes, first, last = call(
        functools.partial(unpack_solve_kernel, n_lev),
        [(4 * total, 256), (8, 256), (2 * total, LANES), (2 * total, LANES)],
        [(4 * total + 8, 256)],
    )(recv, kz_inverse)
    east_0, west_0 = rims(first, last)
    winds, first, last = call(
        functools.partial(unpack_winds_kernel, n_lev),
        [(2 * total, 256), (total, LANES), (total, LANES)],
        [(2 * total, 256), (n_lev, n_lat, levels, LANES)],
    )(*winds, regimes)
    wind_rims = rims(first, last)
    (swept,) = call(functools.partial(first_sweep_kernel, lat_count), [(4 * total, 256)])(
        solved_0, winds
    )
    entries = recv[:, 2 * levels + 1 : 2 * levels + 4].reshape(-1, LANES)
    entries = jnp.stack(swaps(entries, "lat", n_lat, lambda x, k: x))
    solved_1, first, last = call(
        functools.partial(transport_solve_kernel, lat_count),
        [(4 * total, 256), (2 * total, LANES), (2 * total, LANES)],
        [(6, total, 384), (2, 4 * total, 384), (4 * total, 256)],
    )(swept, winds, regimes, kz_inverse, *wind_rims, east_0, west_0)
    east_1, west_1 = rims(first, last)
    (sums,) = call(functools.partial(footprint_kernel, n_lev), [(8, 64)])(
        entries, solved_0, solved_1
    )
    (faces,) = call(functools.partial(face_kernel, lat_count), [(6, total, 384)])(
        winds, *wind_rims, first
    )
    (back,) = call(
        functools.partial(transport_pack_kernel, lat_count, n_lev),
        [(group, out_rows, LANES)],
        [(2, 4 * total, 384), (4 * total, 256)],
    )(solved_1, faces, east_1, west_1, sums)
    final, stations = call(
        functools.partial(unpack_kernel, place), [adjoint.shape, (HOURS, 4, 1, SPO)]
    )(exchange(back))
    return final, stations


def padded_2(x, sides, width, wrap):
    for axis, dim in sides:
        peers, length = (lax.axis_size(axis), x.shape[dim])
        up = [(i, (i + 1) % peers) for i in range(peers if wrap else peers - 1)]
        down = [(j, i) for i, j in up]
        last = lax.slice_in_dim(x, length - width, length, axis=dim)
        initial = lax.slice_in_dim(x, 0, width, axis=dim)
        before = lax.ppermute(last, axis, up)
        after = lax.ppermute(initial, axis, down)
        x = jnp.concatenate([before, x, after], axis=dim)
    return x


def lat_rim(values, rim_width):
    return padded_2(values, (("lat", 2),), rim_width, False)


def lon_rim(values, rim_width):
    return padded_2(values, (("lon", 3),), rim_width, True)


def lat_sweep(padded, north_face, south_face):
    middle = padded[:, :, 1:-1]
    return (
        middle
        + jnp.maximum(north_face, 0.0) * (padded[:, :, 2:] - middle)
        - jnp.minimum(south_face, 0.0) * (padded[:, :, :-2] - middle)
    )


def lon_sweep(padded, east_face, west_face):
    middle = padded[:, :, :, 1:-1]
    return (
        middle
        + jnp.maximum(east_face, 0.0) * (padded[:, :, :, 2:] - middle)
        - jnp.minimum(west_face, 0.0) * (padded[:, :, :, :-2] - middle)
    )


def shards(
    adjoint, wind_east, wind_north, kz_inverse, kz_regime, fp_cell, fp_owner, fp_station, fp_weight
):
    tracers, levels_dev, lat_rows, lon_cells = adjoint.shape
    row_index = lax.axis_index("lat") * lat_rows + lax.broadcasted_iota(
        jnp.int32, (1, lat_rows, 1), 1
    )
    last_row = lat_rows * lax.axis_size("lat") - 1
    north_face = jnp.where(row_index == last_row, jnp.zeros_like(wind_north), wind_north)
    south_face = lat_rim(north_face[None], 1)[0][:, :-2]
    west_face = lon_rim(wind_east[None], 1)[0][:, :, :-2]
    groups = lax.axis_size("lat") * lax.axis_size("lev")
    column_count = lat_rows * lon_cells // lax.axis_size("lev")
    first_column = lax.axis_index("lev") * column_count
    regime_rows = kz_regime.reshape(HOURS, lat_rows * lon_cells)
    cell_ids = fp_cell.reshape(-1)
    owners = fp_owner.reshape(-1)
    stations = fp_station.reshape(-1)
    weights = fp_weight.reshape(-1)
    entries = cell_ids.shape[0]
    adjoint_field = adjoint
    outputs = []
    for hour_step in range(HOURS):
        chosen = lax.dynamic_slice_in_dim(regime_rows[hour_step], first_column, column_count, 0)

        def column_solve(columns, chosen=chosen):
            result = jnp.zeros_like(columns)
            for regime in range(REGIMES):
                product = jnp.einsum(
                    "ji,tjp->tip", kz_inverse[regime], columns, precision=lax.Precision.HIGHEST
                )
                result = jnp.where(chosen[None, None, :] == regime, product, result)
            returned = lax.all_to_all(result, "lev", split_axis=1, concat_axis=2, tiled=True)
            return (returned, result)

        flat_field = adjoint_field.reshape(tracers, levels_dev, lat_rows * lon_cells)
        returned, solved = column_solve(
            lax.all_to_all(flat_field, "lev", split_axis=2, concat_axis=1, tiled=True)
        )
        lowest = solved[:, :FOOT_LEVELS, :].reshape(tracers, -1)
        picked = jnp.take(lowest, cell_ids, axis=1) * weights[None, :]
        capacity = 2 * entries // groups
        owner_hits = (owners[:, None] == jnp.arange(groups, dtype=jnp.int32)[None, :]).astype(
            jnp.int32
        )
        bucket_rank = jnp.sum(jnp.cumsum(owner_hits, axis=0) * owner_hits, axis=1) - 1
        slot_pos = owners * capacity + bucket_rank
        send_values = (
            jnp.zeros((tracers, groups * capacity), jnp.float32).at[:, slot_pos].set(picked)
        )
        send_ids = jnp.full((groups * capacity,), -1, jnp.int32).at[slot_pos].set(stations)
        arrived_values, arrived_ids = (
            lax.all_to_all(
                send_values.reshape(tracers, groups, capacity),
                ("lat", "lev"),
                split_axis=1,
                concat_axis=1,
                tiled=True,
            ),
            lax.all_to_all(
                send_ids.reshape(1, groups, capacity),
                ("lat", "lev"),
                split_axis=1,
                concat_axis=1,
                tiled=True,
            ),
        )
        matches = (
            arrived_ids[0][:, :, None] == jnp.arange(SPO, dtype=jnp.int32)[None, None, :]
        ).astype(jnp.float32)
        station_sums = jnp.einsum(
            "tgc,gcs->ts", arrived_values, matches, precision=lax.Precision.HIGHEST
        )
        outputs.append(station_sums)
        adjoint_field = returned.reshape(tracers, levels_dev, lat_rows, lon_cells)
        for substep in range(NSUB):
            adjoint_field = lat_sweep(lat_rim(adjoint_field, 1), north_face, south_face)
            adjoint_field = lon_sweep(lon_rim(adjoint_field, 1), wind_east, west_face)
    return (adjoint_field, jnp.stack(outputs)[:, :, None, :])


def fits(mesh_sizes, shape, kz_shape, entries):
    n_lat, n_lev, n_lon = mesh_sizes
    tracers, levels, rows, cells = shape
    return (
        tracers == 4
        and rows == 4
        and cells == 256
        and n_lat == 4
        and n_lat * n_lev == 16
        and levels * n_lev == kz_shape[1]
        and kz_shape[1] % 8 == 0
        and levels % 2 == 0
        and entries == 512
    )


def device_part(sizes, *arrays):
    if fits(sizes, arrays[0].shape, arrays[3].shape, arrays[5].shape[-1]):
        return regrouped(sizes, *arrays)
    return shards(*arrays)


def solution(mesh):
    sizes = tuple(mesh.shape[name] for name in RING)
    in_specs = (
        P(None, "lev", "lat", "lon"),
        P("lev", "lat", "lon"),
        P("lev", "lat", "lon"),
        P(),
        P(None, "lat", "lon"),
        P(AXES, "lon", None),
        P(AXES, "lon", None, None),
        P(AXES, "lon", None),
        P(AXES, "lon", None),
    )
    out_specs = (P(None, "lev", "lat", "lon"), P(None, None, "lon", AXES))
    return jax.shard_map(
        functools.partial(device_part, sizes),
        mesh=mesh,
        in_specs=in_specs,
        out_specs=out_specs,
        check_vma=False,
    )
```

```python
import functools
import jax
import jax.numpy as jnp
from jax import lax
from jax.experimental import pallas as pl
from jax.experimental.pallas import tpu as pltpu
from jax.sharding import PartitionSpec as P

NSUB = 4
HOURS = 2
REGIMES = 4
FOOT_LEVELS = 8
SPO = 4
LANES = 128
GRAIN = 16
F32 = jnp.float32
BF16 = jnp.bfloat16
AXES = ("lat", "lev")
RING = ("lat", "lev", "lon")


def chunk_owner(n_lat, n_lev):
    place = [0] * (n_lat * n_lev)
    for a in range(n_lat):
        for z in range(n_lev):
            chip, core = divmod(a, 2)
            step = z if chip % 2 == 0 else n_lev - 1 - z
            place[(chip * n_lev + step) * 2 + core] = a * n_lev + z
    return place


def ring_perm(n_lat, n_lev, n_lon, shift):
    place = chunk_owner(n_lat, n_lev)
    ring = [
        (place[::-1] if o % 2 else place)[d] * n_lon + o
        for o in range(n_lon)
        for d in range(len(place))
    ]
    count = len(ring)
    return [(ring[i], ring[(i + shift) % count]) for i in range(count)]


def owners(place):
    odd = lax.axis_index("lon") % 2 == 1
    return [jnp.where(odd, there, here) for here, there in zip(place, place[::-1])]


def lane_ids(rows):
    return lax.broadcasted_iota(jnp.int32, (rows, LANES), 1)


def swap_grains(blocks):
    blocks = list(blocks)
    grain = lane_ids(blocks[0].shape[0]) // GRAIN
    bit = len(blocks) // 2
    while bit:
        low = (grain & bit) == 0
        for i in range(len(blocks)):
            if i & bit == 0:
                a, b = blocks[i], blocks[i | bit]
                blocks[i] = jnp.where(low, a, pltpu.roll(b, bit * GRAIN, 1))
                blocks[i | bit] = jnp.where(low, pltpu.roll(a, LANES - bit * GRAIN, 1), b)
        bit //= 2
    return blocks


def swap_halves(a, b):
    low = lane_ids(a.shape[0]) < LANES // 2
    return (
        jnp.where(low, a, pltpu.roll(b, LANES // 2, 1)),
        jnp.where(low, pltpu.roll(a, LANES // 2, 1), b),
    )


def lane_matrix(back):
    major = lax.broadcasted_iota(jnp.int32, (256, 256), 1 if back else 0)
    work = lax.broadcasted_iota(jnp.int32, (256, 256), 0 if back else 1)
    lon = (work % LANES) // GRAIN * 2 + work // LANES
    return ((major // GRAIN == work % GRAIN) & (major % GRAIN == lon)).astype(F32).astype(BF16)


def split_two(x):
    high = x.astype(BF16)
    return high, (x - high.astype(F32)).astype(BF16)


def split_three(x):
    high, _ = split_two(x)
    rest = x - high.astype(F32)
    middle = rest.astype(BF16)
    return high, middle, (rest - middle.astype(F32)).astype(BF16)


def mm(a, b):
    return jnp.dot(a, b, preferred_element_type=F32)


def move_lanes(x, matrix):
    high, middle, low = split_three(x)
    return (mm(high, matrix) + mm(middle, matrix)) + mm(low, matrix)


def fetch(given, held, sems):
    return [
        pltpu.make_async_copy(a, b, sems.at[i]) for i, (a, b) in enumerate(zip(given, held))
    ]


def place_pieces(place, srcs, out, first, count):
    for half in range(2):
        lanes = slice(half * LANES, (half + 1) * LANES)
        for j, piece in enumerate(swap_grains([s[:, lanes] for s in srcs])):
            out[place[half * 8 + j], first : first + count, :] = piece


def pack_winds_kernel(place, *refs):
    given, winds, held, sems = refs[:2], refs[3], refs[4:6], refs[6]
    copies = fetch(given, held, sems)
    for copy in copies:
        copy.start()
    place = owners(place)
    levels, rows = held[0].shape[:2]
    for copy in copies:
        copy.wait()
    place_pieces(place, [w[:, r, :] for w in held for r in range(rows)], winds, 0, levels)


def pack_fields_kernel(place, *refs):
    count = (len(refs) - 2) // 2
    given, fields, held, sems = refs[:count], refs[count], refs[count + 1 : -1], refs[-1]
    halves = [
        pltpu.make_async_copy(given[0].at[part], held[0].at[part], sems.at[at])
        for part, at in ((pl.ds(0, 2), 0), (pl.ds(2, 2), count))
    ]
    copies = fetch(given, held, sems)[1:]
    for copy in copies + halves:
        copy.start()
    adj, regime, cell, owner, station, weight = held
    place = owners(place)
    levels, rows = adj.shape[1:3]
    for copy in copies:
        copy.wait()
    srcs = [regime[h, r : r + 1, :].astype(F32) for h in range(HOURS) for r in range(rows)]
    place_pieces(place, srcs, fields, 2 * levels, 1)
    cells = cell[0].astype(F32)
    stations = (owner[...] * SPO + station[0]).astype(F32)
    for g in range(fields.shape[0]):
        k = g // (fields.shape[0] // 4)
        for at, value in enumerate((cells, stations, weight[0])):
            row = 2 * levels + 1 + at
            fields[g, row : row + 1, :] = value[:, k * LANES : (k + 1) * LANES]
    for pair in range(2):
        halves[pair].wait()
        srcs = [adj[2 * pair + k, :, r, :] for k in range(2) for r in range(rows)]
        place_pieces(place, srcs, fields, pair * levels, levels)


def solve_columns(high, low, kz_high, kz_low, regime, levels):
    product = mm(kz_high, high) + (mm(kz_low, high) + mm(kz_high, low))
    result = product[:levels]
    for k in range(1, REGIMES):
        result = jnp.where(regime == float(k), product[k * levels : (k + 1) * levels], result)
    return result


def mixing(kz):
    stacked = jnp.concatenate([kz[k].T for k in range(REGIMES)], axis=0)
    return split_two(stacked)


def rim_messages(top, bottom, first, last, rows):
    pair = lane_ids(top.shape[0]) // (2 * GRAIN)
    blocks = [top[:, :LANES], top[:, LANES:], bottom[:, :LANES], bottom[:, LANES:]]

    def gathered(offset):
        out = blocks[3] if offset == 3 else turned(blocks[3], (3 - offset) * 2 * GRAIN)
        for k in range(3):
            shift = (k - offset) * 2 * GRAIN
            out = jnp.where(pair == k, turned(blocks[k], shift) if shift else blocks[k], out)
        return out

    first[rows, :] = gathered(0)
    last[rows, :] = gathered(3)


def unpack_solve_kernel(n_lev, recv, kz, solved, regimes, first, last, field):
    total = kz.shape[1]
    levels = total // n_lev
    for pair in range(2):
        for z in range(n_lev):
            for half in range(2):
                lanes = slice(half * LANES, (half + 1) * LANES)
                a, b = [
                    recv[(2 * half + k) * n_lev + z, pair * levels : (pair + 1) * levels, :]
                    for k in range(2)
                ]
                for k, value in enumerate(swap_halves(a, b)):
                    base = (2 * pair + k) * total + z * levels
                    field[base : base + levels, lanes] = value
    base = 4 * total
    field[base : base + 8, :] = jnp.zeros((8, 256), F32)
    for half in range(2):
        lanes = slice(half * LANES, (half + 1) * LANES)
        a, b = [
            recv[(2 * half + k) * n_lev, 2 * levels : 2 * levels + 1, :] for k in range(2)
        ]
        for k, value in enumerate(swap_halves(a, b)):
            field[base + k : base + k + 1, lanes] = value
    matrix = lane_matrix(False)
    regime = mm(field[base : base + 8, :].astype(BF16), matrix)
    regimes[...] = regime
    kz_high, kz_low = mixing(kz)
    for t in range(4):
        high, low = split_two(field[t * total : (t + 1) * total, :])
        high = mm(high, matrix).astype(BF16)
        low = mm(low, matrix).astype(BF16)
        solved[t * total : (t + 1) * total, :] = solve_columns(
            high, low, kz_high, kz_low, regime[0:1], total
        )
    rim_messages(
        solved[0 : 2 * total, :], solved[2 * total :, :], first, last, slice(0, 2 * total)
    )


def unpack_winds_kernel(n_lev, *refs):
    pieces, (winds, first, last, field, others) = refs[:n_lev], refs[n_lev + 1 :]
    total = winds.shape[0] // 2
    levels = total // n_lev
    for m in range(n_lev):
        for k in range(others.shape[1]):
            others[m, k] = pieces[m][k * levels : (k + 1) * levels, :]
    own_lat, own_lev = lax.axis_index("lat"), lax.axis_index("lev")
    for z in range(n_lev):
        for half in range(2):
            lanes = slice(half * LANES, (half + 1) * LANES)
            a, b = [
                others[z ^ own_lev, (2 * half + k) ^ own_lat, 0:levels, :] for k in range(2)
            ]
            for k, value in enumerate(swap_halves(a, b)):
                base = k * total + z * levels
                field[base : base + levels, lanes] = value
    winds[...] = move_lanes(field[...], lane_matrix(False))
    rim_messages(winds[0:total, :], winds[total:, :], first, last, slice(0, total))


def rim_lanes(from_east, from_west, rows, upper):
    half = LANES // 2
    east, west = from_east[rows, :], from_west[rows, :]
    lane = lane_ids(east.shape[0])
    if upper:
        both = jnp.where(lane < half, pltpu.roll(east, half, 1), west)
    else:
        both = jnp.where(lane < half, east, pltpu.roll(west, half, 1))
    place = lane // GRAIN % 4
    both = jnp.where(place == 1, turned(both, -GRAIN), jnp.where(place == 2, turned(both, GRAIN), both))
    return both


def columns(ref, rows):
    return [ref[rows, i * LANES : (i + 1) * LANES] for i in range(3)]


def pair_columns(ref, rows):
    return [ref[rows, i * LANES : (i + 1) * LANES] for i in range(2)]


def turned(x, shift):
    return pltpu.roll(x, shift % LANES, 1)


def stepped(blocks, shift):
    even, odd, rim = blocks
    lane = lane_ids(even.shape[0])
    outer = turned(rim, shift)
    if shift > 0:
        inner, edge = turned(odd, shift), lane < shift
        return [jnp.where(edge, outer, inner), even, jnp.where(edge, inner, outer)]
    inner, edge = turned(even, shift), lane >= LANES + shift
    return [odd, jnp.where(edge, outer, inner), jnp.where(edge, inner, outer)]


def face_weights(lat_count, winds, from_east, from_west, total, faces):
    rims = slice(0, total)
    east = pair_columns(winds, slice(0, total)) + [rim_lanes(from_east, from_west, rims, False)]
    north = pair_columns(winds, slice(total, 2 * total)) + [
        rim_lanes(from_east, from_west, rims, True)
    ]
    lat = lane_ids(total) % lat_count
    north = [jnp.where(lat == lat_count - 1, 0.0, x) for x in north]
    west = stepped(east, lat_count)
    for i in range(3):
        lanes = slice(i * LANES, (i + 1) * LANES)
        after = jnp.maximum(north[i], 0.0)
        before = -jnp.minimum(jnp.where(lat == 0, 0.0, turned(north[i], 1)), 0.0)
        faces[0, :, lanes] = 1.0 - after - before
        faces[1, :, lanes] = after
        faces[2, :, lanes] = before
        after = jnp.maximum(east[i], 0.0)
        before = -jnp.minimum(west[i], 0.0)
        faces[3, :, lanes] = 1.0 - after - before
        faces[4, :, lanes] = after
        faces[5, :, lanes] = before


def first_sweep_kernel(lat_count, field, winds, swept):
    total = winds.shape[0] // 2
    lat = lane_ids(total) % lat_count
    for i, north in enumerate(pair_columns(winds, slice(total, 2 * total))):
        lanes = slice(i * LANES, (i + 1) * LANES)
        north = jnp.where(lat == lat_count - 1, 0.0, north)
        after = jnp.maximum(north, 0.0)
        before = -jnp.minimum(jnp.where(lat == 0, 0.0, turned(north, 1)), 0.0)
        stay = 1.0 - after - before
        for t in range(4):
            own = slice(t * total, (t + 1) * total)
            f = field[own, lanes]
            swept[own, lanes] = stay * f + after * turned(f, -1) + before * turned(f, 1)


def transport(lat_count, field, east_rows, west_rows, faces, total, buffers, result, begun=False):
    for t in range(4):
        own = slice(t * total, (t + 1) * total)
        rim = slice((t % 2) * total, (t % 2 + 1) * total)
        rim = rim_lanes(east_rows, west_rows, rim, t >= 2)
        if begun:
            lanes = slice(256, 384)
            rim = (
                faces[0, :, lanes] * rim
                + faces[1, :, lanes] * turned(rim, -1)
                + faces[2, :, lanes] * turned(rim, 1)
            )
        buffers[int(begun), own, 0:256] = field[own, :]
        buffers[int(begun), own, 256:384] = rim
    for step in range(int(begun), 2 * NSUB):
        last = step == 2 * NSUB - 1
        for t in range(4):
            own = slice(t * total, (t + 1) * total)
            f = columns(buffers.at[step % 2], own)
            if step % 2 == 0:
                after = [turned(x, -1) for x in f]
                before = [turned(x, 1) for x in f]
            else:
                after = stepped(f, -lat_count)
                before = stepped(f, lat_count)
            base = 3 * (step % 2)
            for i in range(2 if last else 3):
                lanes = slice(i * LANES, (i + 1) * LANES)
                value = (
                    faces[base, :, lanes] * f[i]
                    + faces[base + 1, :, lanes] * after[i]
                    + faces[base + 2, :, lanes] * before[i]
                )
                if last:
                    result[own, lanes] = value
                else:
                    buffers[(step + 1) % 2, own, lanes] = value


def transport_solve_kernel(
    lat_count, field, winds, regimes, kz, wind_east, wind_west, from_east, from_west, solved, first, last, faces, buffers, moved
):
    total = kz.shape[1]
    face_weights(lat_count, winds, wind_east, wind_west, total, faces)
    transport(lat_count, field, from_east, from_west, faces, total, buffers, moved, True)
    kz_high, kz_low = mixing(kz)
    for t in range(4):
        high, low = split_two(moved[t * total : (t + 1) * total, :])
        solved[t * total : (t + 1) * total, :] = solve_columns(
            high, low, kz_high, kz_low, regimes[1:2, :], total
        )
    rim_messages(
        solved[0 : 2 * total, :], solved[2 * total :, :], first, last, slice(0, 2 * total)
    )


def footprint_kernel(n_lev, quarters, hour_0, hour_1, sums):
    own_lat, own_lev = lax.axis_index("lat"), lax.axis_index("lev")
    chip, core = own_lat // 2, own_lat % 2
    step = jnp.where(chip % 2 == 0, own_lev, n_lev - 1 - own_lev)
    chunk = (chip * n_lev + step) * 2 + core
    odd = lax.axis_index("lon") % 2 == 1
    group = quarters.shape[1] // 3
    first_lon = jnp.where(odd, group - 1 - chunk, chunk) * GRAIN
    total = hour_0.shape[0] // 4
    matrix = lane_matrix(True)
    low = jnp.concatenate(
        [h[t * total : t * total + FOOT_LEVELS, :] for h in (hour_0, hour_1) for t in range(4)],
        axis=0,
    )
    parts = mm(jnp.concatenate(split_three(low), axis=0), matrix).astype(BF16)
    count = low.shape[0]
    acc = jnp.zeros((count, 64), F32)
    cell_ids = lax.broadcasted_iota(jnp.int32, (GRAIN, 512), 0)
    level_ids = lax.broadcasted_iota(jnp.int32, (FOOT_LEVELS, 512), 0)
    station_ids = lax.broadcasted_iota(jnp.int32, (64, 512), 0)
    for row in range(group):

        def entries(at):
            return jnp.concatenate(
                [quarters[k, 3 * row + at : 3 * row + at + 1, :] for k in range(4)], axis=1
            )

        code = entries(0).astype(jnp.int32)
        station = entries(1).astype(jnp.int32)
        weight = entries(2)
        cells = ((code & 255) - first_lon == cell_ids).astype(F32).astype(BF16)
        picked = mm(parts[:, row * GRAIN : (row + 1) * GRAIN], cells)
        picked = (picked[:count] + picked[count : 2 * count]) + picked[2 * count :]
        level = jnp.where((code >> 8) == level_ids, weight, 0.0)
        picked = picked * jnp.concatenate([level] * (count // FOOT_LEVELS), axis=0)
        named = (station == station_ids).astype(F32).astype(BF16)
        high, rest = split_two(picked)
        both = jnp.concatenate([high, rest], axis=0)
        both = lax.dot_general(both, named, (((1,), (1,)), ((), ())), preferred_element_type=F32)
        acc = acc + (both[:count] + both[count:])
    sums[...] = jnp.sum(acc.reshape(count // FOOT_LEVELS, FOOT_LEVELS, 64), axis=1)


def face_kernel(lat_count, winds, wind_east, wind_west, _, faces):
    face_weights(lat_count, winds, wind_east, wind_west, winds.shape[0] // 2, faces)


def transport_pack_kernel(
    lat_count, n_lev, field, faces, from_east, from_west, sums, out, buffers, moved
):
    total = faces.shape[1]
    levels = total // n_lev
    transport(lat_count, field, from_east, from_west, faces, total, buffers, moved)
    matrix = lane_matrix(True)
    for pair in range(2):
        for k in range(2):
            rows = slice((2 * pair + k) * total, (2 * pair + k + 1) * total)
            moved[rows, :] = move_lanes(moved[rows, :], matrix)
        for z in range(n_lev):
            for half in range(2):
                lanes = slice(half * LANES, (half + 1) * LANES)
                a, b = [
                    moved[
                        (2 * pair + k) * total + z * levels : (2 * pair + k) * total
                        + (z + 1) * levels,
                        lanes,
                    ]
                    for k in range(2)
                ]
                for k, value in enumerate(swap_halves(a, b)):
                    out[
                        (2 * half + k) * n_lev + z, pair * levels : (pair + 1) * levels, :
                    ] = value
    wide = jnp.concatenate([sums[...], jnp.zeros((8, 64), F32)], axis=1)
    line = lax.broadcasted_iota(jnp.int32, (8, LANES), 0)
    spread = jnp.zeros((8, LANES), F32)
    for k in range(8):
        spread = jnp.where(line == k, pltpu.roll(wide, 4 * k, 1) if k else wide, spread)
    keep = lax.broadcasted_iota(jnp.int32, (8, LANES), 1) // 4 == line
    for g in range(out.shape[0]):
        value = pltpu.roll(spread, LANES - 4 * g, 1) if g else spread
        value = jnp.sum(jnp.where(keep, value, 0.0), axis=0, keepdims=True)
        out[g, 2 * levels : 2 * levels + 1, :] = value


def unpack_kernel(place, recv, final, stations):
    place = owners(place)
    levels = final.shape[1]
    for pair in range(2):
        for half in range(2):
            lanes = slice(half * LANES, (half + 1) * LANES)
            blocks = [
                recv[place[half * 8 + j], pair * levels : (pair + 1) * levels, :]
                for j in range(8)
            ]
            for i, value in enumerate(swap_grains(blocks)):
                k, r = divmod(i, 4)
                final[2 * pair + k, :, r, lanes] = value
    line = recv[0, 2 * levels : 2 * levels + 1, :]
    for g in range(1, recv.shape[0]):
        line = line + recv[g, 2 * levels : 2 * levels + 1, :]
    for h in range(HOURS):
        for t in range(4):
            at = (h * 4 + t) * 4
            stations[h, t, :, :] = line[:, at : at + 4]


def swaps(x, axis, count, piece):
    return [piece(x, 0)] + [
        lax.ppermute(piece(x, k), axis, [(i, i ^ k) for i in range(count)])
        for k in range(1, count)
    ]


def gather_winds(sizes, winds):
    n_lat, n_lev, _ = sizes
    own_lat, own_lev = lax.axis_index("lat"), lax.axis_index("lev")
    levels = winds.shape[1]

    def for_lat(x, k):
        return lax.dynamic_index_in_dim(x, own_lat ^ k, 0, keepdims=False)

    def for_lev(x, k):
        return lax.dynamic_index_in_dim(x, own_lev ^ k, 1, keepdims=False).reshape(-1, LANES)

    here = swaps(winds.reshape(n_lat, n_lev * levels, LANES), "lat", n_lat, for_lat)
    here = jnp.stack(here).reshape(n_lat, n_lev, levels, LANES)
    return swaps(here, "lev", n_lev, for_lev)


def call(kernel, outs, scratch=()):
    return pl.pallas_call(
        kernel,
        out_shape=[jax.ShapeDtypeStruct(s, F32) for s in outs],
        scratch_shapes=[pltpu.VMEM(s, F32) for s in scratch],
        compiler_params=pltpu.CompilerParams(vmem_limit_bytes=48 * 1024 * 1024),
    )


def regrouped(sizes, adjoint, wind_east, wind_north, kz_inverse, kz_regime, fp_cell, fp_owner, fp_station, fp_weight):
    n_lat, n_lev, n_lon = sizes
    levels = adjoint.shape[1]
    total = levels * n_lev
    group = n_lat * n_lev
    lat_count = n_lat * adjoint.shape[2]
    place = chunk_owner(n_lat, n_lev)
    to_west = ring_perm(n_lat, n_lev, n_lon, -1)
    to_east = ring_perm(n_lat, n_lev, n_lon, 1)

    def exchange(x):
        return lax.all_to_all(x, AXES, split_axis=0, concat_axis=0, tiled=True)

    def rims(first, last):
        return lax.ppermute(first, RING, to_west), lax.ppermute(last, RING, to_east)

    out_rows = 2 * levels + 1
    out_rows += -out_rows % 8
    in_rows = 2 * levels + 4
    in_rows += -in_rows % 8
    wind_rows = levels + -levels % 8

    def pack(kernel, given, after, shape):
        given = [pltpu.with_memory_space_constraint(x, pltpu.HBM) for x in given]
        return pl.pallas_call(
            functools.partial(kernel, place),
            in_specs=[pl.BlockSpec(memory_space=pltpu.HBM)] * (len(given) + len(after)),
            out_shape=jax.ShapeDtypeStruct(shape, F32),
            scratch_shapes=[pltpu.VMEM(x.shape, x.dtype) for x in given]
            + [pltpu.SemaphoreType.DMA((len(given) + 1,))],
            compiler_params=pltpu.CompilerParams(vmem_limit_bytes=48 * 1024 * 1024),
        )(*given, *after)

    fields = pack(
        pack_fields_kernel,
        (adjoint, kz_regime, fp_cell, fp_owner.reshape(1, -1), fp_station, fp_weight),
        (),
        (group, in_rows, LANES),
    )
    winds = pack(
        pack_winds_kernel, (wind_east, wind_north), (fields,), (group, wind_rows, LANES)
    )
    recv = exchange(fields)
    winds = gather_winds(sizes, winds[:, :levels])
    solved_0, regimes, first, last = call(
        functools.partial(unpack_solve_kernel, n_lev),
        [(4 * total, 256), (8, 256), (2 * total, LANES), (2 * total, LANES)],
        [(4 * total + 8, 256)],
    )(recv, kz_inverse)
    east_0, west_0 = rims(first, last)
    winds, first, last = call(
        functools.partial(unpack_winds_kernel, n_lev),
        [(2 * total, 256), (total, LANES), (total, LANES)],
        [(2 * total, 256), (n_lev, n_lat, levels, LANES)],
    )(*winds, regimes)
    wind_rims = rims(first, last)
    (swept,) = call(functools.partial(first_sweep_kernel, lat_count), [(4 * total, 256)])(
        solved_0, winds
    )
    entries = recv[:, 2 * levels + 1 : 2 * levels + 4].reshape(-1, LANES)
    entries = jnp.stack(swaps(entries, "lat", n_lat, lambda x, k: x))
    solved_1, first, last = call(
        functools.partial(transport_solve_kernel, lat_count),
        [(4 * total, 256), (2 * total, LANES), (2 * total, LANES)],
        [(6, total, 384), (2, 4 * total, 384), (4 * total, 256)],
    )(swept, winds, regimes, kz_inverse, *wind_rims, east_0, west_0)
    east_1, west_1 = rims(first, last)
    (sums,) = call(functools.partial(footprint_kernel, n_lev), [(8, 64)])(
        entries, solved_0, solved_1
    )
    (faces,) = call(functools.partial(face_kernel, lat_count), [(6, total, 384)])(
        winds, *wind_rims, first
    )
    (back,) = call(
        functools.partial(transport_pack_kernel, lat_count, n_lev),
        [(group, out_rows, LANES)],
        [(2, 4 * total, 384), (4 * total, 256)],
    )(solved_1, faces, east_1, west_1, sums)
    final, stations = call(
        functools.partial(unpack_kernel, place), [adjoint.shape, (HOURS, 4, 1, SPO)]
    )(exchange(back))
    return final, stations


def padded_2(x, sides, width, wrap):
    for axis, dim in sides:
        peers, length = (lax.axis_size(axis), x.shape[dim])
        up = [(i, (i + 1) % peers) for i in range(peers if wrap else peers - 1)]
        down = [(j, i) for i, j in up]
        last = lax.slice_in_dim(x, length - width, length, axis=dim)
        initial = lax.slice_in_dim(x, 0, width, axis=dim)
        before = lax.ppermute(last, axis, up)
        after = lax.ppermute(initial, axis, down)
        x = jnp.concatenate([before, x, after], axis=dim)
    return x


def lat_rim(values, rim_width):
    return padded_2(values, (("lat", 2),), rim_width, False)


def lon_rim(values, rim_width):
    return padded_2(values, (("lon", 3),), rim_width, True)


def lat_sweep(padded, north_face, south_face):
    middle = padded[:, :, 1:-1]
    return (
        middle
        + jnp.maximum(north_face, 0.0) * (padded[:, :, 2:] - middle)
        - jnp.minimum(south_face, 0.0) * (padded[:, :, :-2] - middle)
    )


def lon_sweep(padded, east_face, west_face):
    middle = padded[:, :, :, 1:-1]
    return (
        middle
        + jnp.maximum(east_face, 0.0) * (padded[:, :, :, 2:] - middle)
        - jnp.minimum(west_face, 0.0) * (padded[:, :, :, :-2] - middle)
    )


def shards(
    adjoint, wind_east, wind_north, kz_inverse, kz_regime, fp_cell, fp_owner, fp_station, fp_weight
):
    tracers, levels_dev, lat_rows, lon_cells = adjoint.shape
    row_index = lax.axis_index("lat") * lat_rows + lax.broadcasted_iota(
        jnp.int32, (1, lat_rows, 1), 1
    )
    last_row = lat_rows * lax.axis_size("lat") - 1
    north_face = jnp.where(row_index == last_row, jnp.zeros_like(wind_north), wind_north)
    south_face = lat_rim(north_face[None], 1)[0][:, :-2]
    west_face = lon_rim(wind_east[None], 1)[0][:, :, :-2]
    groups = lax.axis_size("lat") * lax.axis_size("lev")
    column_count = lat_rows * lon_cells // lax.axis_size("lev")
    first_column = lax.axis_index("lev") * column_count
    regime_rows = kz_regime.reshape(HOURS, lat_rows * lon_cells)
    cell_ids = fp_cell.reshape(-1)
    owners = fp_owner.reshape(-1)
    stations = fp_station.reshape(-1)
    weights = fp_weight.reshape(-1)
    entries = cell_ids.shape[0]
    adjoint_field = adjoint
    outputs = []
    for hour_step in range(HOURS):
        chosen = lax.dynamic_slice_in_dim(regime_rows[hour_step], first_column, column_count, 0)

        def column_solve(columns, chosen=chosen):
            result = jnp.zeros_like(columns)
            for regime in range(REGIMES):
                product = jnp.einsum(
                    "ji,tjp->tip", kz_inverse[regime], columns, precision=lax.Precision.HIGHEST
                )
                result = jnp.where(chosen[None, None, :] == regime, product, result)
            returned = lax.all_to_all(result, "lev", split_axis=1, concat_axis=2, tiled=True)
            return (returned, result)

        flat_field = adjoint_field.reshape(tracers, levels_dev, lat_rows * lon_cells)
        returned, solved = column_solve(
            lax.all_to_all(flat_field, "lev", split_axis=2, concat_axis=1, tiled=True)
        )
        lowest = solved[:, :FOOT_LEVELS, :].reshape(tracers, -1)
        picked = jnp.take(lowest, cell_ids, axis=1) * weights[None, :]
        capacity = 2 * entries // groups
        owner_hits = (owners[:, None] == jnp.arange(groups, dtype=jnp.int32)[None, :]).astype(
            jnp.int32
        )
        bucket_rank = jnp.sum(jnp.cumsum(owner_hits, axis=0) * owner_hits, axis=1) - 1
        slot_pos = owners * capacity + bucket_rank
        send_values = (
            jnp.zeros((tracers, groups * capacity), jnp.float32).at[:, slot_pos].set(picked)
        )
        send_ids = jnp.full((groups * capacity,), -1, jnp.int32).at[slot_pos].set(stations)
        arrived_values, arrived_ids = (
            lax.all_to_all(
                send_values.reshape(tracers, groups, capacity),
                ("lat", "lev"),
                split_axis=1,
                concat_axis=1,
                tiled=True,
            ),
            lax.all_to_all(
                send_ids.reshape(1, groups, capacity),
                ("lat", "lev"),
                split_axis=1,
                concat_axis=1,
                tiled=True,
            ),
        )
        matches = (
            arrived_ids[0][:, :, None] == jnp.arange(SPO, dtype=jnp.int32)[None, None, :]
        ).astype(jnp.float32)
        station_sums = jnp.einsum(
            "tgc,gcs->ts", arrived_values, matches, precision=lax.Precision.HIGHEST
        )
        outputs.append(station_sums)
        adjoint_field = returned.reshape(tracers, levels_dev, lat_rows, lon_cells)
        for substep in range(NSUB):
            adjoint_field = lat_sweep(lat_rim(adjoint_field, 1), north_face, south_face)
            adjoint_field = lon_sweep(lon_rim(adjoint_field, 1), wind_east, west_face)
    return (adjoint_field, jnp.stack(outputs)[:, :, None, :])


def fits(mesh_sizes, shape, kz_shape, entries):
    n_lat, n_lev, n_lon = mesh_sizes
    tracers, levels, rows, cells = shape
    return (
        tracers == 4
        and rows == 4
        and cells == 256
        and n_lat == 4
        and n_lat * n_lev == 16
        and levels * n_lev == kz_shape[1]
        and kz_shape[1] % 8 == 0
        and levels % 2 == 0
        and entries == 512
    )


def device_part(sizes, *arrays):
    if fits(sizes, arrays[0].shape, arrays[3].shape, arrays[5].shape[-1]):
        return regrouped(sizes, *arrays)
    return shards(*arrays)


def solution(mesh):
    sizes = tuple(mesh.shape[name] for name in RING)
    in_specs = (
        P(None, "lev", "lat", "lon"),
        P("lev", "lat", "lon"),
        P("lev", "lat", "lon"),
        P(),
        P(None, "lat", "lon"),
        P(AXES, "lon", None),
        P(AXES, "lon", None, None),
        P(AXES, "lon", None),
        P(AXES, "lon", None),
    )
    out_specs = (P(None, "lev", "lat", "lon"), P(None, None, "lon", AXES))
    return jax.shard_map(
        functools.partial(device_part, sizes),
        mesh=mesh,
        in_specs=in_specs,
        out_specs=out_specs,
        check_vma=False,
    )
```
